32 devices in a mesh: dp: 16 (over z, y, core), seq: 2 (over x).
Axes of the slice: x: 2, y: 2, z: 4, core: 2. Of those that a mesh axis runs over, the one named last changes fastest.
Arguments:
- tokens: bfloat16 [32768, 1024], P(('dp', 'seq')), may hold values from -6 to 6
- ln1_gain: float32 [1024], replicated, may hold values from 0.5 to 1.5
- ln1_bias: float32 [1024], replicated, may hold values from -1.5 to 1.5
- qkv_weight: bfloat16 [1024, 3072], P(('dp', 'seq')), may hold values from -0.1875 to 0.1875
- qkv_bias: float32 [2048], replicated, may hold values from -1.5 to 1.5
- dense_weight: bfloat16 [1024, 1024], P(('dp', 'seq')), may hold values from -0.5 to 0.5
- dense_bias: float32 [1024], replicated, may hold values from -1.5 to 1.5
- ln2_gain: float32 [1024], replicated, may hold values from 0.5 to 1.5
- ln2_bias: float32 [1024], replicated, may hold values from -1.5 to 1.5
- up_weight: bfloat16 [1024, 4096], P(('dp', 'seq')), may hold values from -0.1875 to 0.1875
- up_bias: float32 [4096], replicated, may hold values from -1.5 to 1.5
- down_weight: bfloat16 [4096, 1024], P(('dp', 'seq')), may hold values from -0.09375 to 0.09375
- down_bias: float32 [1024], replicated, may hold values from -1.5 to 1.5
- cotangent: bfloat16 [32768, 1024], P(('dp', 'seq')), may hold values from -6 to 6
- seq_lengths: int32 [32], replicated, may hold values from 256 to 1024, as said below
- slot_order: int32 [32], replicated, may hold values from 0 to 31, as said below
Outputs:
- block_output: bfloat16 [32768, 1024], P(('dp', 'seq'))
- token_grad: bfloat16 [32768, 1024], P(('dp', 'seq'))
- ln1_gain_grad: float32 [1024], replicated
- ln1_bias_grad: float32 [1024], replicated
- qkv_weight_grad: float32 [1024, 3072], P(('dp', 'seq'))
- qkv_bias_grad: float32 [2048], replicated
- dense_weight_grad: float32 [1024, 1024], P(('dp', 'seq'))
- dense_bias_grad: float32 [1024], replicated
- ln2_gain_grad: float32 [1024], replicated
- ln2_bias_grad: float32 [1024], replicated
- up_weight_grad: float32 [1024, 4096], P(('dp', 'seq'))
- up_bias_grad: float32 [4096], replicated
- down_weight_grad: float32 [4096, 1024], P(('dp', 'seq'))
- down_bias_grad: float32 [1024], replicated
The draws below stay inside these ranges and needn't reach their ends.
Inputs may be any that keep to these rules, and one draw needn't show every extreme that they name: `seq_lengths`: in every block of 2 consecutive slots, the sequence of at least one slot has more than 512 valid tokens; some sequence has 1024. `slot_order`: every sequence number appears once.
All inputs are finite; a program needn't handle non-finite values.
Results may differ from the reference program's by a relative error of at most 0.012.
Values may be sent and summed in bfloat16 or wider, within the bound.
No kernel may reach another device: no remote copies, remote signals or barrier semaphores. Data moves between devices by JAX's collectives and lax.ppermute only.
A program may use at most 256 MiB of HBM per device.

```python
import math
import jax
import jax.numpy as jnp
from jax import lax

D = 1024
H = 16
HD = 64
FF = 4096
SEQLEN = 1024
SG = 2
NSEQ = 32
TOKENS = 32768
N_SEQ = 2


def shared_order(key):
    return jax.random.permutation(jax.random.fold_in(key, 11), NSEQ).astype(jnp.int32)


def draw_slot_order(key, part):
    order = shared_order(key)
    return order


def draw_seq_lengths(key, part):
    order = shared_order(key)
    key = jax.random.fold_in(key, 7)
    first, second, third = jax.random.split(key, 3)
    drawn = jax.random.randint(first, (NSEQ,), SEQLEN // 4, SEQLEN + 1)
    groups = NSEQ // SG
    pick = jax.random.randint(second, (groups,), 0, SG)
    full_slots = jnp.arange(groups, dtype=jnp.int32) * SG + pick
    full_seqs = order[full_slots]
    near_full = jax.random.randint(third, (groups,), SEQLEN - SEQLEN // N_SEQ + 1, SEQLEN + 1)
    near_full = near_full.at[0].set(SEQLEN)
    match = jnp.arange(NSEQ, dtype=jnp.int32)[:, None] == full_seqs[None, :]
    marked = jnp.any(match, axis=1)
    marked_len = jnp.sum(jnp.where(match, near_full[None, :], 0), axis=1)
    return jnp.where(marked, marked_len, drawn).astype(jnp.int32)


def steps_of(stream_key, shape, shards, low, top_value):
    factor_of, own = 1.0, jax.random.fold_in(stream_key, 6)
    for axis_at, blocks in shards:
        heights = jnp.exp(jax.random.uniform(jax.random.fold_in(own, axis_at), (blocks,), jnp.float32, low / len(shards), top_value / len(shards)))
        factor_of = factor_of * jnp.repeat(heights, shape[axis_at] // blocks).reshape([-1 if axis == axis_at else 1 for axis in range(len(shape))])
    return factor_of


def normal_values(rng, extent, scale, most, cuts=(), held_as=jnp.bfloat16):
    entries = jax.random.normal(rng, extent, jnp.float32) * scale
    if len(cuts) > 0:
        entries = steps_of(rng, extent, cuts, -0.22, 0.18) * entries
    return jnp.clip(entries, min=-most, max=most).astype(held_as)


def setup_inputs(seed: int = 0) -> dict:
    streams_of = jax.random.split(jax.random.key(seed), 17)
    return {
        "tokens": normal_values(streams_of[0], (TOKENS, D), 1.0, 6.0, ((0, 32),)),
        "ln1_gain": jnp.clip(1.0 + 0.1 * jax.random.normal(streams_of[1], (D,), jnp.float32), 0.5, 1.5),
        "ln1_bias": normal_values(streams_of[2], (D,), 0.3, 1.5, (), jnp.float32),
        "qkv_weight": normal_values(streams_of[3], (D, 3 * D), D ** -0.5, 0.1875, ((0, 32),)),
        "qkv_bias": normal_values(streams_of[4], (2 * D,), 0.3, 1.5, (), jnp.float32),
        "dense_weight": normal_values(streams_of[5], (D, D), (D // 8) ** -0.5, 0.5, ((0, 32),)),
        "dense_bias": normal_values(streams_of[6], (D,), 0.3, 1.5, (), jnp.float32),
        "ln2_gain": jnp.clip(1.0 + 0.1 * jax.random.normal(streams_of[7], (D,), jnp.float32), 0.5, 1.5),
        "ln2_bias": normal_values(streams_of[8], (D,), 0.3, 1.5, (), jnp.float32),
        "up_weight": normal_values(streams_of[9], (D, FF), D ** -0.5, 0.1875, ((0, 32),)),
        "up_bias": normal_values(streams_of[10], (FF,), 0.3, 1.5, (), jnp.float32),
        "down_weight": normal_values(streams_of[11], (FF, D), FF ** -0.5, 0.09375, ((0, 32),)),
        "down_bias": normal_values(streams_of[12], (D,), 0.3, 1.5, (), jnp.float32),
        "cotangent": normal_values(streams_of[13], (TOKENS, D), 1.0, 6.0, ((0, 32),)),
        "seq_lengths": draw_seq_lengths(jax.random.fold_in(streams_of[16], 71), 0),
        "slot_order": draw_slot_order(jax.random.fold_in(streams_of[16], 71), 0),
    }


@jax.custom_vjp
def low(v):
    return lax.optimization_barrier(v.astype(jnp.bfloat16)).astype(jnp.float32)

@jax.custom_vjp
def low_back(v):
    return v

def low_keep(v):
    return (low(v), None)

def low_pass(kept, grad):
    return (grad,)

def back_keep(v):
    return (v, None)

def back_low(kept, grad):
    return (low(grad),)
low.defvjp(low_keep, low_pass)
low_back.defvjp(back_keep, back_low)

def layer_norm(values, gain, shift):
    center = values - lax.optimization_barrier(jnp.mean(values, axis=-1, keepdims=True))
    spread = lax.optimization_barrier(jnp.mean(center * center, axis=-1, keepdims=True))
    return center * lax.rsqrt(spread + 1e-05) * gain + shift

def gelu_tanh(values):
    return jax.nn.gelu(values, approximate=True)

def attend(query, key, value, length, slopes):
    block_rows = min(512, SEQLEN)
    key_place = jnp.arange(SEQLEN, dtype=jnp.int32)

    def block(index):
        query_block = lax.dynamic_slice_in_dim(query, index * block_rows, block_rows, 0)
        query_place = index * block_rows + jnp.arange(block_rows, dtype=jnp.int32)
        scores = jnp.einsum('qhd,khd->hqk', query_block, key, precision=lax.Precision.HIGHEST) * 0.125
        offset = (key_place[None, :] - query_place[:, None]).astype(jnp.float32)
        scores = scores + slopes[:, None, None] * offset[None]
        allowed = (key_place[None, :] <= query_place[:, None]) & (key_place[None, :] < length)
        scores = low_back(jnp.where(allowed[None], scores, -1e+30))
        top = lax.optimization_barrier(jnp.max(scores, axis=-1, keepdims=True))
        expo = jnp.exp(scores - top)
        probs = low(expo / lax.optimization_barrier(jnp.sum(expo, axis=-1, keepdims=True)))
        return jnp.einsum('hqk,khd->qhd', probs, value, precision=lax.Precision.HIGHEST)
    blocks = lax.map(jax.checkpoint(block), jnp.arange(SEQLEN // block_rows, dtype=jnp.int32))
    return blocks.reshape(SEQLEN, H, HD)

def reference(tokens, ln1_gain, ln1_bias, qkv_weight, qkv_bias, dense_weight, dense_bias, ln2_gain, ln2_bias, up_weight, up_bias, down_weight, down_bias, cotangent, seq_lengths, slot_order):
    lengths_slot = seq_lengths[slot_order]
    per_step = math.gcd(NSEQ, max(1, 4096 // SEQLEN))
    step_count = NSEQ // per_step
    slopes = jnp.exp2(-8.0 * (jnp.arange(H, dtype=jnp.float32) + 1.0) / H)
    hidden_high = lax.Precision.HIGHEST

    def group_forward(inputs, lengths, params):
        gain_one, shift_one, w_qkv, b_qkv, w_dense, b_dense, gain_two, shift_two, w_up, b_up, w_down, b_down = params
        count = inputs.shape[0]
        normed = low(layer_norm(inputs, gain_one, shift_one))
        bias_full = jnp.concatenate([b_qkv[:D], jnp.zeros((D,), jnp.float32), b_qkv[D:]])
        joined = low(low_back(jnp.einsum('psd,dc->psc', normed, w_qkv, precision=hidden_high) + bias_full))
        query = joined[..., :D].reshape(count, SEQLEN, H, HD)
        key = joined[..., D:2 * D].reshape(count, SEQLEN, H, HD)
        value = joined[..., 2 * D:].reshape(count, SEQLEN, H, HD)
        context = lax.map(lambda packed: attend(packed[0], packed[1], packed[2], packed[3], slopes), (query, key, value, lengths))
        context = low(low_back(context.reshape(count, SEQLEN, D)))
        hidden = inputs + low_back(jnp.einsum('psd,de->pse', context, w_dense, precision=hidden_high) + b_dense)
        normed_two = low(layer_norm(hidden, gain_two, shift_two))
        before = low_back(jnp.einsum('psd,df->psf', normed_two, w_up, precision=hidden_high) + b_up)
        active = low(gelu_tanh(before))
        return hidden + low_back(jnp.einsum('psf,fd->psd', active, w_down, precision=hidden_high) + b_down)

    def forward(inputs, params):
        blocks = inputs.reshape(step_count, per_step, SEQLEN, D)
        lengths = lengths_slot.reshape(step_count, per_step)

        def step(carry, packed):
            return (carry, group_forward(packed[0], packed[1], params))
        _, outputs = lax.scan(jax.checkpoint(step), jnp.zeros((), jnp.float32), (blocks, lengths))
        return outputs.reshape(TOKENS, D)
    inputs = tokens.astype(jnp.float32)
    params = (ln1_gain, ln1_bias, qkv_weight.astype(jnp.float32), qkv_bias, dense_weight.astype(jnp.float32), dense_bias, ln2_gain, ln2_bias, up_weight.astype(jnp.float32), up_bias, down_weight.astype(jnp.float32), down_bias)
    outputs, backward = jax.vjp(forward, inputs, params)
    valid = (jnp.arange(SEQLEN, dtype=jnp.int32)[None, :] < lengths_slot[:, None]).reshape(TOKENS)
    grad_out = cotangent.astype(jnp.float32) * valid[:, None].astype(jnp.float32)
    grad_in, grads = backward(grad_out)
    return (outputs.astype(jnp.bfloat16), grad_in.astype(jnp.bfloat16), grads[0], grads[1], grads[2], grads[3], grads[4], grads[5], grads[6], grads[7], grads[8], grads[9], grads[10], grads[11])
```

```python
import functools

import jax
import jax.numpy as jnp
import ml_dtypes
import numpy as np
from jax import lax
from jax.experimental import pallas as pl
from jax.experimental.pallas import tpu as pltpu
from jax.sharding import PartitionSpec as P

H = 16
SEQLEN = 1024
SG = 2
BQ = 256
f32 = jnp.float32
bf16 = jnp.bfloat16
NT = (((1,), (1,)), ((), ()))


def dot(a, b):
    return jnp.dot(a, b, preferred_element_type=f32)


def dotnt(a, b):
    return lax.dot_general(a, b, NT, preferred_element_type=f32)


LOG2E=1.4426950408889634

def attn_fwd_kernel(len_ref, slope_ref, q_ref, k_ref, v_ref, o_ref, lse_ref):
    pair=pl.program_id(0)
    n=q_ref.shape[0]
    length=len_ref[0]
    lane=lax.broadcasted_iota(jnp.int32,(1,128),1)
    first=lane<64
    place=lax.broadcasted_iota(jnp.int32,(1,n),1)
    ones=jnp.ones((n,128),bf16)
    vaug=jnp.concatenate([v_ref[...],ones],axis=1)
    k=k_ref[...]
    diag=lax.broadcasted_iota(jnp.int32,(BQ,BQ),1)<=lax.broadcasted_iota(jnp.int32,(BQ,BQ),0)
    bias=[jnp.where(place<length, place.astype(f32)*(slope_ref[2*pair+h]*LOG2E), -1e30) for h in range(2)]
    for i in range(n//BQ):
        nk=(i+1)*BQ
        q=q_ref[i*BQ:(i+1)*BQ,:]*jnp.array(0.125,bf16)
        outs=[];lses=[]
        for h in range(2):
            qh=jnp.where(first if h==0 else ~first, q, jnp.zeros_like(q))
            s=dotnt(qh,k[:nk])*LOG2E+bias[h][:,:nk]
            sd=jnp.where(diag,s[:,nk-BQ:],-1e30)
            s=sd if i==0 else jnp.concatenate([s[:,:nk-BQ],sd],axis=1)
            m=jnp.max(s,axis=1,keepdims=True)
            p=jnp.exp2(s-m).astype(bf16)
            o=dot(p,vaug[:nk])
            tot=o[:,128:]
            outs.append(o[:,:128]/tot)
            lses.append((m+jnp.log2(tot))*(1.0/LOG2E))
        o_ref[i*BQ:(i+1)*BQ,:]=jnp.where(first,outs[0],outs[1]).astype(bf16)
        lse_ref[i*BQ:(i+1)*BQ,:]=jnp.where(first,lses[0],lses[1])

def attn_fwd(length,slopes,q,k,v):
    n,D=q.shape; np_=D//128
    spec=lambda off: pl.BlockSpec((n,128),lambda p,*_: (0,p+off))
    return pl.pallas_call(attn_fwd_kernel,
        grid_spec=pltpu.PrefetchScalarGridSpec(num_scalar_prefetch=2,grid=(np_,),
            in_specs=[spec(0)]*3,out_specs=[spec(0),spec(0)]),
        out_shape=[jax.ShapeDtypeStruct((n,D),bf16),jax.ShapeDtypeStruct((n,D),f32)],
        compiler_params=pltpu.CompilerParams(vmem_limit_bytes=48*2**20),
        cost_estimate=pl.CostEstimate(flops=int(2*2*n*n*D*2.5),bytes_accessed=n*D*12,transcendentals=n*n*10),
        name="attn_fwd")(length,slopes,q,k,v)

def split3(x):
    a=x.astype(bf16); r=x-a.astype(f32); b=r.astype(bf16); c=(r-b.astype(f32)).astype(bf16)
    return a,b,c

def attn_bwd_kernel(len_ref, slope_ref, q_ref, k_ref, v_ref, o_ref, lse_ref, do_ref, dq_ref, dk_ref, dv_ref, qa_ref, doa_ref, dqt_ref):
    pair=pl.program_id(0)
    n=q_ref.shape[0]
    nb=n//BQ
    length=len_ref[0]
    lane=lax.broadcasted_iota(jnp.int32,(1,128),1)
    sub=lane%64
    first=lane<64
    place=lax.broadcasted_iota(jnp.int32,(n,128),0)
    hi=(place//8*8).astype(f32); lo=(place%8).astype(f32)
    kf=jnp.where(sub<3,-1.0,jnp.where(sub<9,jnp.where(sub%2==1,hi,lo),jnp.where(sub==9,jnp.where(place<length,0.0,-1e30),0.0))).astype(bf16)
    vf=jnp.where(sub<3,-1.0,0.0).astype(bf16)
    k=k_ref[...]; v=v_ref[...]
    kaug=jnp.concatenate([k,kf],axis=1)
    vaug=jnp.concatenate([v,jnp.broadcast_to(vf,(n,128))],axis=1)
    q=q_ref[...]*jnp.array(0.125,bf16)
    do=do_ref[...]
    prod=do.astype(f32)*o_ref[...].astype(f32)
    same=(lax.broadcasted_iota(jnp.int32,(128,128),0)//64==lax.broadcasted_iota(jnp.int32,(128,128),1)//64).astype(bf16)
    p1,p2,p3=split3(prod)
    dd=dot(p1,same)+dot(p2,same)+dot(p3,same)
    d1,d2,d3=split3(dd)
    l1,l2,l3=split3(lse_ref[...])
    zero=jnp.zeros((n,128),bf16)
    for h in range(2):
        mine=first if h==0 else ~first
        m1=slope_ref[3*(2*pair+h)];m2=slope_ref[3*(2*pair+h)+1];m3=slope_ref[3*(2*pair+h)+2]
        mf=jnp.where(sub<5,m1,jnp.where(sub<7,m2,jnp.where(sub<9,m3,jnp.where(sub==9,1.0,0.0)))).astype(bf16)
        qf=jnp.where(sub==0,l1,jnp.where(sub==1,l2,jnp.where(sub==2,l3,jnp.broadcast_to(mf,(n,128)))))
        df=jnp.where(sub==0,d1,jnp.where(sub==1,d2,jnp.where(sub==2,d3,zero)))
        qa_ref[h]=jnp.concatenate([jnp.where(mine,q,zero),jnp.where(mine,qf,zero)],axis=1)
        doa_ref[h]=jnp.concatenate([jnp.where(mine,do,zero),jnp.where(mine,df,zero)],axis=1)
    kt=k.T
    diag=lax.broadcasted_iota(jnp.int32,(BQ,BQ),0)<=lax.broadcasted_iota(jnp.int32,(BQ,BQ),1)
    for j in range(nb):
        ks=slice(j*BQ,(j+1)*BQ); qs=slice(j*BQ,n)
        dvs=[];dks=[]
        for h in range(2):
            sT=dotnt(kaug[ks],qa_ref[h,qs,:])
            dpT=dotnt(vaug[ks],doa_ref[h,qs,:])
            p=jnp.exp(sT)
            pd=jnp.where(diag,p[:,:BQ],0.0)
            p=pd if j==nb-1 else jnp.concatenate([pd,p[:,BQ:]],axis=1)
            ds=(p*dpT).astype(bf16)
            dvs.append(dot(p.astype(bf16),do_ref[qs,:]))
            dks.append(dot(ds,q[qs]))
            t=dot(kt[64*h:64*h+64,ks],ds)
            if j==0: dqt_ref[64*h:64*h+64,:]=t
            else: dqt_ref[64*h:64*h+64,qs]+=t
        dv_ref[ks,:]=jnp.where(first,dvs[0],dvs[1]).astype(bf16)
        dk_ref[ks,:]=jnp.where(first,dks[0],dks[1]).astype(bf16)
    dq_ref[...]=(dqt_ref[...]*0.125).T.astype(bf16)

def attn_bwd(length,slopes3,q,k,v,o,lse,do):
    n,D=q.shape; np_=D//128
    spec=lambda off: pl.BlockSpec((n,128),lambda p,*_: (0,p+off))
    return pl.pallas_call(attn_bwd_kernel,
        grid_spec=pltpu.PrefetchScalarGridSpec(num_scalar_prefetch=2,grid=(np_,),
            in_specs=[spec(0)]*6,out_specs=[spec(0)]*3,
            scratch_shapes=[pltpu.VMEM((2,n,256),bf16),pltpu.VMEM((2,n,256),bf16),pltpu.VMEM((128,n),f32)]),
        out_shape=[jax.ShapeDtypeStruct((n,D),bf16)]*3,
        compiler_params=pltpu.CompilerParams(vmem_limit_bytes=48*2**20),
        cost_estimate=pl.CostEstimate(flops=int(5*2*n*n*D*2.5),bytes_accessed=n*D*20,transcendentals=n*n*10),
        name="attn_bwd")(length,slopes3,q,k,v,o,lse,do)


def layer_norm(values, gain, shift):
    center = values - jnp.mean(values, axis=-1, keepdims=True)
    spread = jnp.mean(center * center, axis=-1, keepdims=True)
    return center * lax.rsqrt(spread + 1e-05) * gain + shift


def gelu_tanh(values):
    return jax.nn.gelu(values, approximate=True)


def generic_shards(
    tokens,
    ln1_gain,
    ln1_bias,
    qkv_weight,
    qkv_bias,
    dense_weight,
    dense_bias,
    ln2_gain,
    ln2_bias,
    up_weight,
    up_bias,
    down_weight,
    down_bias,
    cotangent,
    seq_lengths,
    slot_order,
):
    rows = tokens.shape[0]
    width = tokens.shape[1]
    group = rows * lax.axis_size("seq")
    f32 = jnp.float32
    bf16 = jnp.bfloat16
    window = SEQLEN
    w_qkv, w_dense, w_up, w_down = (
        lax.all_gather(qkv_weight, ("dp", "seq"), axis=0, tiled=True),
        lax.all_gather(dense_weight, ("dp", "seq"), axis=0, tiled=True),
        lax.all_gather(up_weight, ("dp", "seq"), axis=0, tiled=True),
        lax.all_gather(down_weight, ("dp", "seq"), axis=0, tiled=True),
    )
    order_group = lax.dynamic_slice_in_dim(slot_order, lax.axis_index("dp") * SG, SG)
    every_seq = jnp.arange(seq_lengths.shape[0], dtype=jnp.int32)
    lengths_group = jnp.sum(
        jnp.where(every_seq[None, :] == order_group[:, None], seq_lengths[None, :], 0), axis=1
    )
    slot_numbers = jnp.arange(SG, dtype=jnp.int32)

    def length_of(slots):
        return jnp.sum(
            jnp.where(slots[:, None] == slot_numbers[None, :], lengths_group[None, :], 0), axis=1
        )

    first_row = lax.axis_index("seq") * rows
    window_start = jnp.minimum(first_row // SEQLEN * SEQLEN, group - window)
    key_index = window_start + jnp.arange(window, dtype=jnp.int32)
    key_slot = key_index // SEQLEN
    key_place = key_index % SEQLEN
    key_live = key_place < length_of(key_slot)
    query_index = first_row + jnp.arange(rows, dtype=jnp.int32)
    query_slot = query_index // SEQLEN
    query_place = query_index % SEQLEN
    valid = (query_place < length_of(query_slot)).astype(f32)
    allowed = (
        (query_slot[:, None] == key_slot[None, :])
        & (key_place[None, :] <= query_place[:, None])
        & key_live[None, :]
    )
    offset = (key_place[None, :] - query_place[:, None]).astype(f32)
    slopes = jnp.exp2(-8.0 * (jnp.arange(H, dtype=f32) + 1.0) / H)
    inputs = tokens.astype(f32)
    normed_one, norm_one_back = jax.vjp(layer_norm, inputs, ln1_gain, ln1_bias)
    normed_low = normed_one.astype(bf16)
    bias_full = jnp.concatenate([qkv_bias[:width], jnp.zeros((width,), f32), qkv_bias[width:]])
    joined = (jnp.dot(normed_low, w_qkv, preferred_element_type=f32) + bias_full).astype(bf16)
    query = joined[:, :width]
    keys_group, values_group = (
        lax.all_gather(joined[:, width : 2 * width], "seq", axis=0, tiled=True),
        lax.all_gather(joined[:, 2 * width :], "seq", axis=0, tiled=True),
    )
    keys_all = lax.dynamic_slice_in_dim(keys_group, window_start, window, 0)
    values_all = lax.dynamic_slice_in_dim(values_group, window_start, window, 0)

    def split_heads(matrix):
        return matrix.reshape(matrix.shape[0], H, width // H).transpose(1, 0, 2)

    def merge_heads(stack):
        return stack.transpose(1, 0, 2).reshape(stack.shape[1], width)

    head_queries = split_heads(query)
    head_keys = split_heads(keys_all)
    head_values = split_heads(values_all)

    def scores_of(head_query, head_key, head_slope):
        scores = jnp.einsum("qd,kd->qk", head_query, head_key, preferred_element_type=f32) * 0.125
        return jnp.where(allowed, scores + head_slope * offset, -1e30)

    def head_forward(packed):
        head_query, head_key, head_value, head_slope = packed
        scores = scores_of(head_query, head_key, head_slope)
        top = jnp.max(scores, axis=-1, keepdims=True)
        expo = jnp.exp(scores - top)
        totals = jnp.sum(expo, axis=-1, keepdims=True)
        probs = (expo / totals).astype(bf16)
        result = jnp.einsum("qk,kd->qd", probs, head_value, preferred_element_type=f32)
        return (result, top[:, 0] + jnp.log(totals[:, 0]))

    head_context, head_lse = lax.map(head_forward, (head_queries, head_keys, head_values, slopes))
    context = merge_heads(head_context).astype(bf16)
    hidden = inputs + jnp.dot(context, w_dense, preferred_element_type=f32) + dense_bias
    normed_two, norm_two_back = jax.vjp(layer_norm, hidden, ln2_gain, ln2_bias)
    normed_two_low = normed_two.astype(bf16)
    before = jnp.dot(normed_two_low, w_up, preferred_element_type=f32) + up_bias
    active, gelu_back = jax.vjp(gelu_tanh, before)
    active_low = active.astype(bf16)
    outputs = hidden + jnp.dot(active_low, w_down, preferred_element_type=f32) + down_bias
    block_output = outputs.astype(bf16)
    back_qkv, back_dense, back_up, back_down = (
        lax.all_gather(qkv_weight, ("dp", "seq"), axis=0, tiled=True),
        lax.all_gather(dense_weight, ("dp", "seq"), axis=0, tiled=True),
        lax.all_gather(up_weight, ("dp", "seq"), axis=0, tiled=True),
        lax.all_gather(down_weight, ("dp", "seq"), axis=0, tiled=True),
    )
    grad_out = cotangent.astype(f32) * valid[:, None]
    grad_out_low = grad_out.astype(bf16)
    grad_down_w = jnp.einsum("rf,rd->fd", active_low, grad_out_low, preferred_element_type=f32)
    grad_down_b = jnp.sum(grad_out_low.astype(f32), axis=0)
    grad_active = jnp.einsum("rd,fd->rf", grad_out_low, back_down, preferred_element_type=f32)
    (grad_before,) = gelu_back(grad_active)
    grad_before_low = grad_before.astype(bf16)
    grad_up_w = jnp.einsum("rd,rf->df", normed_two_low, grad_before_low, preferred_element_type=f32)
    grad_up_b = jnp.sum(grad_before_low.astype(f32), axis=0)
    grad_normed_two = jnp.einsum("rf,df->rd", grad_before_low, back_up, preferred_element_type=f32)
    grad_hidden_norm, grad_gain_two, grad_shift_two = norm_two_back(grad_normed_two)
    grad_hidden = grad_out + grad_hidden_norm
    grad_hidden_low = grad_hidden.astype(bf16)
    grad_dense_w = jnp.einsum("rd,re->de", context, grad_hidden_low, preferred_element_type=f32)
    grad_dense_b = jnp.sum(grad_hidden_low.astype(f32), axis=0)
    grad_context = jnp.einsum(
        "re,de->rd", grad_hidden_low, back_dense, preferred_element_type=f32
    ).astype(bf16)

    def head_backward(packed):
        head_query, head_key, head_value, head_slope, head_grad, head_norm = packed
        scores = scores_of(head_query, head_key, head_slope)
        probs = jnp.exp(scores - head_norm[:, None])
        prob_grad = jnp.einsum("qd,kd->qk", head_grad, head_value, preferred_element_type=f32)
        value_grad = jnp.einsum(
            "qk,qd->kd", probs.astype(bf16), head_grad, preferred_element_type=f32
        )
        row_dot = jnp.sum(probs * prob_grad, axis=-1, keepdims=True)
        score_grad = (probs * (prob_grad - row_dot)).astype(bf16)
        query_grad = (
            jnp.einsum("qk,kd->qd", score_grad, head_key, preferred_element_type=f32) * 0.125
        )
        key_grad = (
            jnp.einsum("qk,qd->kd", score_grad, head_query, preferred_element_type=f32) * 0.125
        )
        return (query_grad, key_grad, value_grad)

    grad_queries, grad_keys, grad_values = lax.map(
        head_backward,
        (head_queries, head_keys, head_values, slopes, split_heads(grad_context), head_lse),
    )
    empty_group = jnp.zeros((group, width), f32)
    key_terms = lax.dynamic_update_slice_in_dim(
        empty_group, merge_heads(grad_keys), window_start, 0
    )
    value_terms = lax.dynamic_update_slice_in_dim(
        empty_group, merge_heads(grad_values), window_start, 0
    )
    grad_key, grad_value = (
        lax.psum_scatter(
            key_terms.astype(jnp.bfloat16), "seq", scatter_dimension=0, tiled=True
        ).astype(jnp.float32),
        lax.psum_scatter(
            value_terms.astype(jnp.bfloat16), "seq", scatter_dimension=0, tiled=True
        ).astype(jnp.float32),
    )
    grad_query = merge_heads(grad_queries)
    grad_joined = jnp.concatenate([grad_query, grad_key, grad_value], axis=1).astype(bf16)
    grad_qkv_w = jnp.einsum("rd,rc->dc", normed_low, grad_joined, preferred_element_type=f32)
    joined_sums = jnp.sum(grad_joined.astype(f32), axis=0)
    grad_qkv_b = jnp.concatenate([joined_sums[:width], joined_sums[2 * width :]])
    grad_normed_one = jnp.einsum("rc,dc->rd", grad_joined, back_qkv, preferred_element_type=f32)
    grad_input_norm, grad_gain_one, grad_shift_one = norm_one_back(grad_normed_one)
    token_grad = (grad_hidden + grad_input_norm).astype(bf16)
    owner_qkv, owner_dense, owner_up, owner_down = (
        lax.psum_scatter(grad_qkv_w, ("dp", "seq"), scatter_dimension=0, tiled=True),
        lax.psum_scatter(grad_dense_w, ("dp", "seq"), scatter_dimension=0, tiled=True),
        lax.psum_scatter(grad_up_w, ("dp", "seq"), scatter_dimension=0, tiled=True),
        lax.psum_scatter(grad_down_w, ("dp", "seq"), scatter_dimension=0, tiled=True),
    )
    (
        total_gain_one,
        total_shift_one,
        total_qkv_b,
        total_dense_b,
        total_gain_two,
        total_shift_two,
        total_up_b,
        total_down_b,
    ) = lax.psum(
        (
            grad_gain_one,
            grad_shift_one,
            grad_qkv_b,
            grad_dense_b,
            grad_gain_two,
            grad_shift_two,
            grad_up_b,
            grad_down_b,
        ),
        ("dp", "seq"),
    )
    return (
        block_output,
        token_grad,
        total_gain_one,
        total_shift_one,
        owner_qkv,
        total_qkv_b,
        owner_dense,
        total_dense_b,
        total_gain_two,
        total_shift_two,
        owner_up,
        total_up_b,
        owner_down,
        total_down_b,
    )


ALL = ("dp", "seq")


def flat_index(z, y, c, x):
    return ((z * 2 + y) * 2 + c) * 2 + x


def permutation(move):
    pairs = []
    for z in range(4):
        for y in range(2):
            for c in range(2):
                for x in range(2):
                    pairs.append((flat_index(z, y, c, x), flat_index(*move(z, y, c, x))))
    return pairs


OVER_X = permutation(lambda z, y, c, x: (z, y, c, 1 - x))
OVER_Y = permutation(lambda z, y, c, x: (z, 1 - y, c, x))
OVER_C = permutation(lambda z, y, c, x: (z, y, 1 - c, x))
OVER_Z = [permutation(lambda z, y, c, x, k=k: ((z + k) % 4, y, c, x)) for k in range(4)]


def send(array, pairs):
    return lax.ppermute(array, ALL, pairs)


def gather_half(parts, first, second):
    own = jnp.stack(parts)
    own_core = send(own, OVER_C)
    near = send(own, first)
    near_core = send(near, OVER_C)
    both = jnp.stack([own, near])
    far = send(both, second)
    far_core = send(far, OVER_C)
    return both, far, own_core, near_core, far_core


def gather_stage(shard):
    parts = [shard] + [send(shard, OVER_Z[k]) for k in (1, 2, 3)]
    return (
        gather_half([p[0] for p in parts], OVER_X, OVER_Y),
        gather_half([p[1] for p in parts], OVER_Y, OVER_X),
    )


def assemble_kernel(put, place_ref, *refs):
    outs, sem = refs[10:-1], refs[-1]
    z, y, c, x = (place_ref[i] for i in range(4))

    def copies(go):
        for half in range(2):
            both, far, own_core, near_core, far_core = refs[5 * half : 5 * half + 5]
            for zr in range(4):
                za = (z + 4 - zr) % 4
                for near in range(2):
                    for turn in range(2):
                        for core in range(2):
                            if core == 0:
                                src = (far if turn else both).at[near, zr]
                            elif turn:
                                src = far_core.at[near, zr]
                            else:
                                src = (near_core if near else own_core).at[zr]
                            xr, yr = (near, turn) if half == 0 else (turn, near)
                            d = flat_index(
                                za, y + yr - 2 * y * yr, c + core - 2 * c * core, x + xr - 2 * x * xr
                            )
                            for b, dst in put(half, d, outs):
                                go(pltpu.make_async_copy(src.at[b], dst, sem))

    copies(lambda copy: copy.start())
    copies(lambda copy: copy.wait())


def put_blocks(half, d, outs):
    return [(b, outs[2 * half + b].at[pl.ds(pl.multiple_of(d * 32, 32), 32), :]) for b in range(2)]


def put_rows(half, d, outs):
    return [(0, outs[0].at[pl.ds(pl.multiple_of(d * 128 + half * 64, 64), 64), :])]


def assemble(place, halves, put, out_shape):
    return pl.pallas_call(
        functools.partial(assemble_kernel, put),
        grid_spec=pltpu.PrefetchScalarGridSpec(
            num_scalar_prefetch=1,
            grid=(),
            in_specs=[pl.BlockSpec(memory_space=pl.ANY)] * 10,
            out_specs=[pl.BlockSpec(memory_space=pltpu.VMEM)] * len(out_shape),
            scratch_shapes=[pltpu.SemaphoreType.DMA],
        ),
        out_shape=out_shape,
        compiler_params=pltpu.CompilerParams(vmem_limit_bytes=32 * 2**20),
        cost_estimate=pl.CostEstimate(flops=0, bytes_accessed=2 * 8 * 2**20, transcendentals=0),
        name="assemble",
    )(place, *halves[0], *halves[1])


def add_low(a, b):
    return (a.astype(f32) + b.astype(f32)).astype(bf16)


def take(array, at, axis):
    return lax.dynamic_index_in_dim(array, at, axis, keepdims=False)


def reduce_half(grads, place, x_first):
    z, y, c, x = place
    g = add_low(take(grads, c, 2), send(take(grads, 1 - c, 2), OVER_C))
    if x_first:
        g = add_low(take(g, x, 2), send(take(g, 1 - x, 2), OVER_X))
        g = add_low(take(g, y, 1), send(take(g, 1 - y, 1), OVER_Y))
    else:
        g = add_low(take(g, y, 1), send(take(g, 1 - y, 1), OVER_Y))
        g = add_low(take(g, x, 1), send(take(g, 1 - x, 1), OVER_X))
    total = take(g, z, 0).astype(f32)
    for k in (1, 2, 3):
        total = total + send(take(g, (z + k) % 4, 0), OVER_Z[k]).astype(f32)
    return total


def reduce_pair(left, right, place, x_first):
    both = jnp.concatenate(
        [left.reshape(4, 2, 2, 2, 32, 1024), right.reshape(4, 2, 2, 2, 32, 1024)], axis=4
    )
    total = reduce_half(both, place, x_first)
    return total[:32], total[32:]


def all_sum(v, place):
    v = v + send(v, OVER_C)
    v = v + send(v, OVER_X)
    v = v + send(v, OVER_Y)
    return v + send(v, OVER_Z[1]) + send(v, OVER_Z[2]) + send(v, OVER_Z[3])


def slope_table():
    slopes = np.exp2(-8.0 * (np.arange(H) + 1.0) / H).astype(np.float32)
    pieces, rest = [], slopes
    for _ in range(3):
        low = rest.astype(ml_dtypes.bfloat16).astype(np.float32)
        pieces.append(low)
        rest = rest - low
    return slopes, np.stack(pieces, axis=1).reshape(-1)


def fast_shards(
    tokens,
    ln1_gain,
    ln1_bias,
    qkv_weight,
    qkv_bias,
    dense_weight,
    dense_bias,
    ln2_gain,
    ln2_bias,
    up_weight,
    up_bias,
    down_weight,
    down_bias,
    cotangent,
    seq_lengths,
    slot_order,
):
    rows, width = tokens.shape
    dp, seq = lax.axis_index("dp"), lax.axis_index("seq")
    place = (dp // 4, (dp // 2) % 2, dp % 2, seq)
    place_vec = jnp.stack([p.astype(jnp.int32) for p in place])

    def columns(w):
        return w.reshape(32, w.shape[1] // 1024, 1024).transpose(1, 0, 2)

    shard_one = jnp.concatenate([columns(qkv_weight), dense_weight[None]]).reshape(2, 2, 32, 1024)
    shard_two = columns(up_weight).reshape(2, 2, 32, 1024)
    shard_three = down_weight.reshape(2, 1, 64, 1024)
    square = [jax.ShapeDtypeStruct((1024, 1024), bf16)] * 4
    w_q, w_k, w_v, w_dense = assemble(place_vec, gather_stage(shard_one), put_blocks, square)
    w_up = assemble(place_vec, gather_stage(shard_two), put_blocks, square)
    (w_down,) = assemble(
        place_vec, gather_stage(shard_three), put_rows, [jax.ShapeDtypeStruct((4096, 1024), bf16)]
    )

    slot = dp * SG + seq
    my_seq = lax.dynamic_index_in_dim(slot_order, slot, 0, keepdims=False)
    every_seq = jnp.arange(seq_lengths.shape[0], dtype=jnp.int32)
    length = jnp.sum(jnp.where(every_seq == my_seq, seq_lengths, 0))
    length_vec = length.reshape(1)
    valid = (jnp.arange(rows, dtype=jnp.int32) < length).astype(f32)
    slopes, slopes_split = slope_table()

    inputs = tokens.astype(f32)
    normed_one, norm_one_back = jax.vjp(layer_norm, inputs, ln1_gain, ln1_bias)
    a1 = normed_one.astype(bf16)
    query = (dot(a1, w_q) + qkv_bias[:width]).astype(bf16)
    key = dot(a1, w_k).astype(bf16)
    value = (dot(a1, w_v) + qkv_bias[width:]).astype(bf16)
    context, lse = attn_fwd(length_vec, jnp.asarray(slopes), query, key, value)
    hidden = inputs + dot(context, w_dense) + dense_bias
    normed_two, norm_two_back = jax.vjp(layer_norm, hidden, ln2_gain, ln2_bias)
    a2 = normed_two.astype(bf16)
    blocks = range(4)
    before = [dot(a2, w_up[i]) + up_bias[i * 1024 : (i + 1) * 1024] for i in blocks]
    active, gelu_back = zip(*[jax.vjp(gelu_tanh, b) for b in before])
    active = [a.astype(bf16) for a in active]
    grad_out = cotangent.astype(f32) * valid[:, None]
    grad_low = grad_out.astype(bf16)
    grad_down_b = jnp.sum(grad_out, axis=0)

    def outer(a, b):
        return jnp.einsum("rd,rf->df", a, b, preferred_element_type=f32).astype(bf16)

    grad_down_w = [outer(active[i], grad_low) for i in blocks]
    mlp = sum(dot(active[i], w_down[i * 1024 : (i + 1) * 1024]) for i in blocks)
    block_output = (hidden + mlp + down_bias).astype(bf16)
    down_terms = jnp.concatenate(grad_down_w).reshape(4, 2, 2, 2, 2, 64, 1024)
    owner_down = jnp.concatenate(
        [
            reduce_half(down_terms[:, :, :, :, 0], place, True),
            reduce_half(down_terms[:, :, :, :, 1], place, False),
        ]
    )
    grad_active = [dotnt(grad_low, w_down[i * 1024 : (i + 1) * 1024]) for i in blocks]
    grad_before = [gelu_back[i](grad_active[i])[0].astype(bf16) for i in blocks]
    grad_up_w = [outer(a2, grad_before[i]) for i in blocks]
    up_01 = reduce_pair(grad_up_w[0], grad_up_w[1], place, True)
    up_23 = reduce_pair(grad_up_w[2], grad_up_w[3], place, False)
    owner_up = jnp.concatenate(up_01 + up_23, axis=1)
    grad_up_b = jnp.concatenate([jnp.sum(g.astype(f32), axis=0) for g in grad_before])
    grad_normed_two = sum(dotnt(grad_before[i], w_up[i]) for i in blocks)
    grad_hidden_norm, grad_gain_two, grad_shift_two = norm_two_back(grad_normed_two)
    grad_hidden = grad_out + grad_hidden_norm
    grad_hidden_low = grad_hidden.astype(bf16)
    grad_dense_w = outer(context, grad_hidden_low)
    grad_dense_b = jnp.sum(grad_hidden_low.astype(f32), axis=0)
    grad_context = dotnt(grad_hidden_low, w_dense).astype(bf16)
    early = all_sum(
        jnp.concatenate(
            [grad_dense_b, grad_gain_two, grad_shift_two, grad_up_b, grad_down_b]
        ).reshape(8, 1024),
        place,
    )
    grad_q, grad_k, grad_v = attn_bwd(
        length_vec, jnp.asarray(slopes_split), query, key, value, context, lse, grad_context
    )
    owner_q, owner_k = reduce_pair(outer(a1, grad_q), outer(a1, grad_k), place, True)
    owner_v, owner_dense = reduce_pair(outer(a1, grad_v), grad_dense_w, place, False)
    grad_qkv_b = [jnp.sum(g.astype(f32), axis=0) for g in (grad_q, grad_v)]
    grad_normed_one = dotnt(grad_q, w_q) + dotnt(grad_k, w_k) + dotnt(grad_v, w_v)
    grad_input_norm, grad_gain_one, grad_shift_one = norm_one_back(grad_normed_one)
    token_grad = (grad_hidden + grad_input_norm).astype(bf16)
    late = all_sum(jnp.stack(grad_qkv_b + [grad_gain_one, grad_shift_one]), place)
    return (
        block_output,
        token_grad,
        late[2],
        late[3],
        jnp.concatenate([owner_q, owner_k, owner_v], axis=1),
        late[:2].reshape(2 * width),
        owner_dense,
        early[0],
        early[1],
        early[2],
        owner_up,
        early[3:7].reshape(4 * width),
        owner_down,
        early[7],
    )


def solution(mesh):
    in_specs = (
        P(("dp", "seq"), None),
        P(),
        P(),
        P(("dp", "seq"), None),
        P(),
        P(("dp", "seq"), None),
        P(),
        P(),
        P(),
        P(("dp", "seq"), None),
        P(),
        P(("dp", "seq"), None),
        P(),
        P(("dp", "seq"), None),
        P(),
        P(),
    )
    out_specs = (
        P(("dp", "seq"), None),
        P(("dp", "seq"), None),
        P(),
        P(),
        P(("dp", "seq"), None),
        P(),
        P(("dp", "seq"), None),
        P(),
        P(),
        P(),
        P(("dp", "seq"), None),
        P(),
        P(("dp", "seq"), None),
        P(),
    )
    body = fast_shards if mesh.shape["dp"] == 16 and mesh.shape["seq"] == 2 else generic_shards
    return jax.shard_map(body, mesh=mesh, in_specs=in_specs, out_specs=out_specs, check_vma=False)
```

```python
import functools
import itertools

import jax
import jax.numpy as jnp
import ml_dtypes
import numpy as np
from jax import lax
from jax.experimental import pallas as pl
from jax.experimental.pallas import tpu as pltpu
from jax.sharding import PartitionSpec as P

H = 16
SEQLEN = 1024
SG = 2
BQ = 256
f32 = jnp.float32
bf16 = jnp.bfloat16
NT = (((1,), (1,)), ((), ()))


def dot(a, b):
    return jnp.dot(a, b, preferred_element_type=f32)


def dotnt(a, b):
    return lax.dot_general(a, b, NT, preferred_element_type=f32)


LOG2E=1.4426950408889634

def attn_fwd_kernel(len_ref, slope_ref, q_ref, k_ref, v_ref, o_ref, lse_ref):
    pair=pl.program_id(0)+len_ref[1]
    n=q_ref.shape[0]
    length=len_ref[0]
    lane=lax.broadcasted_iota(jnp.int32,(1,128),1)
    first=lane<64
    place=lax.broadcasted_iota(jnp.int32,(1,n),1)
    ones=jnp.ones((n,128),bf16)
    vaug=jnp.concatenate([v_ref[...],ones],axis=1)
    k=k_ref[...]
    diag=lax.broadcasted_iota(jnp.int32,(BQ,BQ),1)<=lax.broadcasted_iota(jnp.int32,(BQ,BQ),0)
    bias=[jnp.where(place<length, place.astype(f32)*(slope_ref[2*pair+h]*LOG2E), -1e30) for h in range(2)]
    for i in range(n//BQ):
        nk=(i+1)*BQ
        q=q_ref[i*BQ:(i+1)*BQ,:]*jnp.array(0.125,bf16)
        outs=[];lses=[]
        for h in range(2):
            qh=jnp.where(first if h==0 else ~first, q, jnp.zeros_like(q))
            s=dotnt(qh,k[:nk])*LOG2E+bias[h][:,:nk]
            sd=jnp.where(diag,s[:,nk-BQ:],-1e30)
            s=sd if i==0 else jnp.concatenate([s[:,:nk-BQ],sd],axis=1)
            m=jnp.max(s,axis=1,keepdims=True)
            p=jnp.exp2(s-m).astype(bf16)
            o=dot(p,vaug[:nk])
            tot=o[:,128:]
            outs.append(o[:,:128]/tot)
            lses.append((m+jnp.log2(tot))*(1.0/LOG2E))
        o_ref[i*BQ:(i+1)*BQ,:]=jnp.where(first,outs[0],outs[1]).astype(bf16)
        lse_ref[i*BQ:(i+1)*BQ,:]=jnp.where(first,lses[0],lses[1])

def attn_fwd(length,slopes,qkv,start,count):
    n=qkv.shape[0]; D=qkv.shape[1]//3; full=D//128; np_=count; D=128*count
    length=jnp.stack([length,jnp.int32(start)])
    spec=lambda off: pl.BlockSpec((n,128),lambda p,*_: (0,p+off))
    return pl.pallas_call(attn_fwd_kernel,
        grid_spec=pltpu.PrefetchScalarGridSpec(num_scalar_prefetch=2,grid=(np_,),
            in_specs=[spec(start),spec(full+start),spec(2*full+start)],out_specs=[spec(0),spec(0)]),
        out_shape=[jax.ShapeDtypeStruct((n,D),bf16),jax.ShapeDtypeStruct((n,D),f32)],
        compiler_params=pltpu.CompilerParams(vmem_limit_bytes=48*2**20),
        cost_estimate=pl.CostEstimate(flops=int(2*2*n*n*D*2.5),bytes_accessed=n*D*12,transcendentals=n*n*10),
        name="attn_fwd")(length,slopes,qkv,qkv,qkv)

def split3(x):
    a=x.astype(bf16); r=x-a.astype(f32); b=r.astype(bf16); c=(r-b.astype(f32)).astype(bf16)
    return a,b,c

def attn_bwd_kernel(len_ref, slope_ref, q_ref, k_ref, v_ref, o_ref, lse_ref, do_ref, dq_ref, dk_ref, dv_ref, qa_ref, doa_ref, dqt_ref):
    pair=pl.program_id(0)+len_ref[1]
    n=q_ref.shape[0]
    nb=n//BQ
    length=len_ref[0]
    lane=lax.broadcasted_iota(jnp.int32,(1,128),1)
    sub=lane%64
    first=lane<64
    place=lax.broadcasted_iota(jnp.int32,(n,128),0)
    hi=(place//8*8).astype(f32); lo=(place%8).astype(f32)
    kf=jnp.where(sub<3,-1.0,jnp.where(sub<9,jnp.where(sub%2==1,hi,lo),jnp.where(sub==9,jnp.where(place<length,0.0,-1e30),0.0))).astype(bf16)
    vf=jnp.where(sub<3,-1.0,0.0).astype(bf16)
    k=k_ref[...]; v=v_ref[...]
    kaug=jnp.concatenate([k,kf],axis=1)
    vaug=jnp.concatenate([v,jnp.broadcast_to(vf,(n,128))],axis=1)
    q=q_ref[...]*jnp.array(0.125,bf16)
    do=do_ref[...]
    prod=do.astype(f32)*o_ref[...].astype(f32)
    same=(lax.broadcasted_iota(jnp.int32,(128,128),0)//64==lax.broadcasted_iota(jnp.int32,(128,128),1)//64).astype(bf16)
    p1,p2,p3=split3(prod)
    dd=dot(p1,same)+dot(p2,same)+dot(p3,same)
    d1,d2,d3=split3(dd)
    l1,l2,l3=split3(lse_ref[...])
    zero=jnp.zeros((n,128),bf16)
    for h in range(2):
        mine=first if h==0 else ~first
        m1=slope_ref[3*(2*pair+h)];m2=slope_ref[3*(2*pair+h)+1];m3=slope_ref[3*(2*pair+h)+2]
        mf=jnp.where(sub<5,m1,jnp.where(sub<7,m2,jnp.where(sub<9,m3,jnp.where(sub==9,1.0,0.0)))).astype(bf16)
        qf=jnp.where(sub==0,l1,jnp.where(sub==1,l2,jnp.where(sub==2,l3,jnp.broadcast_to(mf,(n,128)))))
        df=jnp.where(sub==0,d1,jnp.where(sub==1,d2,jnp.where(sub==2,d3,zero)))
        qa_ref[h]=jnp.concatenate([jnp.where(mine,q,zero),jnp.where(mine,qf,zero)],axis=1)
        doa_ref[h]=jnp.concatenate([jnp.where(mine,do,zero),jnp.where(mine,df,zero)],axis=1)
    kt=k.T
    diag=lax.broadcasted_iota(jnp.int32,(BQ,BQ),0)<=lax.broadcasted_iota(jnp.int32,(BQ,BQ),1)
    for j in range(nb):
        ks=slice(j*BQ,(j+1)*BQ); qs=slice(j*BQ,n)
        dvs=[];dks=[]
        for h in range(2):
            sT=dotnt(kaug[ks],qa_ref[h,qs,:])
            dpT=dotnt(vaug[ks],doa_ref[h,qs,:])
            p=jnp.exp(sT)
            pd=jnp.where(diag,p[:,:BQ],0.0)
            p=pd if j==nb-1 else jnp.concatenate([pd,p[:,BQ:]],axis=1)
            ds=(p*dpT).astype(bf16)
            dvs.append(dot(p.astype(bf16),do_ref[qs,:]))
            dks.append(dot(ds,q[qs]))
            t=dot(kt[64*h:64*h+64,ks],ds)
            if j==0: dqt_ref[64*h:64*h+64,:]=t
            else: dqt_ref[64*h:64*h+64,qs]+=t
        dv_ref[ks,:]=jnp.where(first,dvs[0],dvs[1]).astype(bf16)
        dk_ref[ks,:]=jnp.where(first,dks[0],dks[1]).astype(bf16)
    dq_ref[...]=(dqt_ref[...]*0.125).T.astype(bf16)

def attn_bwd(length,slopes3,qkv,o,lse,do,start,count):
    n=qkv.shape[0]; D=qkv.shape[1]//3; full=D//128; np_=count; D=128*count
    length=jnp.stack([length,jnp.int32(start)])
    spec=lambda off: pl.BlockSpec((n,128),lambda p,*_: (0,p+off))
    return pl.pallas_call(attn_bwd_kernel,
        grid_spec=pltpu.PrefetchScalarGridSpec(num_scalar_prefetch=2,grid=(np_,),
            in_specs=[spec(start),spec(full+start),spec(2*full+start),spec(start),spec(start),spec(start)],out_specs=[spec(0)]*3,
            scratch_shapes=[pltpu.VMEM((2,n,256),bf16),pltpu.VMEM((2,n,256),bf16),pltpu.VMEM((128,n),f32)]),
        out_shape=[jax.ShapeDtypeStruct((n,D),bf16)]*3,
        compiler_params=pltpu.CompilerParams(vmem_limit_bytes=48*2**20),
        cost_estimate=pl.CostEstimate(flops=int(5*2*n*n*D*2.5),bytes_accessed=n*D*20,transcendentals=n*n*10),
        name="attn_bwd")(length,slopes3,qkv,qkv,qkv,o,lse,do)


def layer_norm(values, gain, shift):
    center = values - jnp.mean(values, axis=-1, keepdims=True)
    spread = jnp.mean(center * center, axis=-1, keepdims=True)
    return center * lax.rsqrt(spread + 1e-05) * gain + shift


def gelu_tanh(values):
    return jax.nn.gelu(values, approximate=True)


def generic_shards(
    tokens,
    ln1_gain,
    ln1_bias,
    qkv_weight,
    qkv_bias,
    dense_weight,
    dense_bias,
    ln2_gain,
    ln2_bias,
    up_weight,
    up_bias,
    down_weight,
    down_bias,
    cotangent,
    seq_lengths,
    slot_order,
):
    rows = tokens.shape[0]
    width = tokens.shape[1]
    group = rows * lax.axis_size("seq")
    f32 = jnp.float32
    bf16 = jnp.bfloat16
    window = SEQLEN
    w_qkv, w_dense, w_up, w_down = (
        lax.all_gather(qkv_weight, ("dp", "seq"), axis=0, tiled=True),
        lax.all_gather(dense_weight, ("dp", "seq"), axis=0, tiled=True),
        lax.all_gather(up_weight, ("dp", "seq"), axis=0, tiled=True),
        lax.all_gather(down_weight, ("dp", "seq"), axis=0, tiled=True),
    )
    order_group = lax.dynamic_slice_in_dim(slot_order, lax.axis_index("dp") * SG, SG)
    every_seq = jnp.arange(seq_lengths.shape[0], dtype=jnp.int32)
    lengths_group = jnp.sum(
        jnp.where(every_seq[None, :] == order_group[:, None], seq_lengths[None, :], 0), axis=1
    )
    slot_numbers = jnp.arange(SG, dtype=jnp.int32)

    def length_of(slots):
        return jnp.sum(
            jnp.where(slots[:, None] == slot_numbers[None, :], lengths_group[None, :], 0), axis=1
        )

    first_row = lax.axis_index("seq") * rows
    window_start = jnp.minimum(first_row // SEQLEN * SEQLEN, group - window)
    key_index = window_start + jnp.arange(window, dtype=jnp.int32)
    key_slot = key_index // SEQLEN
    key_place = key_index % SEQLEN
    key_live = key_place < length_of(key_slot)
    query_index = first_row + jnp.arange(rows, dtype=jnp.int32)
    query_slot = query_index // SEQLEN
    query_place = query_index % SEQLEN
    valid = (query_place < length_of(query_slot)).astype(f32)
    allowed = (
        (query_slot[:, None] == key_slot[None, :])
        & (key_place[None, :] <= query_place[:, None])
        & key_live[None, :]
    )
    offset = (key_place[None, :] - query_place[:, None]).astype(f32)
    slopes = jnp.exp2(-8.0 * (jnp.arange(H, dtype=f32) + 1.0) / H)
    inputs = tokens.astype(f32)
    normed_one, norm_one_back = jax.vjp(layer_norm, inputs, ln1_gain, ln1_bias)
    normed_low = normed_one.astype(bf16)
    bias_full = jnp.concatenate([qkv_bias[:width], jnp.zeros((width,), f32), qkv_bias[width:]])
    joined = (jnp.dot(normed_low, w_qkv, preferred_element_type=f32) + bias_full).astype(bf16)
    query = joined[:, :width]
    keys_group, values_group = (
        lax.all_gather(joined[:, width : 2 * width], "seq", axis=0, tiled=True),
        lax.all_gather(joined[:, 2 * width :], "seq", axis=0, tiled=True),
    )
    keys_all = lax.dynamic_slice_in_dim(keys_group, window_start, window, 0)
    values_all = lax.dynamic_slice_in_dim(values_group, window_start, window, 0)

    def split_heads(matrix):
        return matrix.reshape(matrix.shape[0], H, width // H).transpose(1, 0, 2)

    def merge_heads(stack):
        return stack.transpose(1, 0, 2).reshape(stack.shape[1], width)

    head_queries = split_heads(query)
    head_keys = split_heads(keys_all)
    head_values = split_heads(values_all)

    def scores_of(head_query, head_key, head_slope):
        scores = jnp.einsum("qd,kd->qk", head_query, head_key, preferred_element_type=f32) * 0.125
        return jnp.where(allowed, scores + head_slope * offset, -1e30)

    def head_forward(packed):
        head_query, head_key, head_value, head_slope = packed
        scores = scores_of(head_query, head_key, head_slope)
        top = jnp.max(scores, axis=-1, keepdims=True)
        expo = jnp.exp(scores - top)
        totals = jnp.sum(expo, axis=-1, keepdims=True)
        probs = (expo / totals).astype(bf16)
        result = jnp.einsum("qk,kd->qd", probs, head_value, preferred_element_type=f32)
        return (result, top[:, 0] + jnp.log(totals[:, 0]))

    head_context, head_lse = lax.map(head_forward, (head_queries, head_keys, head_values, slopes))
    context = merge_heads(head_context).astype(bf16)
    hidden = inputs + jnp.dot(context, w_dense, preferred_element_type=f32) + dense_bias
    normed_two, norm_two_back = jax.vjp(layer_norm, hidden, ln2_gain, ln2_bias)
    normed_two_low = normed_two.astype(bf16)
    before = jnp.dot(normed_two_low, w_up, preferred_element_type=f32) + up_bias
    active, gelu_back = jax.vjp(gelu_tanh, before)
    active_low = active.astype(bf16)
    outputs = hidden + jnp.dot(active_low, w_down, preferred_element_type=f32) + down_bias
    block_output = outputs.astype(bf16)
    back_qkv, back_dense, back_up, back_down = (
        lax.all_gather(qkv_weight, ("dp", "seq"), axis=0, tiled=True),
        lax.all_gather(dense_weight, ("dp", "seq"), axis=0, tiled=True),
        lax.all_gather(up_weight, ("dp", "seq"), axis=0, tiled=True),
        lax.all_gather(down_weight, ("dp", "seq"), axis=0, tiled=True),
    )
    grad_out = cotangent.astype(f32) * valid[:, None]
    grad_out_low = grad_out.astype(bf16)
    grad_down_w = jnp.einsum("rf,rd->fd", active_low, grad_out_low, preferred_element_type=f32)
    grad_down_b = jnp.sum(grad_out_low.astype(f32), axis=0)
    grad_active = jnp.einsum("rd,fd->rf", grad_out_low, back_down, preferred_element_type=f32)
    (grad_before,) = gelu_back(grad_active)
    grad_before_low = grad_before.astype(bf16)
    grad_up_w = jnp.einsum("rd,rf->df", normed_two_low, grad_before_low, preferred_element_type=f32)
    grad_up_b = jnp.sum(grad_before_low.astype(f32), axis=0)
    grad_normed_two = jnp.einsum("rf,df->rd", grad_before_low, back_up, preferred_element_type=f32)
    grad_hidden_norm, grad_gain_two, grad_shift_two = norm_two_back(grad_normed_two)
    grad_hidden = grad_out + grad_hidden_norm
    grad_hidden_low = grad_hidden.astype(bf16)
    grad_dense_w = jnp.einsum("rd,re->de", context, grad_hidden_low, preferred_element_type=f32)
    grad_dense_b = jnp.sum(grad_hidden_low.astype(f32), axis=0)
    grad_context = jnp.einsum(
        "re,de->rd", grad_hidden_low, back_dense, preferred_element_type=f32
    ).astype(bf16)

    def head_backward(packed):
        head_query, head_key, head_value, head_slope, head_grad, head_norm = packed
        scores = scores_of(head_query, head_key, head_slope)
        probs = jnp.exp(scores - head_norm[:, None])
        prob_grad = jnp.einsum("qd,kd->qk", head_grad, head_value, preferred_element_type=f32)
        value_grad = jnp.einsum(
            "qk,qd->kd", probs.astype(bf16), head_grad, preferred_element_type=f32
        )
        row_dot = jnp.sum(probs * prob_grad, axis=-1, keepdims=True)
        score_grad = (probs * (prob_grad - row_dot)).astype(bf16)
        query_grad = (
            jnp.einsum("qk,kd->qd", score_grad, head_key, preferred_element_type=f32) * 0.125
        )
        key_grad = (
            jnp.einsum("qk,qd->kd", score_grad, head_query, preferred_element_type=f32) * 0.125
        )
        return (query_grad, key_grad, value_grad)

    grad_queries, grad_keys, grad_values = lax.map(
        head_backward,
        (head_queries, head_keys, head_values, slopes, split_heads(grad_context), head_lse),
    )
    empty_group = jnp.zeros((group, width), f32)
    key_terms = lax.dynamic_update_slice_in_dim(
        empty_group, merge_heads(grad_keys), window_start, 0
    )
    value_terms = lax.dynamic_update_slice_in_dim(
        empty_group, merge_heads(grad_values), window_start, 0
    )
    grad_key, grad_value = (
        lax.psum_scatter(
            key_terms.astype(jnp.bfloat16), "seq", scatter_dimension=0, tiled=True
        ).astype(jnp.float32),
        lax.psum_scatter(
            value_terms.astype(jnp.bfloat16), "seq", scatter_dimension=0, tiled=True
        ).astype(jnp.float32),
    )
    grad_query = merge_heads(grad_queries)
    grad_joined = jnp.concatenate([grad_query, grad_key, grad_value], axis=1).astype(bf16)
    grad_qkv_w = jnp.einsum("rd,rc->dc", normed_low, grad_joined, preferred_element_type=f32)
    joined_sums = jnp.sum(grad_joined.astype(f32), axis=0)
    grad_qkv_b = jnp.concatenate([joined_sums[:width], joined_sums[2 * width :]])
    grad_normed_one = jnp.einsum("rc,dc->rd", grad_joined, back_qkv, preferred_element_type=f32)
    grad_input_norm, grad_gain_one, grad_shift_one = norm_one_back(grad_normed_one)
    token_grad = (grad_hidden + grad_input_norm).astype(bf16)
    owner_qkv, owner_dense, owner_up, owner_down = (
        lax.psum_scatter(grad_qkv_w, ("dp", "seq"), scatter_dimension=0, tiled=True),
        lax.psum_scatter(grad_dense_w, ("dp", "seq"), scatter_dimension=0, tiled=True),
        lax.psum_scatter(grad_up_w, ("dp", "seq"), scatter_dimension=0, tiled=True),
        lax.psum_scatter(grad_down_w, ("dp", "seq"), scatter_dimension=0, tiled=True),
    )
    (
        total_gain_one,
        total_shift_one,
        total_qkv_b,
        total_dense_b,
        total_gain_two,
        total_shift_two,
        total_up_b,
        total_down_b,
    ) = lax.psum(
        (
            grad_gain_one,
            grad_shift_one,
            grad_qkv_b,
            grad_dense_b,
            grad_gain_two,
            grad_shift_two,
            grad_up_b,
            grad_down_b,
        ),
        ("dp", "seq"),
    )
    return (
        block_output,
        token_grad,
        total_gain_one,
        total_shift_one,
        owner_qkv,
        total_qkv_b,
        owner_dense,
        total_dense_b,
        total_gain_two,
        total_shift_two,
        owner_up,
        total_up_b,
        owner_down,
        total_down_b,
    )


ALL = ("dp", "seq")


def flat_index(z, y, c, x):
    return ((z * 2 + y) * 2 + c) * 2 + x


TN = (((0,), (0,)), ((), ()))
MIB = 2**20


def owner_of(place_ref, half, zr, near, turn, core, turned):
    z, y, c, x = (place_ref[i] for i in range(4))
    xr, yr = (near, turn) if half == 0 else (turn, near)
    za = (z + 4 - zr) % 4 if turned else zr
    return flat_index(za, y + yr - 2 * y * yr, c + core - 2 * c * core, x + xr - 2 * x * xr)


def start_columns(place_ref, pieces, w_ref, sems, turned):
    for half in range(2):
        for zr, near, turn, core in itertools.product(range(4), *[range(2)] * 3):
            d = owner_of(place_ref, half, zr, near, turn, core, turned)
            rows = pl.ds(pl.multiple_of(d * 32, 32), 32)
            src = pieces[4 * half + 2 * core + turn].at[near, zr]
            dst = w_ref.at[2 * half : 2 * half + 2, rows, :]
            pltpu.make_async_copy(src, dst, sems.at[half]).start()


def wait_columns(w_ref, sems, half):
    part = w_ref.at[2 * half : 2 * half + 2]
    pltpu.make_async_copy(part, part, sems.at[half]).wait()


def start_rows(place_ref, pieces, w_ref, sems):
    for zr, half, near, turn, core in itertools.product(range(4), *[range(2)] * 4):
        d = owner_of(place_ref, half, zr, near, turn, core, False)
        rows = pl.ds(pl.multiple_of(d * 128 + half * 64, 64), 64)
        src = pieces[4 * half + 2 * core + turn].at[near, zr, 0]
        pltpu.make_async_copy(src, w_ref.at[rows, :], sems.at[zr]).start()


def wait_rows(w_ref, sems, z):
    part = w_ref.at[pl.ds(pl.multiple_of(z * 1024, 1024), 1024), :]
    pltpu.make_async_copy(part, part, sems.at[z]).wait()


def dottn(a, b):
    return lax.dot_general(a, b, TN, preferred_element_type=f32)


def spec(shape, index):
    return pl.BlockSpec(shape, index)


def params(mib=56):
    return pltpu.CompilerParams(vmem_limit_bytes=mib * MIB)


PIECES = [pl.BlockSpec(memory_space=pltpu.HBM)] * 8


def qkv_kernel(place_ref, *refs):
    pieces, (a_ref, b_ref, o_ref, all_ref, w_ref, sems, out_sems) = refs[:8], refs[8:]
    step = pl.program_id(0)

    @pl.when(step == 0)
    def _():
        start_columns(place_ref, pieces, w_ref, sems, True)

    for half in range(2):
        part = slice(2 * half, 2 * half + 2)
        write = pltpu.make_async_copy(w_ref.at[part], all_ref.at[part], out_sems.at[half])

        @pl.when(step == 4 * half)
        def _():
            wait_columns(w_ref, sems, half)
            write.start()

        @pl.when(step == 5)
        def _():
            write.wait()

    w = w_ref[step // 2, :, pl.ds(pl.multiple_of(step % 2 * 512, 512), 512)]
    o_ref[...] = (dot(a_ref[...], w) + b_ref[...]).astype(bf16)


def qkv_call(place, pieces, a, b):
    n, d = a.shape
    return pl.pallas_call(
        qkv_kernel,
        grid_spec=pltpu.PrefetchScalarGridSpec(
            num_scalar_prefetch=1,
            grid=(6,),
            in_specs=PIECES
            + [spec((n, d), lambda i, *_: (0, 0)), spec((1, 512), lambda i, *_: (0, i))],
            out_specs=[
                spec((n, 512), lambda i, *_: (0, i)),
                pl.BlockSpec(memory_space=pltpu.HBM),
            ],
            scratch_shapes=[
                pltpu.VMEM((4, d, 1024), bf16),
                pltpu.SemaphoreType.DMA((2,)),
                pltpu.SemaphoreType.DMA((2,)),
            ],
        ),
        out_shape=[
            jax.ShapeDtypeStruct((n, 3 * d), bf16),
            jax.ShapeDtypeStruct((4, d, 1024), bf16),
        ],
        compiler_params=params(),
        cost_estimate=pl.CostEstimate(
            flops=2 * n * d * 3 * d, bytes_accessed=2 * (n * d + 8 * d * d + 3 * n * d), transcendentals=0
        ),
        name="qkv",
    )(place, *pieces, a, b.reshape(1, 3 * d))


def up_kernel(place_ref, *refs):
    pieces, (a_ref, b_ref, u_ref, s_ref, w_ref, sems) = refs[:8], refs[8:]
    step = pl.program_id(0)

    @pl.when(step == 0)
    def _():
        start_columns(place_ref, pieces, w_ref, sems, False)

    for half in range(2):

        @pl.when(step == 4 * half)
        def _():
            wait_columns(w_ref, sems, half)

    c = 0.7978845608028654
    w = w_ref[step // 2, :, pl.ds(pl.multiple_of(step % 2 * 512, 512), 512)]
    for r in range(0, a_ref.shape[0], 256):
        v = dot(a_ref[r : r + 256, :], w) + b_ref[...]
        square = v * v
        h = 0.5 + 0.5 * jnp.tanh(v * (c + (c * 0.044715) * square))
        u = v * h
        u_ref[r : r + 256, :] = u.astype(bf16)
        s_ref[r : r + 256, :] = (
            h + u * (1.0 - h) * (2.0 * c + (2.0 * c * 0.134145) * square)
        ).astype(bf16)


def up_call(place, pieces, a, b):
    n, d = a.shape
    ff = b.shape[0]
    kb = 512
    return pl.pallas_call(
        up_kernel,
        grid_spec=pltpu.PrefetchScalarGridSpec(
            num_scalar_prefetch=1,
            grid=(ff // kb,),
            in_specs=PIECES
            + [spec((n, d), lambda i, *_: (0, 0)), spec((1, kb), lambda i, *_: (0, i))],
            out_specs=[spec((n, kb), lambda i, *_: (0, i))] * 2,
            scratch_shapes=[pltpu.VMEM((4, d, 1024), bf16), pltpu.SemaphoreType.DMA((2,))],
        ),
        out_shape=[jax.ShapeDtypeStruct((n, ff), bf16)] * 2,
        compiler_params=params(),
        cost_estimate=pl.CostEstimate(
            flops=2 * n * d * ff, bytes_accessed=2 * (n * d + d * ff + 2 * n * ff), transcendentals=n * ff
        ),
        name="up",
    )(place, *pieces, a, b.reshape(1, ff))


def split_kernel(transposed, where_ref, a_ref, g_ref, keep_ref, give_ref, *scratch):
    core = where_ref[2]
    if transposed:
        (acc_ref,) = scratch
        acc = dottn(a_ref[...], g_ref[...])
    else:
        at_ref, acc_ref = scratch

        @pl.when(pl.program_id(0) == 0)
        def _():
            at_ref[...] = a_ref[...].T

        acc = dot(at_ref[...], g_ref[...])
    acc_ref[...] = acc.astype(bf16).reshape(acc_ref.shape)
    keep_ref[...] = acc_ref[:, pl.ds(core, 1)].reshape(keep_ref.shape)
    give_ref[...] = acc_ref[:, pl.ds(1 - core, 1)].reshape(give_ref.shape)


def down_grad_call(where, u, g):
    n, ff = u.shape
    d = g.shape[1]
    out = spec((1, 256, d), lambda i, *_: (i, 0, 0))
    return pl.pallas_call(
        functools.partial(split_kernel, True),
        grid_spec=pltpu.PrefetchScalarGridSpec(
            num_scalar_prefetch=1,
            grid=(8,),
            in_specs=[spec((n, 512), lambda i, *_: (0, i)), spec((n, d), lambda i, *_: (0, 0))],
            out_specs=[out, out],
            scratch_shapes=[pltpu.VMEM((1, 2, 256, d), bf16)],
        ),
        out_shape=[jax.ShapeDtypeStruct((8, 256, d), bf16)] * 2,
        compiler_params=params(),
        cost_estimate=pl.CostEstimate(
            flops=2 * n * d * ff, bytes_accessed=2 * (n * d + d * ff + n * ff), transcendentals=0
        ),
        name="down_grad",
    )(where, u, g)


def up_grad_call(where, a, g):
    n, d = a.shape
    ff = g.shape[1]
    out = spec((8, 64, 512), lambda i, *_: (0, 0, i))
    return pl.pallas_call(
        functools.partial(split_kernel, False),
        grid_spec=pltpu.PrefetchScalarGridSpec(
            num_scalar_prefetch=1,
            grid=(ff // 512,),
            in_specs=[spec((n, d), lambda i, *_: (0, 0)), spec((n, 512), lambda i, *_: (0, i))],
            out_specs=[out, out],
            scratch_shapes=[pltpu.VMEM((d, n), bf16), pltpu.VMEM((8, 2, 64, 512), bf16)],
        ),
        out_shape=[jax.ShapeDtypeStruct((8, 64, ff), bf16)] * 2,
        compiler_params=params(),
        cost_estimate=pl.CostEstimate(
            flops=2 * n * d * ff, bytes_accessed=2 * (n * d + d * ff + n * ff), transcendentals=0
        ),
        name="up_grad",
    )(where, a, g)


def down_kernel(place_ref, *refs):
    pieces, (u_ref, h_ref, b_ref, o_ref, acc_ref, w_ref, sems) = refs[:8], refs[8:]
    step = pl.program_id(0)

    @pl.when(step == 0)
    def _():
        start_rows(place_ref, pieces, w_ref, sems)

    wait_rows(w_ref, sems, step)
    w = w_ref[pl.ds(pl.multiple_of(step * 1024, 1024), 1024), :]

    @pl.when(step == 0)
    def _():
        acc_ref[...] = dot(u_ref[...], w)

    @pl.when((step > 0) & (step < 3))
    def _():
        acc_ref[...] += dot(u_ref[...], w)

    @pl.when(step == 3)
    def _():
        for r in range(0, u_ref.shape[0], 256):
            rows = slice(r, r + 256)
            part = acc_ref[rows, :] + dot(u_ref[rows, :], w)
            o_ref[rows, :] = (h_ref[rows, :] + part + b_ref[...]).astype(bf16)


def down_call(place, pieces, u, hidden, bias):
    n, ff = u.shape
    d = hidden.shape[1]
    whole = lambda s: spec(s, lambda i, *_: (0, 0))
    return pl.pallas_call(
        down_kernel,
        grid_spec=pltpu.PrefetchScalarGridSpec(
            num_scalar_prefetch=1,
            grid=(4,),
            in_specs=PIECES
            + [spec((n, ff // 4), lambda i, *_: (0, i)), whole((n, d)), whole((1, d))],
            out_specs=whole((n, d)),
            scratch_shapes=[
                pltpu.VMEM((n, d), f32),
                pltpu.VMEM((ff, d), bf16),
                pltpu.SemaphoreType.DMA((4,)),
            ],
        ),
        out_shape=jax.ShapeDtypeStruct((n, d), bf16),
        compiler_params=params(),
        cost_estimate=pl.CostEstimate(
            flops=2 * n * d * ff, bytes_accessed=2 * (3 * n * d + d * ff + n * ff), transcendentals=0
        ),
        name="down",
    )(place, *pieces, u, hidden, bias.reshape(1, d))


def gate_kernel(place_ref, *refs):
    pieces, (g_ref, s_ref, z_ref, b_ref, w_ref, sems) = refs[:8], refs[8:]
    step = pl.program_id(0)

    @pl.when(step == 0)
    def _():
        start_rows(place_ref, pieces, w_ref, sems)

    wait_rows(w_ref, sems, step)
    w = w_ref[pl.ds(pl.multiple_of(step * 1024, 1024), 1024), :]
    total = None
    for r in range(0, g_ref.shape[0], 256):
        rows = slice(r, r + 256)
        v = (dotnt(g_ref[rows, :], w) * s_ref[rows, :].astype(f32)).astype(bf16)
        z_ref[rows, :] = v
        part = jnp.sum(v.astype(f32).reshape(32, 8, v.shape[1]), axis=0)
        total = part if total is None else total + part
    b_ref[...] = jnp.sum(total, axis=0, keepdims=True)


def gate_call(place, pieces, g, slope):
    n, d = g.shape
    ff = slope.shape[1]
    kb = 1024
    return pl.pallas_call(
        gate_kernel,
        grid_spec=pltpu.PrefetchScalarGridSpec(
            num_scalar_prefetch=1,
            grid=(ff // kb,),
            in_specs=PIECES
            + [spec((n, d), lambda i, *_: (0, 0)), spec((n, kb), lambda i, *_: (0, i))],
            out_specs=[spec((n, kb), lambda i, *_: (0, i)), spec((1, kb), lambda i, *_: (0, i))],
            scratch_shapes=[pltpu.VMEM((ff, d), bf16), pltpu.SemaphoreType.DMA((4,))],
        ),
        out_shape=[jax.ShapeDtypeStruct((n, ff), bf16), jax.ShapeDtypeStruct((1, ff), f32)],
        compiler_params=params(),
        cost_estimate=pl.CostEstimate(
            flops=2 * n * d * ff, bytes_accessed=2 * (n * d + d * ff + 2 * n * ff), transcendentals=0
        ),
        name="gate",
    )(place, *pieces, g, slope)


def norm_back(x_ref, gain_ref, res_ref, acc_ref, out_refs, sums_ref):
    n, d = x_ref.shape

    def chunk(i, sums):
        rows = pl.ds(pl.multiple_of(i * 128, 128), 128)
        grad = acc_ref[rows, :]
        x = x_ref[rows, :].astype(f32)
        center = x - jnp.mean(x, axis=1, keepdims=True)
        rsd = lax.rsqrt(jnp.mean(center * center, axis=1, keepdims=True) + 1e-05)
        hat = center * rsd
        e = grad * gain_ref[...]
        back = rsd * (
            e - jnp.mean(e, axis=1, keepdims=True) - hat * jnp.mean(e * hat, axis=1, keepdims=True)
        )
        result = res_ref[rows, :].astype(f32) + back
        low = result.astype(bf16)
        out_refs[0][rows, :] = low
        if len(out_refs) > 1:
            out_refs[1][rows, :] = result
        fold = lambda v: jnp.sum(v.reshape(16, 8, d), axis=0)
        return sums[0] + fold(grad * hat), sums[1] + fold(grad), sums[2] + fold(low.astype(f32))

    zero = jnp.zeros((8, d), f32)
    sums = lax.fori_loop(0, n // 128, chunk, (zero, zero, zero))
    for k in range(3):
        sums_ref[k : k + 1, :] = jnp.sum(sums[k], axis=0, keepdims=True)


def norm_up_kernel(place_ref, *refs):
    pieces, (g_ref, x_ref, gain_ref, res_ref, low_ref, wide_ref, sums_ref, acc_ref, w_ref, sems) = (
        refs[:8],
        refs[8:],
    )
    step = pl.program_id(0)

    @pl.when(step == 0)
    def _():
        start_columns(place_ref, pieces, w_ref, sems, False)

    for half in range(2):

        @pl.when(step == 2 * half)
        def _():
            wait_columns(w_ref, sems, half)

    @pl.when(step == 0)
    def _():
        acc_ref[...] = dotnt(g_ref[...], w_ref[0])

    @pl.when(step > 0)
    def _():
        acc_ref[...] += dotnt(g_ref[...], w_ref[step])

    @pl.when(step == 3)
    def _():
        norm_back(x_ref, gain_ref, res_ref, acc_ref, (low_ref, wide_ref), sums_ref)


def norm_up_call(place, pieces, g, x, gain, residual):
    n, d = x.shape
    ff = g.shape[1]
    whole = lambda s: spec(s, lambda i, *_: (0, 0))
    return pl.pallas_call(
        norm_up_kernel,
        grid_spec=pltpu.PrefetchScalarGridSpec(
            num_scalar_prefetch=1,
            grid=(4,),
            in_specs=PIECES
            + [spec((n, 1024), lambda i, *_: (0, i)), whole((n, d)), whole((1, d)), whole((n, d))],
            out_specs=[whole((n, d)), whole((n, d)), whole((8, d))],
            scratch_shapes=[
                pltpu.VMEM((n, d), f32),
                pltpu.VMEM((4, d, 1024), bf16),
                pltpu.SemaphoreType.DMA((2,)),
            ],
        ),
        out_shape=[
            jax.ShapeDtypeStruct((n, d), bf16),
            jax.ShapeDtypeStruct((n, d), f32),
            jax.ShapeDtypeStruct((8, d), f32),
        ],
        compiler_params=params(),
        cost_estimate=pl.CostEstimate(
            flops=2 * n * d * ff, bytes_accessed=2 * (8 * n * d + 2 * d * ff), transcendentals=0
        ),
        name="norm_up",
    )(place, *pieces, g, x, gain.reshape(1, d), residual)


def norm_qkv_kernel(*refs):
    g_refs = refs[:3]
    w_ref, x_ref, gain_ref, res_ref, start_ref, low_ref, sums_ref, acc_ref = refs[3:]
    step = pl.program_id(0)
    for i in range(3):

        @pl.when(step == i)
        def _(i=i):
            before = start_ref[...] if i == 0 else acc_ref[...]
            acc_ref[...] = before + dotnt(g_refs[i][...], w_ref[0])

    @pl.when(step == 2)
    def _():
        norm_back(x_ref, gain_ref, res_ref, acc_ref, (low_ref,), sums_ref)


def norm_qkv_call(grads, w, x, gain, residual, start):
    n, d = x.shape
    whole = lambda s: spec(s, lambda i: (0, 0))
    return pl.pallas_call(
        norm_qkv_kernel,
        grid=(3,),
        in_specs=[whole((n, 512))] * 3
        + [spec((1, d, 512), lambda i: (i, 0, 1))]
        + [whole((n, d)), whole((1, d)), whole((n, d)), whole((n, d))],
        out_specs=[whole((n, d)), whole((8, d))],
        out_shape=[jax.ShapeDtypeStruct((n, d), bf16), jax.ShapeDtypeStruct((8, d), f32)],
        scratch_shapes=[pltpu.VMEM((n, d), f32)],
        compiler_params=params(),
        cost_estimate=pl.CostEstimate(
            flops=2 * n * d * 1536, bytes_accessed=2 * (8 * n * d + d * 3072), transcendentals=0
        ),
        name="norm_qkv",
    )(*grads, w, x, gain.reshape(1, d), residual, start)


def part_kernel(*refs):
    g_refs, w_ref, o_ref = refs[:-2], refs[-2], refs[-1]
    step = pl.program_id(0)
    for i, g_ref in enumerate(g_refs):

        @pl.when(step == i)
        def _(i=i, g_ref=g_ref):
            value = dotnt(g_ref[...], w_ref[0])
            o_ref[...] = value if i == 0 else o_ref[...] + value


def part_call(grads, w):
    n, kb = grads[0].shape
    d = w.shape[1]
    return pl.pallas_call(
        part_kernel,
        grid=(len(grads),),
        in_specs=[spec((n, kb), lambda i: (0, 0))] * len(grads)
        + [spec((1, d, kb), lambda i: (i, 0, 0))],
        out_specs=spec((n, d), lambda i: (0, 0)),
        out_shape=jax.ShapeDtypeStruct((n, d), f32),
        compiler_params=params(),
        cost_estimate=pl.CostEstimate(
            flops=2 * n * d * kb * len(grads), bytes_accessed=4 * n * d * 4, transcendentals=0
        ),
        name="part",
    )(*grads, w)


def columns_kernel(plan, lefts, where_ref, *refs):
    left_refs, right_refs = refs[:lefts], refs[lefts : lefts + len(plan)]
    keep_ref, give_ref, at_ref, acc_ref = refs[-4:]
    core = where_ref[2]
    step = pl.program_id(0)
    for i, left in enumerate(plan):

        @pl.when(step == i)
        def _(i=i, left=left):
            if i == 0 or plan[i - 1] != left:
                at_ref[...] = left_refs[left][...].T
            acc = dot(at_ref[...], right_refs[i][...])
            acc_ref[...] = acc.astype(bf16).reshape(acc_ref.shape)

    keep_ref[...] = acc_ref[:, pl.ds(core, 1)].reshape(keep_ref.shape)
    give_ref[...] = acc_ref[:, pl.ds(1 - core, 1)].reshape(give_ref.shape)


def columns_call(where, lefts, rights, plan):
    n, d = lefts[0].shape
    wide = 512 * len(rights)
    out = spec((8, 64, 512), lambda i, *_: (0, 0, i))
    return pl.pallas_call(
        functools.partial(columns_kernel, plan, len(lefts)),
        grid_spec=pltpu.PrefetchScalarGridSpec(
            num_scalar_prefetch=1,
            grid=(len(plan),),
            in_specs=[spec((n, d), lambda i, *_: (0, 0))] * len(lefts)
            + [spec((n, 512), lambda i, *_, b=b: (0, b)) for _, b in rights],
            out_specs=[out, out],
            scratch_shapes=[pltpu.VMEM((d, n), bf16), pltpu.VMEM((8, 2, 64, 512), bf16)],
        ),
        out_shape=[jax.ShapeDtypeStruct((8, 64, wide), bf16)] * 2,
        compiler_params=params(),
        cost_estimate=pl.CostEstimate(
            flops=2 * n * d * wide, bytes_accessed=2 * (2 * n * d + d * wide + n * wide), transcendentals=0
        ),
        name="columns",
    )(where, *lefts, *[r for r, _ in rights])


def permutation(move):
    pairs = []
    for z in range(4):
        for y in range(2):
            for c in range(2):
                for x in range(2):
                    pairs.append((flat_index(z, y, c, x), flat_index(*move(z, y, c, x))))
    return pairs


OVER_X = permutation(lambda z, y, c, x: (z, y, c, 1 - x))
OVER_Y = permutation(lambda z, y, c, x: (z, 1 - y, c, x))
OVER_C = permutation(lambda z, y, c, x: (z, y, 1 - c, x))
OVER_Z = [permutation(lambda z, y, c, x, k=k: ((z + k) % 4, y, c, x)) for k in range(4)]


Z_GROUPS = [
    [flat_index(z, y, c, x) for z in range(4)] for y in range(2) for c in range(2) for x in range(2)
]


def send(array, pairs):
    return lax.ppermute(array, ALL, pairs)


def tie(*trees):
    return lax.optimization_barrier(trees)


def gather_z(shard):
    return [shard] + [send(shard, OVER_Z[k]) for k in (1, 2, 3)]


def halves(parts):
    return jnp.stack([p[0] for p in parts]), jnp.stack([p[1] for p in parts])


def gather_z_line(shard):
    return lax.all_gather(shard, ALL, axis=0, tiled=False, axis_index_groups=Z_GROUPS)


def scatter_z_line(array):
    return lax.psum_scatter(array, ALL, scatter_dimension=0, tiled=False, axis_index_groups=Z_GROUPS)


def add_low(a, b):
    return (a.astype(f32) + b.astype(f32)).astype(bf16)


def take(array, at, axis):
    return lax.dynamic_index_in_dim(array, at, axis, keepdims=False)


def fold(g, at, axis, pairs):
    return take(g, at, axis), send(take(g, 1 - at, axis), pairs)


def fold_second(a, b, place):
    return fold(a, place[3], 2, OVER_X), fold(b, place[1], 1, OVER_Y)


def fold_third(pair, place):
    a, b = (add_low(*p) for p in pair)
    return fold(a, place[1], 1, OVER_Y), fold(b, place[3], 1, OVER_X)


def both(pair):
    return jnp.stack([add_low(*p) for p in pair], axis=1)


def fold_z(pair, place):
    z = place[0]
    g = both(pair)
    return [take(g, z, 0)] + [send(take(g, (z + k) % 4, 0), OVER_Z[k]) for k in (1, 2, 3)]


def total(parts):
    return sum(p.astype(f32) for p in parts)


def slope_table():
    slopes = np.exp2(-8.0 * (np.arange(H) + 1.0) / H).astype(np.float32)
    pieces, rest = [], slopes
    for _ in range(3):
        low = rest.astype(ml_dtypes.bfloat16).astype(np.float32)
        pieces.append(low)
        rest = rest - low
    return slopes, np.stack(pieces, axis=1).reshape(-1)


def moments(v):
    mean = jnp.mean(v, axis=-1, keepdims=True)
    center = v - mean
    return center, lax.rsqrt(jnp.mean(center * center, axis=-1, keepdims=True) + 1e-05)


def fast_shards(
    tokens,
    ln1_gain,
    ln1_bias,
    qkv_weight,
    qkv_bias,
    dense_weight,
    dense_bias,
    ln2_gain,
    ln2_bias,
    up_weight,
    up_bias,
    down_weight,
    down_bias,
    cotangent,
    seq_lengths,
    slot_order,
):
    rows, width = tokens.shape
    dp, seq = lax.axis_index("dp"), lax.axis_index("seq")
    place = (dp // 4, (dp // 2) % 2, dp % 2, seq)
    place_vec = jnp.stack([p.astype(jnp.int32) for p in place])

    def columns(w):
        return w.reshape(32, w.shape[1] // 1024, 1024).transpose(1, 0, 2)

    one = jnp.concatenate([columns(qkv_weight), dense_weight[None]]).reshape(2, 2, 32, 1024)
    two = columns(up_weight).reshape(2, 2, 32, 1024)
    three = down_weight.reshape(2, 1, 64, 1024)

    slot = dp * SG + seq
    my_seq = lax.dynamic_index_in_dim(slot_order, slot, 0, keepdims=False)
    every_seq = jnp.arange(seq_lengths.shape[0], dtype=jnp.int32)
    length = jnp.sum(jnp.where(every_seq == my_seq, seq_lengths, 0))
    valid = (jnp.arange(rows, dtype=jnp.int32) < length).astype(f32)
    slopes, slopes_split = slope_table()
    bias_full = jnp.concatenate([qkv_bias[:width], jnp.zeros((width,), f32), qkv_bias[width:]])

    one_z = gather_z(one)
    center, rsd = moments(tokens.astype(f32))
    a1 = (center * rsd * ln1_gain + ln1_bias).astype(bf16)
    grad_low = cotangent * valid[:, None].astype(bf16)
    one_z, a1, grad_low, two = tie(one_z, a1, grad_low, two)

    a, b = halves(one_z)
    one_x, one_y = send(a, OVER_X), send(b, OVER_Y)
    two_z = gather_z_line(two)
    one_x, one_y = tie(one_x, one_y)

    one_a, one_b = jnp.stack([a, one_x]), jnp.stack([b, one_y])
    one_xy, one_yx = send(one_a, OVER_Y), send(one_b, OVER_X)
    one_ca, one_cb = send(one_a, OVER_C), send(one_b, OVER_C)
    one_xy, one_yx, one_ca, one_cb, two_z, three = tie(one_xy, one_yx, one_ca, one_cb, two_z, three)
    one_cxy, one_cyx = send(one_xy, OVER_C), send(one_yx, OVER_C)
    a, b = two_z[:, 0], two_z[:, 1]
    one_cxy, one_cyx, a, b, three = tie(one_cxy, one_cyx, a, b, three)

    two_x, two_y = send(a, OVER_X), send(b, OVER_Y)
    three_z = gather_z_line(three)
    pieces = (one_a, one_xy, one_ca, one_cxy, one_b, one_yx, one_cb, one_cyx)
    qkv, w_one = qkv_call(place_vec, pieces, a1, bias_full)
    qkv, two_x, two_y = tie(qkv, two_x, two_y)

    two_a, two_b = jnp.stack([a, two_x]), jnp.stack([b, two_y])
    two_xy, two_yx = send(two_a, OVER_Y), send(two_b, OVER_X)
    two_ca, two_cb = send(two_a, OVER_C), send(two_b, OVER_C)
    context, lse = attn_fwd(length, jnp.asarray(slopes), qkv, 0, 8)
    context, two_xy, two_yx, two_ca, two_cb, three_z = tie(
        context, two_xy, two_yx, two_ca, two_cb, three_z
    )

    two_cxy, two_cyx = send(two_xy, OVER_C), send(two_yx, OVER_C)
    a, b = three_z[:, 0], three_z[:, 1]
    three_x, three_y = send(a, OVER_X), send(b, OVER_Y)
    hidden = tokens.astype(f32) + dot(context, w_one[3]) + dense_bias
    center, rsd = moments(hidden)
    a2 = (center * rsd * ln2_gain + ln2_bias).astype(bf16)
    a2, hidden, two_cxy, two_cyx, three_x, three_y = tie(
        a2, hidden, two_cxy, two_cyx, three_x, three_y
    )

    up_pieces = (two_a, two_xy, two_ca, two_cxy, two_b, two_yx, two_cb, two_cyx)
    three_a, three_b = jnp.stack([a, three_x]), jnp.stack([b, three_y])
    three_xy, three_yx = send(three_a, OVER_Y), send(three_b, OVER_X)
    three_ca, three_cb = send(three_a, OVER_C), send(three_b, OVER_C)
    active, slope = up_call(place_vec, up_pieces, a2, up_bias)
    active, slope, grad_low = tie(active, slope, grad_low)

    down_keep, down_give = down_grad_call(place_vec, active, grad_low)
    down_keep, down_give, three_xy, three_yx, three_ca, three_cb, grad_low = tie(
        down_keep, down_give, three_xy, three_yx, three_ca, three_cb, grad_low
    )
    three_cxy, three_cyx = send(three_xy, OVER_C), send(three_yx, OVER_C)
    down_b = jnp.sum(grad_low.astype(f32), axis=0)
    active, hidden, down_give, three_cxy, three_cyx, down_b = tie(
        active, hidden, down_give, three_cxy, three_cyx, down_b
    )

    down_pieces = (
        three_a, three_xy, three_ca, three_cxy, three_b, three_yx, three_cb, three_cyx
    )
    down_got = send(down_give, OVER_C)
    block_output = down_call(place_vec, down_pieces, active, hidden, down_bias)
    block_output, down_got, grad_low = tie(block_output, down_got, grad_low)

    down = add_low(down_keep, down_got).reshape(4, 2, 2, 2, 64, 1024)
    down = fold_second(down[:, :, :, 0], down[:, :, :, 1], place)
    grad_before, up_b = gate_call(place_vec, down_pieces, grad_low, slope)
    grad_before, a2 = tie(grad_before, a2)
    up_keep, up_give = up_grad_call(place_vec, a2, grad_before)
    grad_before, up_keep, up_give, down = tie(grad_before, up_keep, up_give, down)

    down = fold_third(down, place)
    up_got = send(up_give, OVER_C)
    grad_low_hidden, grad_hidden, sums = norm_up_call(
        place_vec, up_pieces, grad_before, hidden, ln2_gain, grad_low
    )
    grad_low_hidden, grad_hidden, sums, down, up_got = tie(
        grad_low_hidden, grad_hidden, sums, down, up_got
    )

    owner_down = scatter_z_line(both(down))
    early = jnp.concatenate([sums[2], sums[0], sums[1], up_b.reshape(4096), down_b]).reshape(8, 1024)
    early = lax.all_gather(early, ALL, axis=0, tiled=False)
    up = add_low(up_keep, up_got).reshape(4, 2, 2, 32, 4096)
    up = fold_second(up[..., :2048], up[..., 2048:], place)
    grad_context = dotnt(grad_low_hidden, w_one[3]).astype(bf16)
    q0, k0, v0 = attn_bwd(length, jnp.asarray(slopes_split), qkv, context, lse, grad_context, 0, 4)
    qkv, q0, k0, v0, up, a1 = tie(qkv, q0, k0, v0, up, a1)

    up = fold_third(up, place)
    third_keep, third_give = columns_call(
        place_vec,
        [context, a1],
        [(grad_low_hidden, 0), (grad_low_hidden, 1), (q0, 0), (k0, 0), (v0, 0)],
        (0, 0, 1, 1, 1),
    )
    third_keep, third_give, qkv = tie(third_keep, third_give, qkv)

    third_got = send(third_give, OVER_C)
    q1, k1, v1 = attn_bwd(length, jnp.asarray(slopes_split), qkv, context, lse, grad_context, 4, 4)
    q1, k1, v1, third_got, up = tie(q1, k1, v1, third_got, up)

    owner_up = scatter_z_line(both(up))
    third = add_low(third_keep, third_got).reshape(4, 2, 2, 32, 2560)
    third = fold_second(third[..., :1280], third[..., 1280:], place)
    last_keep, last_give = columns_call(place_vec, [a1], [(q1, 0), (k1, 0), (v1, 0)], (0, 0, 0))
    last_keep, last_give, q0, q1, k1, v1 = tie(last_keep, last_give, q0, q1, k1, v1)

    last_got = send(last_give, OVER_C)
    part = part_call([q0, k0, v0], w_one)
    part, last_got, third = tie(part, last_got, third)
    third = fold_third(third, place)
    last = add_low(last_keep, last_got).reshape(4, 2, 2, 32, 1536)
    last = fold_second(last[..., :768], last[..., 768:], place)
    qkv_b = [jnp.sum(g.astype(f32), axis=0) for g in (q0, q1, v0, v1)]
    token_grad, sums = norm_qkv_call([q1, k1, v1], w_one, tokens, ln1_gain, grad_hidden, part)
    token_grad, sums, last, third = tie(token_grad, sums, last, third)

    last = fold_third(last, place)
    third = fold_z(third, place)
    late = jnp.concatenate(qkv_b + [sums[0], sums[1]]).reshape(4, 1024)
    late_c = send(late, OVER_C)
    last, third, late, late_c = tie(last, third, late, late_c)

    last = fold_z(last, place)
    late = late + late_c
    late_x = send(late, OVER_X)
    third = total(third)
    third = jnp.concatenate([third[0], third[1]], axis=1)
    last, late, late_x, third, owner_up, owner_down, early = tie(
        last, late, late_x, third, owner_up, owner_down, early
    )
    late = late + late_x
    late_y = send(late, OVER_Y)
    early = jnp.sum(early, axis=0)
    owner_down = owner_down.astype(f32).reshape(128, 1024)
    owner_up = owner_up.astype(f32)
    owner_up = jnp.concatenate([owner_up[0], owner_up[1]], axis=1)
    late, late_y = tie(late, late_y)
    late = late + late_y
    late = late + send(late, OVER_Z[1]) + send(late, OVER_Z[2]) + send(late, OVER_Z[3])
    last = total(last)
    last = jnp.concatenate([last[0], last[1]], axis=1)
    owner_qkv = jnp.concatenate(
        [
            part
            for i in range(3)
            for part in (third[:, 1024 + 512 * i : 1536 + 512 * i], last[:, 512 * i : 512 * i + 512])
        ],
        axis=1,
    )
    return (
        block_output,
        token_grad,
        late[2],
        late[3],
        owner_qkv,
        late[:2].reshape(2 * width),
        third[:, :1024],
        early[0],
        early[1],
        early[2],
        owner_up,
        early[3:7].reshape(4 * width),
        owner_down,
        early[7],
    )


def solution(mesh):
    in_specs = (
        P(("dp", "seq"), None),
        P(),
        P(),
        P(("dp", "seq"), None),
        P(),
        P(("dp", "seq"), None),
        P(),
        P(),
        P(),
        P(("dp", "seq"), None),
        P(),
        P(("dp", "seq"), None),
        P(),
        P(("dp", "seq"), None),
        P(),
        P(),
    )
    out_specs = (
        P(("dp", "seq"), None),
        P(("dp", "seq"), None),
        P(),
        P(),
        P(("dp", "seq"), None),
        P(),
        P(("dp", "seq"), None),
        P(),
        P(),
        P(),
        P(("dp", "seq"), None),
        P(),
        P(("dp", "seq"), None),
        P(),
    )
    body = fast_shards if mesh.shape["dp"] == 16 and mesh.shape["seq"] == 2 else generic_shards
    return jax.shard_map(body, mesh=mesh, in_specs=in_specs, out_specs=out_specs, check_vma=False)
```

```python
import functools
import itertools

import jax
import jax.numpy as jnp
import ml_dtypes
import numpy as np
from jax import lax
from jax.experimental import pallas as pl
from jax.experimental.layout import Layout, with_layout_constraint
from jax.experimental.pallas import tpu as pltpu
from jax.sharding import PartitionSpec as P

H = 16
SEQLEN = 1024
SG = 2
BQ = 256
f32 = jnp.float32
bf16 = jnp.bfloat16
NT = (((1,), (1,)), ((), ()))


def dot(a, b):
    return jnp.dot(a, b, preferred_element_type=f32)


def dotnt(a, b):
    return lax.dot_general(a, b, NT, preferred_element_type=f32)


LOG2E=1.4426950408889634

def attn_fwd_kernel(len_ref, slope_ref, q_ref, k_ref, v_ref, o_ref, lse_ref):
    pair=pl.program_id(0)+len_ref[1]
    n=q_ref.shape[0]
    length=len_ref[0]
    lane=lax.broadcasted_iota(jnp.int32,(1,128),1)
    first=lane<64
    place=lax.broadcasted_iota(jnp.int32,(1,n),1)
    ones=jnp.ones((n,128),bf16)
    vaug=jnp.concatenate([v_ref[...],ones],axis=1)
    k=k_ref[...]
    diag=lax.broadcasted_iota(jnp.int32,(BQ,BQ),1)<=lax.broadcasted_iota(jnp.int32,(BQ,BQ),0)
    bias=[jnp.where(place<length, place.astype(f32)*(slope_ref[2*pair+h]*LOG2E), -1e30) for h in range(2)]
    for i in range(n//BQ):
        nk=(i+1)*BQ
        q=q_ref[i*BQ:(i+1)*BQ,:]*jnp.array(0.125,bf16)
        outs=[];lses=[]
        for h in range(2):
            qh=jnp.where(first if h==0 else ~first, q, jnp.zeros_like(q))
            s=dotnt(qh,k[:nk])*LOG2E+bias[h][:,:nk]
            sd=jnp.where(diag,s[:,nk-BQ:],-1e30)
            s=sd if i==0 else jnp.concatenate([s[:,:nk-BQ],sd],axis=1)
            m=jnp.max(s,axis=1,keepdims=True)
            p=jnp.exp2(s-m).astype(bf16)
            o=dot(p,vaug[:nk])
            tot=o[:,128:]
            outs.append(o[:,:128]/tot)
            lses.append((m+jnp.log2(tot))*(1.0/LOG2E))
        o_ref[i*BQ:(i+1)*BQ,:]=jnp.where(first,outs[0],outs[1]).astype(bf16)
        lse_ref[i*BQ:(i+1)*BQ,:]=jnp.where(first,lses[0],lses[1])

def attn_fwd(length,slopes,qkv,start):
    n=qkv.shape[0]; D=qkv.shape[1]//3; np_=D//128
    length=jnp.stack([length,jnp.int32(start)])
    spec=lambda off: pl.BlockSpec((n,128),lambda p,*_: (0,p+off))
    return pl.pallas_call(attn_fwd_kernel,
        grid_spec=pltpu.PrefetchScalarGridSpec(num_scalar_prefetch=2,grid=(np_,),
            in_specs=[spec(0),spec(np_),spec(2*np_)],out_specs=[spec(0),spec(0)]),
        out_shape=[jax.ShapeDtypeStruct((n,D),bf16),jax.ShapeDtypeStruct((n,D),f32)],
        compiler_params=pltpu.CompilerParams(vmem_limit_bytes=63*2**20),
        cost_estimate=pl.CostEstimate(flops=int(2*2*n*n*D*2.5),bytes_accessed=n*D*12,transcendentals=n*n*10),
        name="attn_fwd")(length,slopes,qkv,qkv,qkv)

def split3(x):
    a=x.astype(bf16); r=x-a.astype(f32); b=r.astype(bf16); c=(r-b.astype(f32)).astype(bf16)
    return a,b,c

def attn_bwd_kernel(len_ref, slope_ref, q_ref, k_ref, v_ref, o_ref, lse_ref, do_ref, dq_ref, dk_ref, dv_ref, qa_ref, doa_ref, dqt_ref):
    pair=pl.program_id(0)+len_ref[1]
    n=q_ref.shape[0]
    nb=n//BQ
    length=len_ref[0]
    lane=lax.broadcasted_iota(jnp.int32,(1,128),1)
    sub=lane%64
    first=lane<64
    place=lax.broadcasted_iota(jnp.int32,(n,128),0)
    hi=(place//8*8).astype(f32); lo=(place%8).astype(f32)
    kf=jnp.where(sub<3,-1.0,jnp.where(sub<9,jnp.where(sub%2==1,hi,lo),jnp.where(sub==9,jnp.where(place<length,0.0,-1e30),0.0))).astype(bf16)
    vf=jnp.where(sub<3,-1.0,0.0).astype(bf16)
    k=k_ref[...]; v=v_ref[...]
    kaug=jnp.concatenate([k,kf],axis=1)
    vaug=jnp.concatenate([v,jnp.broadcast_to(vf,(n,128))],axis=1)
    q=q_ref[...]*jnp.array(0.125,bf16)
    do=do_ref[...]
    prod=do.astype(f32)*o_ref[...].astype(f32)
    same=(lax.broadcasted_iota(jnp.int32,(128,128),0)//64==lax.broadcasted_iota(jnp.int32,(128,128),1)//64).astype(bf16)
    p1,p2,p3=split3(prod)
    dd=dot(p1,same)+dot(p2,same)+dot(p3,same)
    d1,d2,d3=split3(dd)
    l1,l2,l3=split3(lse_ref[...])
    zero=jnp.zeros((n,128),bf16)
    for h in range(2):
        mine=first if h==0 else ~first
        m1=slope_ref[3*(2*pair+h)];m2=slope_ref[3*(2*pair+h)+1];m3=slope_ref[3*(2*pair+h)+2]
        mf=jnp.where(sub<5,m1,jnp.where(sub<7,m2,jnp.where(sub<9,m3,jnp.where(sub==9,1.0,0.0)))).astype(bf16)
        qf=jnp.where(sub==0,l1,jnp.where(sub==1,l2,jnp.where(sub==2,l3,jnp.broadcast_to(mf,(n,128)))))
        df=jnp.where(sub==0,d1,jnp.where(sub==1,d2,jnp.where(sub==2,d3,zero)))
        qa_ref[h]=jnp.concatenate([jnp.where(mine,q,zero),jnp.where(mine,qf,zero)],axis=1)
        doa_ref[h]=jnp.concatenate([jnp.where(mine,do,zero),jnp.where(mine,df,zero)],axis=1)
    kt=k.T
    diag=lax.broadcasted_iota(jnp.int32,(BQ,BQ),0)<=lax.broadcasted_iota(jnp.int32,(BQ,BQ),1)
    for j in range(nb):
        ks=slice(j*BQ,(j+1)*BQ); qs=slice(j*BQ,n)
        dvs=[];dks=[]
        for h in range(2):
            sT=dotnt(kaug[ks],qa_ref[h,qs,:])
            dpT=dotnt(vaug[ks],doa_ref[h,qs,:])
            p=jnp.exp(sT)
            pd=jnp.where(diag,p[:,:BQ],0.0)
            p=pd if j==nb-1 else jnp.concatenate([pd,p[:,BQ:]],axis=1)
            ds=(p*dpT).astype(bf16)
            dvs.append(dot(p.astype(bf16),do_ref[qs,:]))
            dks.append(dot(ds,q[qs]))
            t=dot(kt[64*h:64*h+64,ks],ds)
            if j==0: dqt_ref[64*h:64*h+64,:]=t
            else: dqt_ref[64*h:64*h+64,qs]+=t
        dv_ref[ks,:]=jnp.where(first,dvs[0],dvs[1]).astype(bf16)
        dk_ref[ks,:]=jnp.where(first,dks[0],dks[1]).astype(bf16)
    dq_ref[...]=(dqt_ref[...]*0.125).T.astype(bf16)

def attn_bwd(length,slopes3,qkv,o,lse,do,start):
    n=qkv.shape[0]; D=qkv.shape[1]//3; np_=D//128
    length=jnp.stack([length,jnp.int32(start)])
    spec=lambda off: pl.BlockSpec((n,128),lambda p,*_: (0,p+off))
    return pl.pallas_call(attn_bwd_kernel,
        grid_spec=pltpu.PrefetchScalarGridSpec(num_scalar_prefetch=2,grid=(np_,),
            in_specs=[spec(0),spec(np_),spec(2*np_),spec(0),spec(0),spec(start)],out_specs=[spec(0)]*3,
            scratch_shapes=[pltpu.VMEM((2,n,256),bf16),pltpu.VMEM((2,n,256),bf16),pltpu.VMEM((128,n),f32)]),
        out_shape=[jax.ShapeDtypeStruct((n,D),bf16)]*3,
        compiler_params=pltpu.CompilerParams(vmem_limit_bytes=48*2**20),
        cost_estimate=pl.CostEstimate(flops=int(5*2*n*n*D*2.5),bytes_accessed=n*D*20,transcendentals=n*n*10),
        name="attn_bwd")(length,slopes3,qkv,qkv,qkv,o,lse,do)


def layer_norm(values, gain, shift):
    center = values - jnp.mean(values, axis=-1, keepdims=True)
    spread = jnp.mean(center * center, axis=-1, keepdims=True)
    return center * lax.rsqrt(spread + 1e-05) * gain + shift


def gelu_tanh(values):
    return jax.nn.gelu(values, approximate=True)


def generic_shards(
    tokens,
    ln1_gain,
    ln1_bias,
    qkv_weight,
    qkv_bias,
    dense_weight,
    dense_bias,
    ln2_gain,
    ln2_bias,
    up_weight,
    up_bias,
    down_weight,
    down_bias,
    cotangent,
    seq_lengths,
    slot_order,
):
    rows = tokens.shape[0]
    width = tokens.shape[1]
    group = rows * lax.axis_size("seq")
    f32 = jnp.float32
    bf16 = jnp.bfloat16
    window = SEQLEN
    w_qkv, w_dense, w_up, w_down = (
        lax.all_gather(qkv_weight, ("dp", "seq"), axis=0, tiled=True),
        lax.all_gather(dense_weight, ("dp", "seq"), axis=0, tiled=True),
        lax.all_gather(up_weight, ("dp", "seq"), axis=0, tiled=True),
        lax.all_gather(down_weight, ("dp", "seq"), axis=0, tiled=True),
    )
    order_group = lax.dynamic_slice_in_dim(slot_order, lax.axis_index("dp") * SG, SG)
    every_seq = jnp.arange(seq_lengths.shape[0], dtype=jnp.int32)
    lengths_group = jnp.sum(
        jnp.where(every_seq[None, :] == order_group[:, None], seq_lengths[None, :], 0), axis=1
    )
    slot_numbers = jnp.arange(SG, dtype=jnp.int32)

    def length_of(slots):
        return jnp.sum(
            jnp.where(slots[:, None] == slot_numbers[None, :], lengths_group[None, :], 0), axis=1
        )

    first_row = lax.axis_index("seq") * rows
    window_start = jnp.minimum(first_row // SEQLEN * SEQLEN, group - window)
    key_index = window_start + jnp.arange(window, dtype=jnp.int32)
    key_slot = key_index // SEQLEN
    key_place = key_index % SEQLEN
    key_live = key_place < length_of(key_slot)
    query_index = first_row + jnp.arange(rows, dtype=jnp.int32)
    query_slot = query_index // SEQLEN
    query_place = query_index % SEQLEN
    valid = (query_place < length_of(query_slot)).astype(f32)
    allowed = (
        (query_slot[:, None] == key_slot[None, :])
        & (key_place[None, :] <= query_place[:, None])
        & key_live[None, :]
    )
    offset = (key_place[None, :] - query_place[:, None]).astype(f32)
    slopes = jnp.exp2(-8.0 * (jnp.arange(H, dtype=f32) + 1.0) / H)
    inputs = tokens.astype(f32)
    normed_one, norm_one_back = jax.vjp(layer_norm, inputs, ln1_gain, ln1_bias)
    normed_low = normed_one.astype(bf16)
    bias_full = jnp.concatenate([qkv_bias[:width], jnp.zeros((width,), f32), qkv_bias[width:]])
    joined = (jnp.dot(normed_low, w_qkv, preferred_element_type=f32) + bias_full).astype(bf16)
    query = joined[:, :width]
    keys_group, values_group = (
        lax.all_gather(joined[:, width : 2 * width], "seq", axis=0, tiled=True),
        lax.all_gather(joined[:, 2 * width :], "seq", axis=0, tiled=True),
    )
    keys_all = lax.dynamic_slice_in_dim(keys_group, window_start, window, 0)
    values_all = lax.dynamic_slice_in_dim(values_group, window_start, window, 0)

    def split_heads(matrix):
        return matrix.reshape(matrix.shape[0], H, width // H).transpose(1, 0, 2)

    def merge_heads(stack):
        return stack.transpose(1, 0, 2).reshape(stack.shape[1], width)

    head_queries = split_heads(query)
    head_keys = split_heads(keys_all)
    head_values = split_heads(values_all)

    def scores_of(head_query, head_key, head_slope):
        scores = jnp.einsum("qd,kd->qk", head_query, head_key, preferred_element_type=f32) * 0.125
        return jnp.where(allowed, scores + head_slope * offset, -1e30)

    def head_forward(packed):
        head_query, head_key, head_value, head_slope = packed
        scores = scores_of(head_query, head_key, head_slope)
        top = jnp.max(scores, axis=-1, keepdims=True)
        expo = jnp.exp(scores - top)
        totals = jnp.sum(expo, axis=-1, keepdims=True)
        probs = (expo / totals).astype(bf16)
        result = jnp.einsum("qk,kd->qd", probs, head_value, preferred_element_type=f32)
        return (result, top[:, 0] + jnp.log(totals[:, 0]))

    head_context, head_lse = lax.map(head_forward, (head_queries, head_keys, head_values, slopes))
    context = merge_heads(head_context).astype(bf16)
    hidden = inputs + jnp.dot(context, w_dense, preferred_element_type=f32) + dense_bias
    normed_two, norm_two_back = jax.vjp(layer_norm, hidden, ln2_gain, ln2_bias)
    normed_two_low = normed_two.astype(bf16)
    before = jnp.dot(normed_two_low, w_up, preferred_element_type=f32) + up_bias
    active, gelu_back = jax.vjp(gelu_tanh, before)
    active_low = active.astype(bf16)
    outputs = hidden + jnp.dot(active_low, w_down, preferred_element_type=f32) + down_bias
    block_output = outputs.astype(bf16)
    back_qkv, back_dense, back_up, back_down = (
        lax.all_gather(qkv_weight, ("dp", "seq"), axis=0, tiled=True),
        lax.all_gather(dense_weight, ("dp", "seq"), axis=0, tiled=True),
        lax.all_gather(up_weight, ("dp", "seq"), axis=0, tiled=True),
        lax.all_gather(down_weight, ("dp", "seq"), axis=0, tiled=True),
    )
    grad_out = cotangent.astype(f32) * valid[:, None]
    grad_out_low = grad_out.astype(bf16)
    grad_down_w = jnp.einsum("rf,rd->fd", active_low, grad_out_low, preferred_element_type=f32)
    grad_down_b = jnp.sum(grad_out_low.astype(f32), axis=0)
    grad_active = jnp.einsum("rd,fd->rf", grad_out_low, back_down, preferred_element_type=f32)
    (grad_before,) = gelu_back(grad_active)
    grad_before_low = grad_before.astype(bf16)
    grad_up_w = jnp.einsum("rd,rf->df", normed_two_low, grad_before_low, preferred_element_type=f32)
    grad_up_b = jnp.sum(grad_before_low.astype(f32), axis=0)
    grad_normed_two = jnp.einsum("rf,df->rd", grad_before_low, back_up, preferred_element_type=f32)
    grad_hidden_norm, grad_gain_two, grad_shift_two = norm_two_back(grad_normed_two)
    grad_hidden = grad_out + grad_hidden_norm
    grad_hidden_low = grad_hidden.astype(bf16)
    grad_dense_w = jnp.einsum("rd,re->de", context, grad_hidden_low, preferred_element_type=f32)
    grad_dense_b = jnp.sum(grad_hidden_low.astype(f32), axis=0)
    grad_context = jnp.einsum(
        "re,de->rd", grad_hidden_low, back_dense, preferred_element_type=f32
    ).astype(bf16)

    def head_backward(packed):
        head_query, head_key, head_value, head_slope, head_grad, head_norm = packed
        scores = scores_of(head_query, head_key, head_slope)
        probs = jnp.exp(scores - head_norm[:, None])
        prob_grad = jnp.einsum("qd,kd->qk", head_grad, head_value, preferred_element_type=f32)
        value_grad = jnp.einsum(
            "qk,qd->kd", probs.astype(bf16), head_grad, preferred_element_type=f32
        )
        row_dot = jnp.sum(probs * prob_grad, axis=-1, keepdims=True)
        score_grad = (probs * (prob_grad - row_dot)).astype(bf16)
        query_grad = (
            jnp.einsum("qk,kd->qd", score_grad, head_key, preferred_element_type=f32) * 0.125
        )
        key_grad = (
            jnp.einsum("qk,qd->kd", score_grad, head_query, preferred_element_type=f32) * 0.125
        )
        return (query_grad, key_grad, value_grad)

    grad_queries, grad_keys, grad_values = lax.map(
        head_backward,
        (head_queries, head_keys, head_values, slopes, split_heads(grad_context), head_lse),
    )
    empty_group = jnp.zeros((group, width), f32)
    key_terms = lax.dynamic_update_slice_in_dim(
        empty_group, merge_heads(grad_keys), window_start, 0
    )
    value_terms = lax.dynamic_update_slice_in_dim(
        empty_group, merge_heads(grad_values), window_start, 0
    )
    grad_key, grad_value = (
        lax.psum_scatter(
            key_terms.astype(jnp.bfloat16), "seq", scatter_dimension=0, tiled=True
        ).astype(jnp.float32),
        lax.psum_scatter(
            value_terms.astype(jnp.bfloat16), "seq", scatter_dimension=0, tiled=True
        ).astype(jnp.float32),
    )
    grad_query = merge_heads(grad_queries)
    grad_joined = jnp.concatenate([grad_query, grad_key, grad_value], axis=1).astype(bf16)
    grad_qkv_w = jnp.einsum("rd,rc->dc", normed_low, grad_joined, preferred_element_type=f32)
    joined_sums = jnp.sum(grad_joined.astype(f32), axis=0)
    grad_qkv_b = jnp.concatenate([joined_sums[:width], joined_sums[2 * width :]])
    grad_normed_one = jnp.einsum("rc,dc->rd", grad_joined, back_qkv, preferred_element_type=f32)
    grad_input_norm, grad_gain_one, grad_shift_one = norm_one_back(grad_normed_one)
    token_grad = (grad_hidden + grad_input_norm).astype(bf16)
    owner_qkv, owner_dense, owner_up, owner_down = (
        lax.psum_scatter(grad_qkv_w, ("dp", "seq"), scatter_dimension=0, tiled=True),
        lax.psum_scatter(grad_dense_w, ("dp", "seq"), scatter_dimension=0, tiled=True),
        lax.psum_scatter(grad_up_w, ("dp", "seq"), scatter_dimension=0, tiled=True),
        lax.psum_scatter(grad_down_w, ("dp", "seq"), scatter_dimension=0, tiled=True),
    )
    (
        total_gain_one,
        total_shift_one,
        total_qkv_b,
        total_dense_b,
        total_gain_two,
        total_shift_two,
        total_up_b,
        total_down_b,
    ) = lax.psum(
        (
            grad_gain_one,
            grad_shift_one,
            grad_qkv_b,
            grad_dense_b,
            grad_gain_two,
            grad_shift_two,
            grad_up_b,
            grad_down_b,
        ),
        ("dp", "seq"),
    )
    return (
        block_output,
        token_grad,
        total_gain_one,
        total_shift_one,
        owner_qkv,
        total_qkv_b,
        owner_dense,
        total_dense_b,
        total_gain_two,
        total_shift_two,
        owner_up,
        total_up_b,
        owner_down,
        total_down_b,
    )


ALL = ("dp", "seq")


def flat_index(z, y, c, x):
    return ((z * 2 + y) * 2 + c) * 2 + x


TN = (((0,), (0,)), ((), ()))
MIB = 2**20


def owner_of(place_ref, half, zr, near, turn, core, turned):
    z, y, c, x = (place_ref[i] for i in range(4))
    xr, yr = (near, turn) if half == 0 else (turn, near)
    za = (z + 4 - zr) % 4 if turned else zr
    return flat_index(za, y + yr - 2 * y * yr, c + core - 2 * c * core, x + xr - 2 * x * xr)


def start_mixed(place_ref, pieces, w_ref, sem, turned):
    for half, zr, near, turn, core in itertools.product(range(2), range(4), *[range(2)] * 3):
        d = owner_of(place_ref, half, zr, near, turn, core, turned)
        rows = pl.ds(pl.multiple_of(d * 32 + half * 16, 16), 16)
        src = pieces[4 * half + 2 * core + turn].at[near, zr]
        pltpu.make_async_copy(src, w_ref.at[:, rows, :], sem).start()


def of_half(pieces, half):
    return [pieces[5 * core + i] for core in range(2) for i in (0, 1, 2, 3 + half)]


def piece(pieces, half, zr, xr, yr, core):
    ref = pieces[4 * core + xr + 2 * yr]
    return ref.at[zr] if xr and yr else ref.at[zr, half]


def owner(place_ref, zr, xr, yr, core):
    _, y, c, x = (place_ref[i] for i in range(4))
    return flat_index(zr, y + yr - 2 * y * yr, c + core - 2 * c * core, x + xr - 2 * x * xr)


def start_columns(place_ref, pieces, w_ref, sem, half):
    for zr, xr, yr, core in itertools.product(range(4), *[range(2)] * 3):
        d = owner(place_ref, zr, xr, yr, core)
        rows = pl.ds(pl.multiple_of(d * 32, 32), 32)
        src = piece(pieces, half, zr, xr, yr, core)
        pltpu.make_async_copy(src, w_ref.at[:, rows, :], sem).start()


def wait_all(ref, sem):
    pltpu.make_async_copy(ref, ref, sem).wait()


def start_rows(place_ref, pieces, w_ref, sems):
    for zr, half, xr, yr, core in itertools.product(range(4), *[range(2)] * 4):
        d = owner(place_ref, zr, xr, yr, core)
        rows = pl.ds(pl.multiple_of(d * 128 + half * 64, 64), 64)
        src = piece(of_half(pieces, half), half, zr, xr, yr, core).at[0]
        pltpu.make_async_copy(src, w_ref.at[rows, :], sems.at[zr]).start()


def wait_rows(w_ref, sems, z):
    part = w_ref.at[pl.ds(pl.multiple_of(z * 1024, 1024), 1024), :]
    pltpu.make_async_copy(part, part, sems.at[z]).wait()


def dottn(a, b):
    return lax.dot_general(a, b, TN, preferred_element_type=f32)


def spec(shape, index):
    return pl.BlockSpec(shape, index)


def params(mib=56):
    return pltpu.CompilerParams(vmem_limit_bytes=mib * MIB)


HBM = pl.BlockSpec(memory_space=pltpu.HBM)


def qkv_kernel(turned, place_ref, *refs):
    pieces, (a_ref, b_ref, o_ref, all_ref, w_ref, sem, out_sem) = refs[:8], refs[8:]
    step = pl.program_id(0)
    write = pltpu.make_async_copy(w_ref, all_ref, out_sem)

    @pl.when(step == 0)
    def _():
        start_mixed(place_ref, pieces, w_ref, sem, turned)
        wait_all(w_ref, sem)
        write.start()

    o_ref[...] = (dot(a_ref[...], w_ref[step]) + b_ref[...]).astype(bf16)

    @pl.when(step == 2)
    def _():
        write.wait()


def qkv_call(place, pieces, a, b, turned):
    n, d = a.shape
    blocks = pieces[0].shape[2]
    return pl.pallas_call(
        functools.partial(qkv_kernel, turned),
        grid_spec=pltpu.PrefetchScalarGridSpec(
            num_scalar_prefetch=1,
            grid=(3,),
            in_specs=[HBM] * 8
            + [spec((n, d), lambda i, *_: (0, 0)), spec((1, 512), lambda i, *_: (0, i))],
            out_specs=[spec((n, 512), lambda i, *_: (0, i)), HBM],
            scratch_shapes=[
                pltpu.VMEM((blocks, d, 512), bf16),
                pltpu.SemaphoreType.DMA,
                pltpu.SemaphoreType.DMA,
            ],
        ),
        out_shape=[
            jax.ShapeDtypeStruct((n, 1536), bf16),
            jax.ShapeDtypeStruct((blocks, d, 512), bf16),
        ],
        compiler_params=params(63),
        cost_estimate=pl.CostEstimate(
            flops=2 * n * d * 1536, bytes_accessed=2 * (n * d + 8 * d * 512 + 1536 * n), transcendentals=0
        ),
        name="qkv",
    )(place, *pieces, a, b.reshape(1, 1536))


def dense_kernel(c0_ref, c1_ref, w0_ref, w1_ref, x_ref, b_ref, g_ref, s_ref, h_ref, a_ref):
    half = [
        dot(c0_ref[...], w_ref[0, :512, :]) + dot(c1_ref[...], w_ref[0, 512:, :])
        for w_ref in (w0_ref, w1_ref)
    ]
    hidden = x_ref[...].astype(f32) + jnp.concatenate(half, axis=1) + b_ref[...]
    h_ref[...] = hidden
    center = hidden - jnp.mean(hidden, axis=1, keepdims=True)
    rsd = lax.rsqrt(jnp.mean(center * center, axis=1, keepdims=True) + 1e-05)
    a_ref[...] = (center * rsd * g_ref[...] + s_ref[...]).astype(bf16)


def dense_call(c0, c1, w, x, bias, gain, shift):
    n, d = x.shape
    rows = lambda c: spec((256, c), lambda i: (i, 0))
    vector = spec((1, d), lambda i: (0, 0))
    return pl.pallas_call(
        dense_kernel,
        grid=(n // 256,),
        in_specs=[rows(512), rows(512)]
        + [spec((1, d, 512), lambda i, b=b: (b, 0, 0)) for b in (3, 4)]
        + [rows(d), vector, vector, vector],
        out_specs=[rows(d), rows(d)],
        out_shape=[jax.ShapeDtypeStruct((n, d), f32), jax.ShapeDtypeStruct((n, d), bf16)],
        compiler_params=params(40),
        cost_estimate=pl.CostEstimate(flops=2 * n * d * d, bytes_accessed=12 * n * d, transcendentals=0),
        name="dense",
    )(c0, c1, w, w, x, bias.reshape(1, d), gain.reshape(1, d), shift.reshape(1, d))


def dense_back_kernel(g_ref, w0_ref, w1_ref, o_ref):
    o_ref[...] = (
        dotnt(g_ref[:, :512], w0_ref[0]) + dotnt(g_ref[:, 512:], w1_ref[0])
    ).astype(bf16)


def dense_back_call(g, w):
    n, d = g.shape
    rows = spec((256, d), lambda i: (i, 0))
    return pl.pallas_call(
        dense_back_kernel,
        grid=(n // 256,),
        in_specs=[rows] + [spec((1, d, 512), lambda i, b=b: (b, 0, 0)) for b in (3, 4)],
        out_specs=rows,
        out_shape=jax.ShapeDtypeStruct((n, d), bf16),
        compiler_params=params(40),
        cost_estimate=pl.CostEstimate(flops=2 * n * d * d, bytes_accessed=6 * n * d, transcendentals=0),
        name="dense_back",
    )(g, w, w)


def up_kernel(half, place_ref, *refs):
    pieces, (a_ref, b_ref, u_ref, s_ref, w_ref, sem) = refs[:8], refs[8:]
    step = pl.program_id(0)

    @pl.when(step == 0)
    def _():
        start_columns(place_ref, pieces, w_ref, sem, half)
        wait_all(w_ref, sem)

    c = 0.7978845608028654
    w = w_ref[step // 2, :, pl.ds(pl.multiple_of(step % 2 * 512, 512), 512)]
    for r in range(0, a_ref.shape[0], 256):
        v = dot(a_ref[r : r + 256, :], w) + b_ref[...]
        square = v * v
        h = 0.5 + 0.5 * jnp.tanh(v * (c + (c * 0.044715) * square))
        u = v * h
        u_ref[r : r + 256, :] = u.astype(bf16)
        s_ref[r : r + 256, :] = (
            h + u * (1.0 - h) * (2.0 * c + (2.0 * c * 0.134145) * square)
        ).astype(bf16)


def up_call(place, half, pieces, a, b):
    n, d = a.shape
    return pl.pallas_call(
        functools.partial(up_kernel, half),
        grid_spec=pltpu.PrefetchScalarGridSpec(
            num_scalar_prefetch=1,
            grid=(4,),
            in_specs=[HBM] * 8
            + [spec((n, d), lambda i, *_: (0, 0)), spec((1, 512), lambda i, *_: (0, 4 * half + i))],
            out_specs=[spec((n, 512), lambda i, *_: (0, i))] * 2,
            scratch_shapes=[pltpu.VMEM((2, d, 1024), bf16), pltpu.SemaphoreType.DMA],
        ),
        out_shape=[jax.ShapeDtypeStruct((n, 2048), bf16)] * 2,
        compiler_params=params(40),
        cost_estimate=pl.CostEstimate(
            flops=2 * n * d * 2048, bytes_accessed=2 * (n * d + d * 2048 + 4096 * n), transcendentals=n * 2048
        ),
        name="up",
    )(place, *of_half(pieces, half), a, b.reshape(1, 4096))


def divide(acc_ref, keep_ref, give_ref, core):
    keep_ref[...] = acc_ref[:, pl.ds(core, 1)].reshape(keep_ref.shape)
    give_ref[...] = acc_ref[:, pl.ds(1 - core, 1)].reshape(give_ref.shape)


def down_grad_kernel(where_ref, u0_ref, u1_ref, g_ref, keep_ref, give_ref, acc_ref):
    step = pl.program_id(0)
    for half, u_ref in enumerate((u0_ref, u1_ref)):

        @pl.when(step // 4 == half)
        def _(u_ref=u_ref):
            acc_ref[...] = dottn(u_ref[...], g_ref[...]).astype(bf16).reshape(acc_ref.shape)

    divide(acc_ref, keep_ref, give_ref, where_ref[2])


def down_grad_call(where, u, g):
    n, d = g.shape
    out = spec((1, 256, d), lambda i, *_: (i, 0, 0))
    return pl.pallas_call(
        down_grad_kernel,
        grid_spec=pltpu.PrefetchScalarGridSpec(
            num_scalar_prefetch=1,
            grid=(8,),
            in_specs=[
                spec((n, 512), lambda i, *_: (0, jnp.minimum(i, 3))),
                spec((n, 512), lambda i, *_: (0, jnp.maximum(i - 4, 0))),
                spec((n, d), lambda i, *_: (0, 0)),
            ],
            out_specs=[out, out],
            scratch_shapes=[pltpu.VMEM((1, 2, 256, d), bf16)],
        ),
        out_shape=[jax.ShapeDtypeStruct((8, 256, d), bf16)] * 2,
        compiler_params=params(40),
        cost_estimate=pl.CostEstimate(
            flops=2 * n * d * 4096, bytes_accessed=2 * (n * d + d * 4096 + n * 4096), transcendentals=0
        ),
        name="down_grad",
    )(where, *u, g)


def down_kernel(place_ref, *refs):
    pieces, (u0_ref, u1_ref, h_ref, b_ref, o_ref, acc_ref, w_ref, sems) = refs[:10], refs[10:]
    step = pl.program_id(0)

    @pl.when(step == 0)
    def _():
        start_rows(place_ref, pieces, w_ref, sems)

    wait_rows(w_ref, sems, step)
    w = w_ref[pl.ds(pl.multiple_of(step * 1024, 1024), 1024), :]

    @pl.when(step == 0)
    def _():
        acc_ref[...] = dot(u0_ref[...], w)

    @pl.when(step == 1)
    def _():
        acc_ref[...] += dot(u0_ref[...], w)

    @pl.when(step == 2)
    def _():
        acc_ref[...] += dot(u1_ref[...], w)

    @pl.when(step == 3)
    def _():
        for r in range(0, u1_ref.shape[0], 256):
            rows = slice(r, r + 256)
            part = acc_ref[rows, :] + dot(u1_ref[rows, :], w)
            o_ref[rows, :] = (h_ref[rows, :] + part + b_ref[...]).astype(bf16)


def down_call(place, pieces, u, hidden, bias):
    n, d = hidden.shape
    whole = lambda s: spec(s, lambda i, *_: (0, 0))
    return pl.pallas_call(
        down_kernel,
        grid_spec=pltpu.PrefetchScalarGridSpec(
            num_scalar_prefetch=1,
            grid=(4,),
            in_specs=[HBM] * 10
            + [
                spec((n, 1024), lambda i, *_: (0, jnp.minimum(i, 1))),
                spec((n, 1024), lambda i, *_: (0, jnp.maximum(i - 2, 0))),
                whole((n, d)),
                whole((1, d)),
            ],
            out_specs=whole((n, d)),
            scratch_shapes=[
                pltpu.VMEM((n, d), f32),
                pltpu.VMEM((4096, d), bf16),
                pltpu.SemaphoreType.DMA((4,)),
            ],
        ),
        out_shape=jax.ShapeDtypeStruct((n, d), bf16),
        compiler_params=params(),
        cost_estimate=pl.CostEstimate(
            flops=2 * n * d * 4096, bytes_accessed=2 * (3 * n * d + d * 4096 + n * 4096), transcendentals=0
        ),
        name="down",
    )(place, *pieces, *u, hidden, bias.reshape(1, d))


def gate_kernel(place_ref, *refs):
    pieces, (g_ref, s0_ref, s1_ref, z_ref, b_ref, w_ref, sems) = refs[:10], refs[10:]
    step = pl.program_id(0)

    @pl.when(step == 0)
    def _():
        start_rows(place_ref, pieces, w_ref, sems)

    wait_rows(w_ref, sems, step)
    w = w_ref[pl.ds(pl.multiple_of(step * 1024, 1024), 1024), :]
    total = None
    for r in range(0, g_ref.shape[0], 256):
        rows = slice(r, r + 256)
        slope = jnp.where(step < 2, s0_ref[rows, :], s1_ref[rows, :])
        v = (dotnt(g_ref[rows, :], w) * slope.astype(f32)).astype(bf16)
        z_ref[rows, :] = v
        part = jnp.sum(v.astype(f32).reshape(32, 8, v.shape[1]), axis=0)
        total = part if total is None else total + part
    b_ref[...] = jnp.sum(total, axis=0, keepdims=True)


def gate_call(place, pieces, g, slopes):
    n, d = g.shape
    return pl.pallas_call(
        gate_kernel,
        grid_spec=pltpu.PrefetchScalarGridSpec(
            num_scalar_prefetch=1,
            grid=(4,),
            in_specs=[HBM] * 10
            + [
                spec((n, d), lambda i, *_: (0, 0)),
                spec((n, 1024), lambda i, *_: (0, jnp.minimum(i, 1))),
                spec((n, 1024), lambda i, *_: (0, jnp.maximum(i - 2, 0))),
            ],
            out_specs=[
                spec((n, 1024), lambda i, *_: (0, i)),
                spec((1, 1024), lambda i, *_: (0, i)),
            ],
            scratch_shapes=[pltpu.VMEM((4096, d), bf16), pltpu.SemaphoreType.DMA((4,))],
        ),
        out_shape=[jax.ShapeDtypeStruct((n, 4096), bf16), jax.ShapeDtypeStruct((1, 4096), f32)],
        compiler_params=params(),
        cost_estimate=pl.CostEstimate(
            flops=2 * n * d * 4096, bytes_accessed=2 * (n * d + d * 4096 + 8192 * n), transcendentals=0
        ),
        name="gate",
    )(place, *pieces, g, *slopes)


def norm_back(x_ref, gain_ref, res_ref, acc_ref, out_refs, sums_ref):
    n, d = x_ref.shape

    def chunk(i, sums):
        rows = pl.ds(pl.multiple_of(i * 128, 128), 128)
        grad = acc_ref[rows, :]
        x = x_ref[rows, :].astype(f32)
        center = x - jnp.mean(x, axis=1, keepdims=True)
        rsd = lax.rsqrt(jnp.mean(center * center, axis=1, keepdims=True) + 1e-05)
        hat = center * rsd
        e = grad * gain_ref[...]
        back = rsd * (
            e - jnp.mean(e, axis=1, keepdims=True) - hat * jnp.mean(e * hat, axis=1, keepdims=True)
        )
        result = res_ref[rows, :].astype(f32) + back
        low = result.astype(bf16)
        out_refs[0][rows, :] = low
        if len(out_refs) > 1:
            out_refs[1][rows, :] = result
        fold = lambda v: jnp.sum(v.reshape(16, 8, d), axis=0)
        return sums[0] + fold(grad * hat), sums[1] + fold(grad), sums[2] + fold(low.astype(f32))

    zero = jnp.zeros((8, d), f32)
    sums = lax.fori_loop(0, n // 128, chunk, (zero, zero, zero))
    for k in range(3):
        sums_ref[k : k + 1, :] = jnp.sum(sums[k], axis=0, keepdims=True)


def norm_up_kernel(place_ref, *refs):
    pieces, (g_ref, x_ref, gain_ref, res_ref, low_ref, wide_ref, sums_ref, acc_ref, w_ref, sems) = (
        refs[:10],
        refs[10:],
    )
    step = pl.program_id(0)

    @pl.when(step == 0)
    def _():
        for half in range(2):
            part = w_ref.at[2 * half : 2 * half + 2]
            start_columns(place_ref, of_half(pieces, half), part, sems.at[half], half)

    for half in range(2):

        @pl.when(step == 2 * half)
        def _():
            wait_all(w_ref.at[2 * half : 2 * half + 2], sems.at[half])

    @pl.when(step == 0)
    def _():
        acc_ref[...] = dotnt(g_ref[...], w_ref[0])

    @pl.when(step > 0)
    def _():
        acc_ref[...] += dotnt(g_ref[...], w_ref[step])

    @pl.when(step == 3)
    def _():
        norm_back(x_ref, gain_ref, res_ref, acc_ref, (low_ref, wide_ref), sums_ref)


def norm_up_call(place, pieces, g, x, gain, residual):
    n, d = x.shape
    ff = g.shape[1]
    whole = lambda s: spec(s, lambda i, *_: (0, 0))
    return pl.pallas_call(
        norm_up_kernel,
        grid_spec=pltpu.PrefetchScalarGridSpec(
            num_scalar_prefetch=1,
            grid=(4,),
            in_specs=[HBM] * 10
            + [spec((n, 1024), lambda i, *_: (0, i)), whole((n, d)), whole((1, d)), whole((n, d))],
            out_specs=[whole((n, d)), whole((n, d)), whole((8, d))],
            scratch_shapes=[
                pltpu.VMEM((n, d), f32),
                pltpu.VMEM((4, d, 1024), bf16),
                pltpu.SemaphoreType.DMA((2,)),
            ],
        ),
        out_shape=[
            jax.ShapeDtypeStruct((n, d), bf16),
            jax.ShapeDtypeStruct((n, d), f32),
            jax.ShapeDtypeStruct((8, d), f32),
        ],
        compiler_params=params(),
        cost_estimate=pl.CostEstimate(
            flops=2 * n * d * ff, bytes_accessed=2 * (8 * n * d + 2 * d * ff), transcendentals=0
        ),
        name="norm_up",
    )(place, *pieces, g, x, gain.reshape(1, d), residual)


def norm_qkv_kernel(*refs):
    g_refs = refs[:6]
    w0_ref, w1_ref, x_ref, gain_ref, res_ref, low_ref, sums_ref, acc_ref = refs[6:]
    step = pl.program_id(0)
    for i in range(3):

        @pl.when(step == i)
        def _(i=i):
            part = dotnt(g_refs[i][...], w0_ref[0]) + dotnt(g_refs[3 + i][...], w1_ref[0])
            acc_ref[...] = part if i == 0 else acc_ref[...] + part

    @pl.when(step == 2)
    def _():
        norm_back(x_ref, gain_ref, res_ref, acc_ref, (low_ref,), sums_ref)


def norm_qkv_call(grads, w0, w1, x, gain, residual):
    n, d = x.shape
    whole = lambda s: spec(s, lambda i: (0, 0))
    return pl.pallas_call(
        norm_qkv_kernel,
        grid=(3,),
        in_specs=[whole((n, 512))] * 6
        + [spec((1, d, 512), lambda i: (i, 0, 0))] * 2
        + [whole((n, d)), whole((1, d)), whole((n, d))],
        out_specs=[whole((n, d)), whole((8, d))],
        out_shape=[jax.ShapeDtypeStruct((n, d), bf16), jax.ShapeDtypeStruct((8, d), f32)],
        scratch_shapes=[pltpu.VMEM((n, d), f32)],
        compiler_params=params(),
        cost_estimate=pl.CostEstimate(
            flops=2 * n * d * 3072, bytes_accessed=2 * (8 * n * d + d * 3072), transcendentals=0
        ),
        name="norm_qkv",
    )(*grads, w0, w1, x, gain.reshape(1, d), residual)


def columns_kernel(plan, parts, where_ref, *refs):
    count = sum(parts)
    left_refs, right_refs = refs[:count], refs[count : count + len(plan)]
    keep_ref, give_ref, sums_ref, at_ref, acc_ref = refs[-5:]
    step = pl.program_id(0)
    for i, left in enumerate(plan):

        @pl.when(step == i)
        def _(i=i, left=left):
            if i == 0 or plan[i - 1] != left:
                begin = sum(parts[:left])
                row = 0
                for ref in left_refs[begin : begin + parts[left]]:
                    at_ref[row : row + ref.shape[1], :] = ref[...].T
                    row += ref.shape[1]
            right = right_refs[i][...]
            acc = dot(at_ref[...], right)
            acc_ref[...] = acc.astype(bf16).reshape(acc_ref.shape)
            total = jnp.sum(right.astype(f32).reshape(-1, 8, right.shape[1]), axis=0)
            sums_ref[...] = jnp.sum(total, axis=0, keepdims=True)

    divide(acc_ref, keep_ref, give_ref, where_ref[2])


def columns_call(where, lefts, rights, plan, name):
    flat = [a for left in lefts for a in left]
    n = flat[0].shape[0]
    d = sum(a.shape[1] for a in lefts[0])
    wide = 512 * len(rights)
    out = spec((8, 64, 512), lambda i, *_: (0, 0, i))
    return pl.pallas_call(
        functools.partial(columns_kernel, plan, [len(left) for left in lefts]),
        grid_spec=pltpu.PrefetchScalarGridSpec(
            num_scalar_prefetch=1,
            grid=(len(plan),),
            in_specs=[spec(a.shape, lambda i, *_: (0, 0)) for a in flat]
            + [spec((n, 512), lambda i, *_, b=b: (0, b)) for _, b in rights],
            out_specs=[out, out, spec((1, 512), lambda i, *_: (0, i))],
            scratch_shapes=[pltpu.VMEM((d, n), bf16), pltpu.VMEM((8, 2, 64, 512), bf16)],
        ),
        out_shape=[jax.ShapeDtypeStruct((8, 64, wide), bf16)] * 2
        + [jax.ShapeDtypeStruct((1, wide), f32)],
        compiler_params=params(40),
        cost_estimate=pl.CostEstimate(
            flops=2 * n * d * wide, bytes_accessed=2 * (2 * n * d + d * wide + n * wide), transcendentals=0
        ),
        name=name,
    )(where, *flat, *[r for r, _ in rights])


def up_grad_kernel(where_ref, a_ref, g_ref, keep_ref, give_ref, at_ref, acc_ref):
    @pl.when(pl.program_id(0) == 0)
    def _():
        at_ref[...] = a_ref[...].T

    acc_ref[...] = dot(at_ref[...], g_ref[...]).astype(bf16).reshape(acc_ref.shape)
    divide(acc_ref, keep_ref, give_ref, where_ref[2])


def up_grad_call(where, a, g):
    n, d = a.shape
    ff = g.shape[1]
    out = spec((8, 64, 512), lambda i, *_: (0, 0, i))
    return pl.pallas_call(
        up_grad_kernel,
        grid_spec=pltpu.PrefetchScalarGridSpec(
            num_scalar_prefetch=1,
            grid=(ff // 512,),
            in_specs=[spec((n, d), lambda i, *_: (0, 0)), spec((n, 512), lambda i, *_: (0, i))],
            out_specs=[out, out],
            scratch_shapes=[pltpu.VMEM((d, n), bf16), pltpu.VMEM((8, 2, 64, 512), bf16)],
        ),
        out_shape=[jax.ShapeDtypeStruct((8, 64, ff), bf16)] * 2,
        compiler_params=params(40),
        cost_estimate=pl.CostEstimate(
            flops=2 * n * d * ff, bytes_accessed=2 * (n * d + d * ff + n * ff), transcendentals=0
        ),
        name="up_grad",
    )(where, a, g)


def permutation(move):
    pairs = []
    for z in range(4):
        for y in range(2):
            for c in range(2):
                for x in range(2):
                    pairs.append((flat_index(z, y, c, x), flat_index(*move(z, y, c, x))))
    return pairs


OVER_X = permutation(lambda z, y, c, x: (z, y, c, 1 - x))
OVER_Y = permutation(lambda z, y, c, x: (z, 1 - y, c, x))
OVER_C = permutation(lambda z, y, c, x: (z, y, 1 - c, x))
OVER_CX = permutation(lambda z, y, c, x: (z, y, 1 - c, 1 - x))
OVER_Z = [permutation(lambda z, y, c, x, k=k: ((z + k) % 4, y, c, x)) for k in range(4)]


Z_GROUPS = [
    [flat_index(z, y, c, x) for z in range(4)] for y in range(2) for c in range(2) for x in range(2)
]


def send(array, pairs):
    return lax.ppermute(array, ALL, pairs)


def plain(array):
    return with_layout_constraint(array, Layout(major_to_minor=tuple(range(array.ndim))))


def tie(*trees):
    return lax.optimization_barrier(trees)


def gather_z(shard):
    return [shard] + [send(shard, OVER_Z[k]) for k in (1, 2, 3)]


def halves(parts):
    return jnp.stack([p[0] for p in parts]), jnp.stack([p[1] for p in parts])


def gather_z_line(shard):
    return plain(lax.all_gather(shard, ALL, axis=0, tiled=False, axis_index_groups=Z_GROUPS))


def scatter_z_line(array):
    return lax.psum_scatter(array, ALL, scatter_dimension=0, tiled=False, axis_index_groups=Z_GROUPS)


def add_low(a, b):
    return (a.astype(f32) + b.astype(f32)).astype(bf16)


def take(array, at, axis):
    return lax.dynamic_index_in_dim(array, at, axis, keepdims=False)


def fold(g, at, axis, pairs):
    return take(g, at, axis), send(take(g, 1 - at, axis), pairs)


def fold_second(a, b, place):
    return fold(a, place[3], 2, OVER_X), fold(b, place[1], 1, OVER_Y)


def fold_third(pair, place):
    a, b = (add_low(*p) for p in pair)
    return fold(a, place[1], 1, OVER_Y), fold(b, place[3], 1, OVER_X)


def both(pair):
    return jnp.stack([add_low(*p) for p in pair], axis=1)


def fold_z(pair, place):
    z = place[0]
    g = both(pair)
    return [take(g, z, 0)] + [send(take(g, (z + k) % 4, 0), OVER_Z[k]) for k in (1, 2, 3)]


def total(parts):
    return sum(p.astype(f32) for p in parts)


def slope_table():
    slopes = np.exp2(-8.0 * (np.arange(H) + 1.0) / H).astype(np.float32)
    pieces, rest = [], slopes
    for _ in range(3):
        low = rest.astype(ml_dtypes.bfloat16).astype(np.float32)
        pieces.append(low)
        rest = rest - low
    return slopes, np.stack(pieces, axis=1).reshape(-1)


def moments(v):
    mean = jnp.mean(v, axis=-1, keepdims=True)
    center = v - mean
    return center, lax.rsqrt(jnp.mean(center * center, axis=-1, keepdims=True) + 1e-05)


def fast_shards(
    tokens,
    ln1_gain,
    ln1_bias,
    qkv_weight,
    qkv_bias,
    dense_weight,
    dense_bias,
    ln2_gain,
    ln2_bias,
    up_weight,
    up_bias,
    down_weight,
    down_bias,
    cotangent,
    seq_lengths,
    slot_order,
):
    rows, width = tokens.shape
    dp, seq = lax.axis_index("dp"), lax.axis_index("seq")
    place = (dp // 4, (dp // 2) % 2, dp % 2, seq)
    place_vec = jnp.stack([p.astype(jnp.int32) for p in place])

    def mixed(*blocks):
        stacked = jnp.stack(blocks).reshape(len(blocks), 2, 16, 512)
        return stacked.transpose(1, 0, 2, 3)

    w_in = [qkv_weight[:, 512 * i : 512 * i + 512] for i in range(6)]
    one = mixed(*w_in[0::2], *w_in[1::2], dense_weight[:, :512], dense_weight[:, 512:])
    two = up_weight.reshape(32, 4, 1024).transpose(1, 0, 2).reshape(2, 2, 32, 1024)
    three = down_weight.reshape(2, 1, 64, 1024)

    slot = dp * SG + seq
    my_seq = lax.dynamic_index_in_dim(slot_order, slot, 0, keepdims=False)
    every_seq = jnp.arange(seq_lengths.shape[0], dtype=jnp.int32)
    length = jnp.sum(jnp.where(every_seq == my_seq, seq_lengths, 0))
    valid = (jnp.arange(rows, dtype=jnp.int32) < length).astype(f32)
    slopes, slopes_split = slope_table()
    no_bias = jnp.zeros((512,), f32)
    bias0 = jnp.concatenate([qkv_bias[:512], no_bias, qkv_bias[1024:1536]])
    bias1 = jnp.concatenate([qkv_bias[512:1024], no_bias, qkv_bias[1536:]])

    one_z = gather_z(one)
    one_z, two, tokens, cotangent = tie(one_z, two, tokens, cotangent)

    a, b = halves([p[:, :3] for p in one_z])
    one_x, one_y = send(a, OVER_X), send(b, OVER_Y)
    two_z = gather_z_line(two)
    also_za, also_zb = halves([p[:, 3:] for p in one_z])
    one_x, one_y, also_za, also_zb, tokens, cotangent = tie(
        one_x, one_y, also_za, also_zb, tokens, cotangent
    )

    one_a, one_b = jnp.stack([a, one_x]), jnp.stack([b, one_y])
    one_xy, one_yx = send(one_a, OVER_Y), send(one_b, OVER_X)
    one_ca, one_cb = send(one_a, OVER_C), send(one_b, OVER_C)
    center, rsd = moments(tokens.astype(f32))
    a1 = (center * rsd * ln1_gain + ln1_bias).astype(bf16)
    grad_low = cotangent * valid[:, None].astype(bf16)
    one_xy, one_yx, one_ca, one_cb, a1, grad_low = tie(
        one_xy, one_yx, one_ca, one_cb, a1, grad_low
    )
    one_cxy, one_cyx = send(one_xy, OVER_C), send(one_yx, OVER_C)
    a, b = also_za, also_zb
    one_cxy, one_cyx, a, b, three = tie(one_cxy, one_cyx, a, b, three)

    also_x, also_y = send(a, OVER_X), send(b, OVER_Y)
    pieces = (one_a, one_xy, one_ca, one_cxy, one_b, one_yx, one_cb, one_cyx)
    qkv0, w0 = qkv_call(place_vec, pieces, a1, bias0, True)
    qkv0, also_x, also_y, two_z = tie(qkv0, also_x, also_y, two_z)
    also_a, also_b = jnp.stack([a, also_x]), jnp.stack([b, also_y])
    also_xy, also_yx = send(also_a, OVER_Y), send(also_b, OVER_X)
    also_ca, also_cb = send(also_a, OVER_C), send(also_b, OVER_C)
    three_z = gather_z_line(three)
    context0, lse0 = attn_fwd(length, jnp.asarray(slopes), qkv0, 0)
    context0, also_xy, also_yx, also_ca, also_cb, a1 = tie(
        context0, also_xy, also_yx, also_ca, also_cb, a1
    )

    also_cxy, also_cyx = send(also_xy, OVER_C), send(also_yx, OVER_C)
    also_cxy, also_cyx = tie(also_cxy, also_cyx)
    pieces = (also_a, also_xy, also_ca, also_cxy, also_b, also_yx, also_cb, also_cyx)
    two_c = send(two_z, OVER_C)
    two_x, two_y = plain(send(two_z, OVER_X)), plain(send(two_z, OVER_Y))
    qkv1, w1 = qkv_call(place_vec, pieces, a1, bias1, True)
    qkv1, two_c, three_z = tie(qkv1, two_c, three_z)
    context1, lse1 = attn_fwd(length, jnp.asarray(slopes), qkv1, 4)
    context0, context1, two_x, two_y, three_z = tie(context0, context1, two_x, two_y, three_z)

    two_xy, two_yx = send(two_x[:, 0], OVER_Y), send(two_y[:, 1], OVER_X)
    two_cx, two_cy = send(two_x, OVER_C), send(two_y, OVER_C)
    hidden, a2 = dense_call(context0, context1, w1, tokens, dense_bias, ln2_gain, ln2_bias)
    a2, two_xy, two_yx, two_cx, two_cy, three_z = tie(a2, two_xy, two_yx, two_cx, two_cy, three_z)
    two_cxy, two_cyx = send(two_xy, OVER_C), send(two_yx, OVER_C)
    two_cxy, a2, three_z = tie(two_cxy, a2, three_z)

    three_c = send(three_z, OVER_C)
    three_x, three_y = plain(send(three_z, OVER_X)), plain(send(three_z, OVER_Y))
    up_pieces = (two_z, two_x, two_y, two_xy, two_yx, two_c, two_cx, two_cy, two_cxy, two_cyx)
    u0, slope0 = up_call(place_vec, 0, up_pieces, a2, up_bias)
    u0, a2, two_cyx, three_c = tie(u0, a2, two_cyx, three_c)
    up_pieces = (two_z, two_x, two_y, two_xy, two_yx, two_c, two_cx, two_cy, two_cxy, two_cyx)
    u1, slope1 = up_call(place_vec, 1, up_pieces, a2, up_bias)
    u0, u1, grad_low, three_x, three_y = tie(u0, u1, grad_low, three_x, three_y)
    three_xy, three_yx = send(three_x[:, 0], OVER_Y), send(three_y[:, 1], OVER_X)
    three_cx, three_cy = send(three_x, OVER_C), send(three_y, OVER_C)

    down_keep, down_give = down_grad_call(place_vec, (u0, u1), grad_low)
    down_keep, down_give, grad_low, three_cx, three_cy, three_xy, three_yx = tie(
        down_keep, down_give, grad_low, three_cx, three_cy, three_xy, three_yx
    )
    three_cxy, three_cyx = send(three_xy, OVER_C), send(three_yx, OVER_C)
    down_b = jnp.sum(grad_low.astype(f32), axis=0)
    down_give, three_cxy, three_cyx, down_b, grad_low = tie(
        down_give, three_cxy, three_cyx, down_b, grad_low
    )

    pieces = (
        three_z, three_x, three_y, three_xy, three_yx,
        three_c, three_cx, three_cy, three_cxy, three_cyx,
    )
    down_got = send(down_give, OVER_C)
    grad_before, up_bias_grad = gate_call(place_vec, pieces, grad_low, (slope0, slope1))
    grad_before, a2, down_got = tie(grad_before, a2, down_got)
    down = add_low(down_keep, down_got).reshape(4, 2, 2, 2, 64, 1024)
    down = fold_second(down[:, :, :, 0], down[:, :, :, 1], place)
    up_keep, up_give = up_grad_call(place_vec, a2, grad_before)
    grad_before, up_keep, up_give = tie(grad_before, up_keep, up_give)

    up_got = send(up_give, OVER_C)
    grad_low_hidden, grad_hidden, sums = norm_up_call(
        place_vec, up_pieces, grad_before, hidden, ln2_gain, grad_low
    )
    grad_low_hidden, grad_hidden, sums, down, up_got = tie(
        grad_low_hidden, grad_hidden, sums, down, up_got
    )

    down = fold_third(down, place)
    up = add_low(up_keep, up_got).reshape(4, 2, 2, 32, 4096)
    up = fold_second(up[..., :2048], up[..., 2048:], place)
    early = jnp.concatenate(
        [sums[2], sums[0], sums[1], up_bias_grad.reshape(4096), down_b]
    ).reshape(8, 1024)
    grad_context = dense_back_call(grad_low_hidden, w1)
    q0, k0, v0 = attn_bwd(
        length, jnp.asarray(slopes_split), qkv0, context0, lse0, grad_context, 0
    )
    q0, k0, v0, down, up, a1, early = tie(q0, k0, v0, down, up, a1, early)

    owner_down = scatter_z_line(both(down))
    up = fold_third(up, place)
    third_keep, third_give, sums0 = columns_call(
        place_vec,
        [(context0, context1), (a1,)],
        [(grad_low_hidden, 0), (grad_low_hidden, 1), (q0, 0), (k0, 0), (v0, 0)],
        (0, 0, 1, 1, 1),
        "dense_grad",
    )
    third_keep, third_give, qkv1, up = tie(third_keep, third_give, qkv1, up)
    third_got = send(third_give, OVER_C)
    up = both(up)
    third_got, up, qkv1 = tie(third_got, up, qkv1)

    owner_up = scatter_z_line(up)
    third = add_low(third_keep, third_got).reshape(4, 2, 2, 32, 2560)
    third = fold_second(third[..., :1280], third[..., 1280:], place)
    q1, k1, v1 = attn_bwd(
        length, jnp.asarray(slopes_split), qkv1, context1, lse1, grad_context, 4
    )
    q1, k1, v1, third = tie(q1, k1, v1, third)

    third = fold_third(third, place)
    last_keep, last_give, sums1 = columns_call(
        place_vec, [(a1,)], [(q1, 0), (k1, 0), (v1, 0)], (0, 0, 0), "heads_grad"
    )
    last_keep, last_give, third, q0 = tie(last_keep, last_give, third, q0)
    last_got = send(last_give, OVER_C)
    third = both(third)
    last_got, third, q0, tokens = tie(last_got, third, q0, tokens)

    last = add_low(last_keep, last_got).reshape(4, 2, 2, 32, 1536)
    last = fold_second(last[..., :768], last[..., 768:], place)
    third = scatter_z_line(third)
    token_grad, sums = norm_qkv_call(
        [q0, k0, v0, q1, k1, v1], w0, w1, tokens, ln1_gain, grad_hidden
    )
    token_grad, sums, last, u0 = tie(token_grad, sums, last, u0)

    last = fold_third(last, place)
    vectors = [sums0[0, 1024:1536], sums1[0, :512], sums0[0, 2048:], sums1[0, 1024:]]
    late = jnp.concatenate(vectors + [sums[0], sums[1]]).reshape(4, 1024)
    late = jnp.concatenate([late, early])
    late_near = [send(late, pairs) for pairs in (OVER_C, OVER_X, OVER_CX)]
    block_output = down_call(place_vec, pieces, (u0, u1), hidden, down_bias)
    block_output, last, late, late_near = tie(block_output, last, late, late_near)

    late = late + sum(late_near)
    late_y = send(late, OVER_Y)
    last = fold_z(last, place)
    late, late_y, owner_up, owner_down, third = tie(late, late_y, owner_up, owner_down, third)
    late = late + late_y
    late_z = [send(late, OVER_Z[k]) for k in (1, 2, 3)]
    third = third.astype(f32)
    third = jnp.concatenate([third[0], third[1]], axis=1)
    owner_down = owner_down.astype(f32).reshape(128, 1024)
    owner_up = owner_up.astype(f32)
    owner_up = jnp.concatenate([owner_up[0], owner_up[1]], axis=1)
    late, late_z, last, owner_up, owner_down, third = tie(
        late, late_z, last, owner_up, owner_down, third
    )
    last = total(last)
    last = jnp.concatenate([last[0], last[1]], axis=1)
    late = late + sum(late_z)
    early = late[4:]
    owner_qkv = jnp.concatenate(
        [
            part
            for i in range(3)
            for part in (third[:, 1024 + 512 * i : 1536 + 512 * i], last[:, 512 * i : 512 * i + 512])
        ],
        axis=1,
    )
    return (
        block_output,
        token_grad,
        late[2],
        late[3],
        owner_qkv,
        late[:2].reshape(2 * width),
        third[:, :1024],
        early[0],
        early[1],
        early[2],
        owner_up,
        early[3:7].reshape(4 * width),
        owner_down,
        early[7],
    )


def solution(mesh):
    in_specs = (
        P(("dp", "seq"), None),
        P(),
        P(),
        P(("dp", "seq"), None),
        P(),
        P(("dp", "seq"), None),
        P(),
        P(),
        P(),
        P(("dp", "seq"), None),
        P(),
        P(("dp", "seq"), None),
        P(),
        P(("dp", "seq"), None),
        P(),
        P(),
    )
    out_specs = (
        P(("dp", "seq"), None),
        P(("dp", "seq"), None),
        P(),
        P(),
        P(("dp", "seq"), None),
        P(),
        P(("dp", "seq"), None),
        P(),
        P(),
        P(),
        P(("dp", "seq"), None),
        P(),
        P(("dp", "seq"), None),
        P(),
    )
    body = fast_shards if mesh.shape["dp"] == 16 and mesh.shape["seq"] == 2 else generic_shards
    return jax.shard_map(body, mesh=mesh, in_specs=in_specs, out_specs=out_specs, check_vma=False)
```

```python
import functools
import itertools

import jax
import jax.numpy as jnp
import ml_dtypes
import numpy as np
from jax import lax
from jax.experimental import pallas as pl
from jax.experimental.layout import Layout, with_layout_constraint
from jax.experimental.pallas import tpu as pltpu
from jax.sharding import PartitionSpec as P

H = 16
SEQLEN = 1024
SG = 2
BQ = 256
f32 = jnp.float32
bf16 = jnp.bfloat16
NT = (((1,), (1,)), ((), ()))


def dot(a, b):
    return jnp.dot(a, b, preferred_element_type=f32)


def dotnt(a, b):
    return lax.dot_general(a, b, NT, preferred_element_type=f32)


LOG2E=1.4426950408889634

def attn_fwd_kernel(len_ref, slope_ref, q_ref, k_ref, v_ref, o_ref, lse_ref):
    pair=pl.program_id(0)+len_ref[1]
    n=q_ref.shape[0]
    length=len_ref[0]
    lane=lax.broadcasted_iota(jnp.int32,(1,128),1)
    first=lane<64
    place=lax.broadcasted_iota(jnp.int32,(n,128),0)
    hi=(place//8*8).astype(f32); lo=(place%8).astype(f32)
    kf=jnp.where(lane<6,jnp.where(lane%2==0,hi,lo),jnp.where(lane==6,jnp.where(place<length,0.0,-1e30),0.0)).astype(bf16)
    kaug=jnp.concatenate([k_ref[...],kf],axis=1)
    vaug=jnp.concatenate([v_ref[...],jnp.ones((n,128),bf16)],axis=1)
    diag=lax.broadcasted_iota(jnp.int32,(BQ,BQ),1)<=lax.broadcasted_iota(jnp.int32,(BQ,BQ),0)
    feats=[]
    for h in range(2):
        j=3*(2*pair+h)
        mf=jnp.where(lane<2,slope_ref[j],jnp.where(lane<4,slope_ref[j+1],jnp.where(lane<6,slope_ref[j+2],jnp.where(lane==6,1.0,0.0)))).astype(bf16)
        feats.append(jnp.broadcast_to(mf,(BQ,128)))
    for i in range(n//BQ):
        nk=(i+1)*BQ
        q=q_ref[i*BQ:(i+1)*BQ,:]*jnp.array(0.125,bf16)
        outs=[];lses=[]
        for h in range(2):
            qa=jnp.concatenate([jnp.where(first if h==0 else ~first, q, jnp.zeros_like(q)),feats[h]],axis=1)
            s=dotnt(qa,kaug[:nk])
            sd=jnp.where(diag,s[:,nk-BQ:],-1e30)
            s=sd if i==0 else jnp.concatenate([s[:,:nk-BQ],sd],axis=1)
            m=jnp.max(s,axis=1,keepdims=True)*LOG2E
            p=jnp.exp2(s*LOG2E-m).astype(bf16)
            o=dot(p,vaug[:nk])
            tot=o[:,128:]
            outs.append(o[:,:128]/tot)
            lses.append((m+jnp.log2(tot))*(1.0/LOG2E))
        o_ref[i*BQ:(i+1)*BQ,:]=jnp.where(first,outs[0],outs[1]).astype(bf16)
        lse_ref[i*BQ:(i+1)*BQ,:]=jnp.where(first,lses[0],lses[1])

def attn_fwd(length,slopes,qkv,start):
    n=qkv.shape[0]; D=qkv.shape[1]//3; np_=D//128
    length=jnp.stack([length,jnp.int32(start)])
    spec=lambda off: pl.BlockSpec((n,128),lambda p,*_: (0,p+off))
    return pl.pallas_call(attn_fwd_kernel,
        grid_spec=pltpu.PrefetchScalarGridSpec(num_scalar_prefetch=2,grid=(np_,),
            in_specs=[spec(0),spec(np_),spec(2*np_)],out_specs=[spec(0),spec(0)]),
        out_shape=[jax.ShapeDtypeStruct((n,D),bf16),jax.ShapeDtypeStruct((n,D),f32)],
        compiler_params=pltpu.CompilerParams(vmem_limit_bytes=63*2**20),
        cost_estimate=pl.CostEstimate(flops=int(2*2*n*n*D*2.5),bytes_accessed=n*D*12,transcendentals=n*n*10),
        name="attn_fwd")(length,slopes,qkv,qkv,qkv)

def split3(x):
    a=x.astype(bf16); r=x-a.astype(f32); b=r.astype(bf16); c=(r-b.astype(f32)).astype(bf16)
    return a,b,c

def attn_bwd_kernel(len_ref, slope_ref, q_ref, k_ref, v_ref, o_ref, lse_ref, do_ref, dq_ref, dk_ref, dv_ref, qa_ref, doa_ref, dqt_ref):
    pair=pl.program_id(0)+len_ref[1]
    n=q_ref.shape[0]
    nb=n//BQ
    length=len_ref[0]
    lane=lax.broadcasted_iota(jnp.int32,(1,128),1)
    sub=lane%64
    first=lane<64
    place=lax.broadcasted_iota(jnp.int32,(n,128),0)
    hi=(place//8*8).astype(f32); lo=(place%8).astype(f32)
    kf=jnp.where(sub<3,-1.0,jnp.where(sub<9,jnp.where(sub%2==1,hi,lo),jnp.where(sub==9,jnp.where(place<length,0.0,-1e30),0.0))).astype(bf16)
    vf=jnp.where(sub<3,-1.0,0.0).astype(bf16)
    k=k_ref[...]; v=v_ref[...]
    kaug=jnp.concatenate([k,kf],axis=1)
    vaug=jnp.concatenate([v,jnp.broadcast_to(vf,(n,128))],axis=1)
    q=q_ref[...]*jnp.array(0.125,bf16)
    do=do_ref[...]
    prod=do.astype(f32)*o_ref[...].astype(f32)
    same=(lax.broadcasted_iota(jnp.int32,(128,128),0)//64==lax.broadcasted_iota(jnp.int32,(128,128),1)//64).astype(bf16)
    p1,p2,p3=split3(prod)
    dd=dot(p1,same)+dot(p2,same)+dot(p3,same)
    d1,d2,d3=split3(dd)
    l1,l2,l3=split3(lse_ref[...])
    zero=jnp.zeros((n,128),bf16)
    for h in range(2):
        mine=first if h==0 else ~first
        m1=slope_ref[3*(2*pair+h)];m2=slope_ref[3*(2*pair+h)+1];m3=slope_ref[3*(2*pair+h)+2]
        mf=jnp.where(sub<5,m1,jnp.where(sub<7,m2,jnp.where(sub<9,m3,jnp.where(sub==9,1.0,0.0)))).astype(bf16)
        qf=jnp.where(sub==0,l1,jnp.where(sub==1,l2,jnp.where(sub==2,l3,jnp.broadcast_to(mf,(n,128)))))
        df=jnp.where(sub==0,d1,jnp.where(sub==1,d2,jnp.where(sub==2,d3,zero)))
        qa_ref[h]=jnp.concatenate([jnp.where(mine,q,zero),jnp.where(mine,qf,zero)],axis=1)
        doa_ref[h]=jnp.concatenate([jnp.where(mine,do,zero),jnp.where(mine,df,zero)],axis=1)
    kt=k.T
    diag=lax.broadcasted_iota(jnp.int32,(BQ,BQ),0)<=lax.broadcasted_iota(jnp.int32,(BQ,BQ),1)
    for j in range(nb):
        ks=slice(j*BQ,(j+1)*BQ); qs=slice(j*BQ,n)
        dvs=[];dks=[]
        for h in range(2):
            sT=dotnt(kaug[ks],qa_ref[h,qs,:])
            dpT=dotnt(vaug[ks],doa_ref[h,qs,:])
            p=jnp.exp(sT)
            pd=jnp.where(diag,p[:,:BQ],0.0)
            p=pd if j==nb-1 else jnp.concatenate([pd,p[:,BQ:]],axis=1)
            ds=(p*dpT).astype(bf16)
            dvs.append(dot(p.astype(bf16),do_ref[qs,:]))
            dks.append(dot(ds,q[qs]))
            t=dot(kt[64*h:64*h+64,ks],ds)
            if j==0: dqt_ref[64*h:64*h+64,:]=t
            else: dqt_ref[64*h:64*h+64,qs]+=t
        dv_ref[ks,:]=jnp.where(first,dvs[0],dvs[1]).astype(bf16)
        dk_ref[ks,:]=jnp.where(first,dks[0],dks[1]).astype(bf16)
    dq_ref[...]=(dqt_ref[...]*0.125).T.astype(bf16)

def attn_bwd(length,slopes3,qkv,o,lse,do,start):
    n=qkv.shape[0]; D=qkv.shape[1]//3; np_=D//128
    length=jnp.stack([length,jnp.int32(start)])
    spec=lambda off: pl.BlockSpec((n,128),lambda p,*_: (0,p+off))
    return pl.pallas_call(attn_bwd_kernel,
        grid_spec=pltpu.PrefetchScalarGridSpec(num_scalar_prefetch=2,grid=(np_,),
            in_specs=[spec(0),spec(np_),spec(2*np_),spec(0),spec(0),spec(start)],out_specs=[spec(0)]*3,
            scratch_shapes=[pltpu.VMEM((2,n,256),bf16),pltpu.VMEM((2,n,256),bf16),pltpu.VMEM((128,n),f32)]),
        out_shape=[jax.ShapeDtypeStruct((n,D),bf16)]*3,
        compiler_params=pltpu.CompilerParams(vmem_limit_bytes=48*2**20),
        cost_estimate=pl.CostEstimate(flops=int(5*2*n*n*D*2.5),bytes_accessed=n*D*20,transcendentals=n*n*10),
        name="attn_bwd")(length,slopes3,qkv,qkv,qkv,o,lse,do)


def layer_norm(values, gain, shift):
    center = values - jnp.mean(values, axis=-1, keepdims=True)
    spread = jnp.mean(center * center, axis=-1, keepdims=True)
    return center * lax.rsqrt(spread + 1e-05) * gain + shift


def gelu_tanh(values):
    return jax.nn.gelu(values, approximate=True)


def generic_shards(
    tokens,
    ln1_gain,
    ln1_bias,
    qkv_weight,
    qkv_bias,
    dense_weight,
    dense_bias,
    ln2_gain,
    ln2_bias,
    up_weight,
    up_bias,
    down_weight,
    down_bias,
    cotangent,
    seq_lengths,
    slot_order,
):
    rows = tokens.shape[0]
    width = tokens.shape[1]
    group = rows * lax.axis_size("seq")
    f32 = jnp.float32
    bf16 = jnp.bfloat16
    window = SEQLEN
    w_qkv, w_dense, w_up, w_down = (
        lax.all_gather(qkv_weight, ("dp", "seq"), axis=0, tiled=True),
        lax.all_gather(dense_weight, ("dp", "seq"), axis=0, tiled=True),
        lax.all_gather(up_weight, ("dp", "seq"), axis=0, tiled=True),
        lax.all_gather(down_weight, ("dp", "seq"), axis=0, tiled=True),
    )
    order_group = lax.dynamic_slice_in_dim(slot_order, lax.axis_index("dp") * SG, SG)
    every_seq = jnp.arange(seq_lengths.shape[0], dtype=jnp.int32)
    lengths_group = jnp.sum(
        jnp.where(every_seq[None, :] == order_group[:, None], seq_lengths[None, :], 0), axis=1
    )
    slot_numbers = jnp.arange(SG, dtype=jnp.int32)

    def length_of(slots):
        return jnp.sum(
            jnp.where(slots[:, None] == slot_numbers[None, :], lengths_group[None, :], 0), axis=1
        )

    first_row = lax.axis_index("seq") * rows
    window_start = jnp.minimum(first_row // SEQLEN * SEQLEN, group - window)
    key_index = window_start + jnp.arange(window, dtype=jnp.int32)
    key_slot = key_index // SEQLEN
    key_place = key_index % SEQLEN
    key_live = key_place < length_of(key_slot)
    query_index = first_row + jnp.arange(rows, dtype=jnp.int32)
    query_slot = query_index // SEQLEN
    query_place = query_index % SEQLEN
    valid = (query_place < length_of(query_slot)).astype(f32)
    allowed = (
        (query_slot[:, None] == key_slot[None, :])
        & (key_place[None, :] <= query_place[:, None])
        & key_live[None, :]
    )
    offset = (key_place[None, :] - query_place[:, None]).astype(f32)
    slopes = jnp.exp2(-8.0 * (jnp.arange(H, dtype=f32) + 1.0) / H)
    inputs = tokens.astype(f32)
    normed_one, norm_one_back = jax.vjp(layer_norm, inputs, ln1_gain, ln1_bias)
    normed_low = normed_one.astype(bf16)
    bias_full = jnp.concatenate([qkv_bias[:width], jnp.zeros((width,), f32), qkv_bias[width:]])
    joined = (jnp.dot(normed_low, w_qkv, preferred_element_type=f32) + bias_full).astype(bf16)
    query = joined[:, :width]
    keys_group, values_group = (
        lax.all_gather(joined[:, width : 2 * width], "seq", axis=0, tiled=True),
        lax.all_gather(joined[:, 2 * width :], "seq", axis=0, tiled=True),
    )
    keys_all = lax.dynamic_slice_in_dim(keys_group, window_start, window, 0)
    values_all = lax.dynamic_slice_in_dim(values_group, window_start, window, 0)

    def split_heads(matrix):
        return matrix.reshape(matrix.shape[0], H, width // H).transpose(1, 0, 2)

    def merge_heads(stack):
        return stack.transpose(1, 0, 2).reshape(stack.shape[1], width)

    head_queries = split_heads(query)
    head_keys = split_heads(keys_all)
    head_values = split_heads(values_all)

    def scores_of(head_query, head_key, head_slope):
        scores = jnp.einsum("qd,kd->qk", head_query, head_key, preferred_element_type=f32) * 0.125
        return jnp.where(allowed, scores + head_slope * offset, -1e30)

    def head_forward(packed):
        head_query, head_key, head_value, head_slope = packed
        scores = scores_of(head_query, head_key, head_slope)
        top = jnp.max(scores, axis=-1, keepdims=True)
        expo = jnp.exp(scores - top)
        totals = jnp.sum(expo, axis=-1, keepdims=True)
        probs = (expo / totals).astype(bf16)
        result = jnp.einsum("qk,kd->qd", probs, head_value, preferred_element_type=f32)
        return (result, top[:, 0] + jnp.log(totals[:, 0]))

    head_context, head_lse = lax.map(head_forward, (head_queries, head_keys, head_values, slopes))
    context = merge_heads(head_context).astype(bf16)
    hidden = inputs + jnp.dot(context, w_dense, preferred_element_type=f32) + dense_bias
    normed_two, norm_two_back = jax.vjp(layer_norm, hidden, ln2_gain, ln2_bias)
    normed_two_low = normed_two.astype(bf16)
    before = jnp.dot(normed_two_low, w_up, preferred_element_type=f32) + up_bias
    active, gelu_back = jax.vjp(gelu_tanh, before)
    active_low = active.astype(bf16)
    outputs = hidden + jnp.dot(active_low, w_down, preferred_element_type=f32) + down_bias
    block_output = outputs.astype(bf16)
    back_qkv, back_dense, back_up, back_down = (
        lax.all_gather(qkv_weight, ("dp", "seq"), axis=0, tiled=True),
        lax.all_gather(dense_weight, ("dp", "seq"), axis=0, tiled=True),
        lax.all_gather(up_weight, ("dp", "seq"), axis=0, tiled=True),
        lax.all_gather(down_weight, ("dp", "seq"), axis=0, tiled=True),
    )
    grad_out = cotangent.astype(f32) * valid[:, None]
    grad_out_low = grad_out.astype(bf16)
    grad_down_w = jnp.einsum("rf,rd->fd", active_low, grad_out_low, preferred_element_type=f32)
    grad_down_b = jnp.sum(grad_out_low.astype(f32), axis=0)
    grad_active = jnp.einsum("rd,fd->rf", grad_out_low, back_down, preferred_element_type=f32)
    (grad_before,) = gelu_back(grad_active)
    grad_before_low = grad_before.astype(bf16)
    grad_up_w = jnp.einsum("rd,rf->df", normed_two_low, grad_before_low, preferred_element_type=f32)
    grad_up_b = jnp.sum(grad_before_low.astype(f32), axis=0)
    grad_normed_two = jnp.einsum("rf,df->rd", grad_before_low, back_up, preferred_element_type=f32)
    grad_hidden_norm, grad_gain_two, grad_shift_two = norm_two_back(grad_normed_two)
    grad_hidden = grad_out + grad_hidden_norm
    grad_hidden_low = grad_hidden.astype(bf16)
    grad_dense_w = jnp.einsum("rd,re->de", context, grad_hidden_low, preferred_element_type=f32)
    grad_dense_b = jnp.sum(grad_hidden_low.astype(f32), axis=0)
    grad_context = jnp.einsum(
        "re,de->rd", grad_hidden_low, back_dense, preferred_element_type=f32
    ).astype(bf16)

    def head_backward(packed):
        head_query, head_key, head_value, head_slope, head_grad, head_norm = packed
        scores = scores_of(head_query, head_key, head_slope)
        probs = jnp.exp(scores - head_norm[:, None])
        prob_grad = jnp.einsum("qd,kd->qk", head_grad, head_value, preferred_element_type=f32)
        value_grad = jnp.einsum(
            "qk,qd->kd", probs.astype(bf16), head_grad, preferred_element_type=f32
        )
        row_dot = jnp.sum(probs * prob_grad, axis=-1, keepdims=True)
        score_grad = (probs * (prob_grad - row_dot)).astype(bf16)
        query_grad = (
            jnp.einsum("qk,kd->qd", score_grad, head_key, preferred_element_type=f32) * 0.125
        )
        key_grad = (
            jnp.einsum("qk,qd->kd", score_grad, head_query, preferred_element_type=f32) * 0.125
        )
        return (query_grad, key_grad, value_grad)

    grad_queries, grad_keys, grad_values = lax.map(
        head_backward,
        (head_queries, head_keys, head_values, slopes, split_heads(grad_context), head_lse),
    )
    empty_group = jnp.zeros((group, width), f32)
    key_terms = lax.dynamic_update_slice_in_dim(
        empty_group, merge_heads(grad_keys), window_start, 0
    )
    value_terms = lax.dynamic_update_slice_in_dim(
        empty_group, merge_heads(grad_values), window_start, 0
    )
    grad_key, grad_value = (
        lax.psum_scatter(
            key_terms.astype(jnp.bfloat16), "seq", scatter_dimension=0, tiled=True
        ).astype(jnp.float32),
        lax.psum_scatter(
            value_terms.astype(jnp.bfloat16), "seq", scatter_dimension=0, tiled=True
        ).astype(jnp.float32),
    )
    grad_query = merge_heads(grad_queries)
    grad_joined = jnp.concatenate([grad_query, grad_key, grad_value], axis=1).astype(bf16)
    grad_qkv_w = jnp.einsum("rd,rc->dc", normed_low, grad_joined, preferred_element_type=f32)
    joined_sums = jnp.sum(grad_joined.astype(f32), axis=0)
    grad_qkv_b = jnp.concatenate([joined_sums[:width], joined_sums[2 * width :]])
    grad_normed_one = jnp.einsum("rc,dc->rd", grad_joined, back_qkv, preferred_element_type=f32)
    grad_input_norm, grad_gain_one, grad_shift_one = norm_one_back(grad_normed_one)
    token_grad = (grad_hidden + grad_input_norm).astype(bf16)
    owner_qkv, owner_dense, owner_up, owner_down = (
        lax.psum_scatter(grad_qkv_w, ("dp", "seq"), scatter_dimension=0, tiled=True),
        lax.psum_scatter(grad_dense_w, ("dp", "seq"), scatter_dimension=0, tiled=True),
        lax.psum_scatter(grad_up_w, ("dp", "seq"), scatter_dimension=0, tiled=True),
        lax.psum_scatter(grad_down_w, ("dp", "seq"), scatter_dimension=0, tiled=True),
    )
    (
        total_gain_one,
        total_shift_one,
        total_qkv_b,
        total_dense_b,
        total_gain_two,
        total_shift_two,
        total_up_b,
        total_down_b,
    ) = lax.psum(
        (
            grad_gain_one,
            grad_shift_one,
            grad_qkv_b,
            grad_dense_b,
            grad_gain_two,
            grad_shift_two,
            grad_up_b,
            grad_down_b,
        ),
        ("dp", "seq"),
    )
    return (
        block_output,
        token_grad,
        total_gain_one,
        total_shift_one,
        owner_qkv,
        total_qkv_b,
        owner_dense,
        total_dense_b,
        total_gain_two,
        total_shift_two,
        owner_up,
        total_up_b,
        owner_down,
        total_down_b,
    )


ALL = ("dp", "seq")


def flat_index(z, y, c, x):
    return ((z * 2 + y) * 2 + c) * 2 + x


TN = (((0,), (0,)), ((), ()))
MIB = 2**20


def owner_of(place_ref, half, zr, near, turn, core, turned):
    z, y, c, x = (place_ref[i] for i in range(4))
    xr, yr = (near, turn) if half == 0 else (turn, near)
    za = (z + 4 - zr) % 4 if turned else zr
    return flat_index(za, y + yr - 2 * y * yr, c + core - 2 * c * core, x + xr - 2 * x * xr)


def start_mixed(place_ref, pieces, w_ref, sem, turned):
    for half, zr, near, turn, core in itertools.product(range(2), range(4), *[range(2)] * 3):
        d = owner_of(place_ref, half, zr, near, turn, core, turned)
        rows = pl.ds(pl.multiple_of(d * 32 + half * 16, 16), 16)
        src = pieces[4 * half + 2 * core + turn].at[near, zr]
        pltpu.make_async_copy(src, w_ref.at[:, rows, :], sem).start()


def of_half(pieces, half):
    return [pieces[5 * core + i] for core in range(2) for i in (0, 1, 2, 3 + half)]


def piece(pieces, half, zr, xr, yr, core):
    ref = pieces[4 * core + xr + 2 * yr]
    return ref.at[zr] if xr and yr else ref.at[zr, half]


def owner(place_ref, zr, xr, yr, core):
    _, y, c, x = (place_ref[i] for i in range(4))
    return flat_index(zr, y + yr - 2 * y * yr, c + core - 2 * c * core, x + xr - 2 * x * xr)


def start_columns(place_ref, pieces, w_ref, sem, half):
    for zr, xr, yr, core in itertools.product(range(4), *[range(2)] * 3):
        d = owner(place_ref, zr, xr, yr, core)
        rows = pl.ds(pl.multiple_of(d * 32, 32), 32)
        src = piece(pieces, half, zr, xr, yr, core)
        pltpu.make_async_copy(src, w_ref.at[:, rows, :], sem).start()


def wait_all(ref, sem):
    pltpu.make_async_copy(ref, ref, sem).wait()


def start_rows(place_ref, pieces, w_ref, sems, step):
    for zr in range(4):

        @pl.when(step == max(zr - 1, 0))
        def _(zr=zr):
            for half, xr, yr, core in itertools.product(range(2), repeat=4):
                d = owner(place_ref, zr, xr, yr, core)
                rows = pl.ds(pl.multiple_of(d * 128 + half * 64, 64), 64)
                src = piece(of_half(pieces, half), half, zr, xr, yr, core).at[0]
                pltpu.make_async_copy(src, w_ref.at[rows, :], sems.at[zr]).start()


def wait_rows(w_ref, sems, z):
    part = w_ref.at[pl.ds(pl.multiple_of(z * 1024, 1024), 1024), :]
    pltpu.make_async_copy(part, part, sems.at[z]).wait()


def dottn(a, b):
    return lax.dot_general(a, b, TN, preferred_element_type=f32)


def spec(shape, index):
    return pl.BlockSpec(shape, index)


def params(mib=56):
    return pltpu.CompilerParams(vmem_limit_bytes=mib * MIB)


HBM = pl.BlockSpec(memory_space=pltpu.HBM)


def qkv_kernel(turned, place_ref, *refs):
    pieces, (a_ref, b_ref, o_ref, all_ref, w_ref, sem, out_sem) = refs[:8], refs[8:]
    step = pl.program_id(0)
    write = pltpu.make_async_copy(w_ref, all_ref, out_sem)

    @pl.when(step == 0)
    def _():
        start_mixed(place_ref, pieces, w_ref, sem, turned)
        wait_all(w_ref, sem)
        write.start()

    o_ref[...] = (dot(a_ref[...], w_ref[step]) + b_ref[...]).astype(bf16)

    @pl.when(step == 2)
    def _():
        write.wait()


def qkv_call(place, pieces, a, b, turned):
    n, d = a.shape
    blocks = pieces[0].shape[2]
    return pl.pallas_call(
        functools.partial(qkv_kernel, turned),
        grid_spec=pltpu.PrefetchScalarGridSpec(
            num_scalar_prefetch=1,
            grid=(3,),
            in_specs=[HBM] * 8
            + [spec((n, d), lambda i, *_: (0, 0)), spec((1, 512), lambda i, *_: (0, i))],
            out_specs=[spec((n, 512), lambda i, *_: (0, i)), HBM],
            scratch_shapes=[
                pltpu.VMEM((blocks, d, 512), bf16),
                pltpu.SemaphoreType.DMA,
                pltpu.SemaphoreType.DMA,
            ],
        ),
        out_shape=[
            jax.ShapeDtypeStruct((n, 1536), bf16),
            jax.ShapeDtypeStruct((blocks, d, 512), bf16),
        ],
        compiler_params=params(63),
        cost_estimate=pl.CostEstimate(
            flops=2 * n * d * 1536, bytes_accessed=2 * (n * d + 8 * d * 512 + 1536 * n), transcendentals=0
        ),
        name="qkv",
    )(place, *pieces, a, b.reshape(1, 1536))


def dense_kernel(c0_ref, c1_ref, w0_ref, w1_ref, x_ref, b_ref, g_ref, s_ref, h_ref, a_ref):
    half = [
        dot(c0_ref[...], w_ref[0, :512, :]) + dot(c1_ref[...], w_ref[0, 512:, :])
        for w_ref in (w0_ref, w1_ref)
    ]
    hidden = x_ref[...].astype(f32) + jnp.concatenate(half, axis=1) + b_ref[...]
    h_ref[...] = hidden
    center = hidden - jnp.mean(hidden, axis=1, keepdims=True)
    rsd = lax.rsqrt(jnp.mean(center * center, axis=1, keepdims=True) + 1e-05)
    a_ref[...] = (center * rsd * g_ref[...] + s_ref[...]).astype(bf16)


def dense_call(c0, c1, w, x, bias, gain, shift):
    n, d = x.shape
    rows = lambda c: spec((256, c), lambda i: (i, 0))
    vector = spec((1, d), lambda i: (0, 0))
    return pl.pallas_call(
        dense_kernel,
        grid=(n // 256,),
        in_specs=[rows(512), rows(512)]
        + [spec((1, d, 512), lambda i, b=b: (b, 0, 0)) for b in (3, 4)]
        + [rows(d), vector, vector, vector],
        out_specs=[rows(d), rows(d)],
        out_shape=[jax.ShapeDtypeStruct((n, d), f32), jax.ShapeDtypeStruct((n, d), bf16)],
        compiler_params=params(40),
        cost_estimate=pl.CostEstimate(flops=2 * n * d * d, bytes_accessed=12 * n * d, transcendentals=0),
        name="dense",
    )(c0, c1, w, w, x, bias.reshape(1, d), gain.reshape(1, d), shift.reshape(1, d))


def dense_back_kernel(g_ref, w0_ref, w1_ref, o_ref):
    o_ref[...] = (
        dotnt(g_ref[:, :512], w0_ref[0]) + dotnt(g_ref[:, 512:], w1_ref[0])
    ).astype(bf16)


def dense_back_call(g, w):
    n, d = g.shape
    rows = spec((256, d), lambda i: (i, 0))
    return pl.pallas_call(
        dense_back_kernel,
        grid=(n // 256,),
        in_specs=[rows] + [spec((1, d, 512), lambda i, b=b: (b, 0, 0)) for b in (3, 4)],
        out_specs=rows,
        out_shape=jax.ShapeDtypeStruct((n, d), bf16),
        compiler_params=params(40),
        cost_estimate=pl.CostEstimate(flops=2 * n * d * d, bytes_accessed=6 * n * d, transcendentals=0),
        name="dense_back",
    )(g, w, w)


def up_kernel(place_ref, *refs):
    pieces, (a_ref, b_ref, u0_ref, u1_ref, s0_ref, s1_ref, w_ref, sems) = refs[:10], refs[10:]
    step = pl.program_id(0)
    for half in range(2):
        part = w_ref.at[2 * half : 2 * half + 2]

        @pl.when(step == half)
        def _(half=half, part=part):
            start_columns(place_ref, of_half(pieces, half), part, sems.at[half], half)

        @pl.when(step == 4 * half)
        def _(half=half, part=part):
            wait_all(part, sems.at[half])

    c = 0.7978845608028654

    def block(u_ref, s_ref):
        w = w_ref[step // 2, :, pl.ds(pl.multiple_of(step % 2 * 512, 512), 512)]
        for r in range(0, a_ref.shape[0], 256):
            v = dot(a_ref[r : r + 256, :], w) + b_ref[...]
            square = v * v
            h = 0.5 + 0.5 * jnp.tanh(v * (c + (c * 0.044715) * square))
            u = v * h
            u_ref[r : r + 256, :] = u.astype(bf16)
            s_ref[r : r + 256, :] = (
                h + u * (1.0 - h) * (2.0 * c + (2.0 * c * 0.134145) * square)
            ).astype(bf16)

    @pl.when(step < 4)
    def _():
        block(u0_ref, s0_ref)

    @pl.when(step >= 4)
    def _():
        block(u1_ref, s1_ref)


def up_call(place, pieces, a, b):
    n, d = a.shape
    outs = [
        spec((n, 512), lambda i, *_: (0, jnp.minimum(i, 3))),
        spec((n, 512), lambda i, *_: (0, jnp.maximum(i - 4, 0))),
    ]
    return pl.pallas_call(
        up_kernel,
        grid_spec=pltpu.PrefetchScalarGridSpec(
            num_scalar_prefetch=1,
            grid=(8,),
            in_specs=[HBM] * 10
            + [spec((n, d), lambda i, *_: (0, 0)), spec((1, 512), lambda i, *_: (0, i))],
            out_specs=outs + outs,
            scratch_shapes=[pltpu.VMEM((4, d, 1024), bf16), pltpu.SemaphoreType.DMA((2,))],
        ),
        out_shape=[jax.ShapeDtypeStruct((n, 2048), bf16)] * 4,
        compiler_params=params(),
        cost_estimate=pl.CostEstimate(
            flops=2 * n * d * 4096, bytes_accessed=2 * (n * d + d * 4096 + 8192 * n), transcendentals=n * 4096
        ),
        name="up",
    )(place, *pieces, a, b.reshape(1, 4096))


def divide(acc_ref, keep_ref, give_ref, core):
    keep_ref[...] = acc_ref[:, pl.ds(core, 1)].reshape(keep_ref.shape)
    give_ref[...] = acc_ref[:, pl.ds(1 - core, 1)].reshape(give_ref.shape)


def down_grad_kernel(where_ref, u0_ref, u1_ref, g_ref, keep_ref, give_ref, acc_ref):
    step = pl.program_id(0)
    for half, u_ref in enumerate((u0_ref, u1_ref)):

        @pl.when(step // 4 == half)
        def _(u_ref=u_ref):
            acc_ref[...] = dottn(u_ref[...], g_ref[...]).astype(bf16).reshape(acc_ref.shape)

    divide(acc_ref, keep_ref, give_ref, where_ref[2])


def down_grad_call(where, u, g):
    n, d = g.shape
    out = spec((1, 256, d), lambda i, *_: (i, 0, 0))
    return pl.pallas_call(
        down_grad_kernel,
        grid_spec=pltpu.PrefetchScalarGridSpec(
            num_scalar_prefetch=1,
            grid=(8,),
            in_specs=[
                spec((n, 512), lambda i, *_: (0, jnp.minimum(i, 3))),
                spec((n, 512), lambda i, *_: (0, jnp.maximum(i - 4, 0))),
                spec((n, d), lambda i, *_: (0, 0)),
            ],
            out_specs=[out, out],
            scratch_shapes=[pltpu.VMEM((1, 2, 256, d), bf16)],
        ),
        out_shape=[jax.ShapeDtypeStruct((8, 256, d), bf16)] * 2,
        compiler_params=params(40),
        cost_estimate=pl.CostEstimate(
            flops=2 * n * d * 4096, bytes_accessed=2 * (n * d + d * 4096 + n * 4096), transcendentals=0
        ),
        name="down_grad",
    )(where, *u, g)


def down_kernel(place_ref, *refs):
    pieces, (u0_ref, u1_ref, h_ref, b_ref, o_ref, acc_ref, w_ref, sems) = refs[:10], refs[10:]
    step = pl.program_id(0)

    start_rows(place_ref, pieces, w_ref, sems, step)
    wait_rows(w_ref, sems, step)
    w = w_ref[pl.ds(pl.multiple_of(step * 1024, 1024), 1024), :]

    @pl.when(step == 0)
    def _():
        acc_ref[...] = dot(u0_ref[...], w)

    @pl.when(step == 1)
    def _():
        acc_ref[...] += dot(u0_ref[...], w)

    @pl.when(step == 2)
    def _():
        acc_ref[...] += dot(u1_ref[...], w)

    @pl.when(step == 3)
    def _():
        for r in range(0, u1_ref.shape[0], 256):
            rows = slice(r, r + 256)
            part = acc_ref[rows, :] + dot(u1_ref[rows, :], w)
            o_ref[rows, :] = (h_ref[rows, :] + part + b_ref[...]).astype(bf16)


def down_call(place, pieces, u, hidden, bias):
    n, d = hidden.shape
    whole = lambda s: spec(s, lambda i, *_: (0, 0))
    return pl.pallas_call(
        down_kernel,
        grid_spec=pltpu.PrefetchScalarGridSpec(
            num_scalar_prefetch=1,
            grid=(4,),
            in_specs=[HBM] * 10
            + [
                spec((n, 1024), lambda i, *_: (0, jnp.minimum(i, 1))),
                spec((n, 1024), lambda i, *_: (0, jnp.maximum(i - 2, 0))),
                whole((n, d)),
                whole((1, d)),
            ],
            out_specs=whole((n, d)),
            scratch_shapes=[
                pltpu.VMEM((n, d), f32),
                pltpu.VMEM((4096, d), bf16),
                pltpu.SemaphoreType.DMA((4,)),
            ],
        ),
        out_shape=jax.ShapeDtypeStruct((n, d), bf16),
        compiler_params=params(),
        cost_estimate=pl.CostEstimate(
            flops=2 * n * d * 4096, bytes_accessed=2 * (3 * n * d + d * 4096 + n * 4096), transcendentals=0
        ),
        name="down",
    )(place, *pieces, *u, hidden, bias.reshape(1, d))


def gate_kernel(place_ref, *refs):
    pieces, (g_ref, s0_ref, s1_ref, z_ref, b_ref, w_ref, sems) = refs[:10], refs[10:]
    step = pl.program_id(0)

    start_rows(place_ref, pieces, w_ref, sems, step)
    wait_rows(w_ref, sems, step)
    w = w_ref[pl.ds(pl.multiple_of(step * 1024, 1024), 1024), :]
    total = None
    for r in range(0, g_ref.shape[0], 256):
        rows = slice(r, r + 256)
        slope = jnp.where(step < 2, s0_ref[rows, :], s1_ref[rows, :])
        v = (dotnt(g_ref[rows, :], w) * slope.astype(f32)).astype(bf16)
        z_ref[rows, :] = v
        part = jnp.sum(v.astype(f32).reshape(32, 8, v.shape[1]), axis=0)
        total = part if total is None else total + part
    b_ref[...] = jnp.sum(total, axis=0, keepdims=True)


def gate_call(place, pieces, g, slopes):
    n, d = g.shape
    return pl.pallas_call(
        gate_kernel,
        grid_spec=pltpu.PrefetchScalarGridSpec(
            num_scalar_prefetch=1,
            grid=(4,),
            in_specs=[HBM] * 10
            + [
                spec((n, d), lambda i, *_: (0, 0)),
                spec((n, 1024), lambda i, *_: (0, jnp.minimum(i, 1))),
                spec((n, 1024), lambda i, *_: (0, jnp.maximum(i - 2, 0))),
            ],
            out_specs=[
                spec((n, 1024), lambda i, *_: (0, i)),
                spec((1, 1024), lambda i, *_: (0, i)),
            ],
            scratch_shapes=[pltpu.VMEM((4096, d), bf16), pltpu.SemaphoreType.DMA((4,))],
        ),
        out_shape=[jax.ShapeDtypeStruct((n, 4096), bf16), jax.ShapeDtypeStruct((1, 4096), f32)],
        compiler_params=params(),
        cost_estimate=pl.CostEstimate(
            flops=2 * n * d * 4096, bytes_accessed=2 * (n * d + d * 4096 + 8192 * n), transcendentals=0
        ),
        name="gate",
    )(place, *pieces, g, *slopes)


def norm_back(x_ref, gain_ref, res_ref, acc_ref, out_refs, sums_ref):
    n, d = x_ref.shape

    def chunk(i, sums):
        rows = pl.ds(pl.multiple_of(i * 128, 128), 128)
        grad = acc_ref[rows, :]
        x = x_ref[rows, :].astype(f32)
        center = x - jnp.mean(x, axis=1, keepdims=True)
        rsd = lax.rsqrt(jnp.mean(center * center, axis=1, keepdims=True) + 1e-05)
        hat = center * rsd
        e = grad * gain_ref[...]
        back = rsd * (
            e - jnp.mean(e, axis=1, keepdims=True) - hat * jnp.mean(e * hat, axis=1, keepdims=True)
        )
        result = res_ref[rows, :].astype(f32) + back
        low = result.astype(bf16)
        out_refs[0][rows, :] = low
        if len(out_refs) > 1:
            out_refs[1][rows, :] = result
        fold = lambda v: jnp.sum(v.reshape(16, 8, d), axis=0)
        return sums[0] + fold(grad * hat), sums[1] + fold(grad), sums[2] + fold(low.astype(f32))

    zero = jnp.zeros((8, d), f32)
    sums = lax.fori_loop(0, n // 128, chunk, (zero, zero, zero))
    for k in range(3):
        sums_ref[k : k + 1, :] = jnp.sum(sums[k], axis=0, keepdims=True)


def norm_up_kernel(place_ref, *refs):
    pieces, (g_ref, x_ref, gain_ref, res_ref, low_ref, wide_ref, sums_ref, acc_ref, w_ref, sems) = (
        refs[:10],
        refs[10:],
    )
    step = pl.program_id(0)

    for half in range(2):

        @pl.when(step == half)
        def _(half=half):
            part = w_ref.at[2 * half : 2 * half + 2]
            start_columns(place_ref, of_half(pieces, half), part, sems.at[half], half)

    for half in range(2):

        @pl.when(step == 2 * half)
        def _():
            wait_all(w_ref.at[2 * half : 2 * half + 2], sems.at[half])

    @pl.when(step == 0)
    def _():
        acc_ref[...] = dotnt(g_ref[...], w_ref[0])

    @pl.when(step > 0)
    def _():
        acc_ref[...] += dotnt(g_ref[...], w_ref[step])

    @pl.when(step == 3)
    def _():
        norm_back(x_ref, gain_ref, res_ref, acc_ref, (low_ref, wide_ref), sums_ref)


def norm_up_call(place, pieces, g, x, gain, residual):
    n, d = x.shape
    ff = g.shape[1]
    whole = lambda s: spec(s, lambda i, *_: (0, 0))
    return pl.pallas_call(
        norm_up_kernel,
        grid_spec=pltpu.PrefetchScalarGridSpec(
            num_scalar_prefetch=1,
            grid=(4,),
            in_specs=[HBM] * 10
            + [spec((n, 1024), lambda i, *_: (0, i)), whole((n, d)), whole((1, d)), whole((n, d))],
            out_specs=[whole((n, d)), whole((n, d)), whole((8, d))],
            scratch_shapes=[
                pltpu.VMEM((n, d), f32),
                pltpu.VMEM((4, d, 1024), bf16),
                pltpu.SemaphoreType.DMA((2,)),
            ],
        ),
        out_shape=[
            jax.ShapeDtypeStruct((n, d), bf16),
            jax.ShapeDtypeStruct((n, d), f32),
            jax.ShapeDtypeStruct((8, d), f32),
        ],
        compiler_params=params(),
        cost_estimate=pl.CostEstimate(
            flops=2 * n * d * ff, bytes_accessed=2 * (8 * n * d + 2 * d * ff), transcendentals=0
        ),
        name="norm_up",
    )(place, *pieces, g, x, gain.reshape(1, d), residual)


def norm_qkv_kernel(*refs):
    g_refs = refs[:6]
    w0_ref, w1_ref, x_ref, gain_ref, res_ref, low_ref, sums_ref, acc_ref = refs[6:]
    step = pl.program_id(0)
    for i in range(3):

        @pl.when(step == i)
        def _(i=i):
            part = dotnt(g_refs[i][...], w0_ref[0]) + dotnt(g_refs[3 + i][...], w1_ref[0])
            acc_ref[...] = part if i == 0 else acc_ref[...] + part

    @pl.when(step == 2)
    def _():
        norm_back(x_ref, gain_ref, res_ref, acc_ref, (low_ref,), sums_ref)


def norm_qkv_call(grads, w0, w1, x, gain, residual):
    n, d = x.shape
    whole = lambda s: spec(s, lambda i: (0, 0))
    return pl.pallas_call(
        norm_qkv_kernel,
        grid=(3,),
        in_specs=[whole((n, 512))] * 6
        + [spec((1, d, 512), lambda i: (i, 0, 0))] * 2
        + [whole((n, d)), whole((1, d)), whole((n, d))],
        out_specs=[whole((n, d)), whole((8, d))],
        out_shape=[jax.ShapeDtypeStruct((n, d), bf16), jax.ShapeDtypeStruct((8, d), f32)],
        scratch_shapes=[pltpu.VMEM((n, d), f32)],
        compiler_params=params(),
        cost_estimate=pl.CostEstimate(
            flops=2 * n * d * 3072, bytes_accessed=2 * (8 * n * d + d * 3072), transcendentals=0
        ),
        name="norm_qkv",
    )(*grads, w0, w1, x, gain.reshape(1, d), residual)


def columns_kernel(plan, parts, where_ref, *refs):
    count = sum(parts)
    left_refs, right_refs = refs[:count], refs[count : count + len(plan)]
    keep_ref, give_ref, sums_ref, at_ref, acc_ref = refs[-5:]
    step = pl.program_id(0)
    for i, left in enumerate(plan):

        @pl.when(step == i)
        def _(i=i, left=left):
            if i == 0 or plan[i - 1] != left:
                begin = sum(parts[:left])
                row = 0
                for ref in left_refs[begin : begin + parts[left]]:
                    at_ref[row : row + ref.shape[1], :] = ref[...].T
                    row += ref.shape[1]
            right = right_refs[i][...]
            acc = dot(at_ref[...], right)
            acc_ref[...] = acc.astype(bf16).reshape(acc_ref.shape)
            total = jnp.sum(right.astype(f32).reshape(-1, 8, right.shape[1]), axis=0)
            sums_ref[...] = jnp.sum(total, axis=0, keepdims=True)

    divide(acc_ref, keep_ref, give_ref, where_ref[2])


def columns_call(where, lefts, rights, plan, name):
    flat = [a for left in lefts for a in left]
    n = flat[0].shape[0]
    d = sum(a.shape[1] for a in lefts[0])
    wide = 512 * len(rights)
    out = spec((8, 64, 512), lambda i, *_: (0, 0, i))
    return pl.pallas_call(
        functools.partial(columns_kernel, plan, [len(left) for left in lefts]),
        grid_spec=pltpu.PrefetchScalarGridSpec(
            num_scalar_prefetch=1,
            grid=(len(plan),),
            in_specs=[spec(a.shape, lambda i, *_: (0, 0)) for a in flat]
            + [spec((n, 512), lambda i, *_, b=b: (0, b)) for _, b in rights],
            out_specs=[out, out, spec((1, 512), lambda i, *_: (0, i))],
            scratch_shapes=[pltpu.VMEM((d, n), bf16), pltpu.VMEM((8, 2, 64, 512), bf16)],
        ),
        out_shape=[jax.ShapeDtypeStruct((8, 64, wide), bf16)] * 2
        + [jax.ShapeDtypeStruct((1, wide), f32)],
        compiler_params=params(40),
        cost_estimate=pl.CostEstimate(
            flops=2 * n * d * wide, bytes_accessed=2 * (2 * n * d + d * wide + n * wide), transcendentals=0
        ),
        name=name,
    )(where, *flat, *[r for r, _ in rights])


def up_grad_kernel(where_ref, a_ref, g_ref, keep_ref, give_ref, at_ref, acc_ref):
    @pl.when(pl.program_id(0) == 0)
    def _():
        at_ref[...] = a_ref[...].T

    acc_ref[...] = dot(at_ref[...], g_ref[...]).astype(bf16).reshape(acc_ref.shape)
    divide(acc_ref, keep_ref, give_ref, where_ref[2])


def up_grad_call(where, a, g):
    n, d = a.shape
    ff = g.shape[1]
    out = spec((8, 64, 512), lambda i, *_: (0, 0, i))
    return pl.pallas_call(
        up_grad_kernel,
        grid_spec=pltpu.PrefetchScalarGridSpec(
            num_scalar_prefetch=1,
            grid=(ff // 512,),
            in_specs=[spec((n, d), lambda i, *_: (0, 0)), spec((n, 512), lambda i, *_: (0, i))],
            out_specs=[out, out],
            scratch_shapes=[pltpu.VMEM((d, n), bf16), pltpu.VMEM((8, 2, 64, 512), bf16)],
        ),
        out_shape=[jax.ShapeDtypeStruct((8, 64, ff), bf16)] * 2,
        compiler_params=params(40),
        cost_estimate=pl.CostEstimate(
            flops=2 * n * d * ff, bytes_accessed=2 * (n * d + d * ff + n * ff), transcendentals=0
        ),
        name="up_grad",
    )(where, a, g)


def permutation(move):
    pairs = []
    for z in range(4):
        for y in range(2):
            for c in range(2):
                for x in range(2):
                    pairs.append((flat_index(z, y, c, x), flat_index(*move(z, y, c, x))))
    return pairs


OVER_X = permutation(lambda z, y, c, x: (z, y, c, 1 - x))
OVER_Y = permutation(lambda z, y, c, x: (z, 1 - y, c, x))
OVER_C = permutation(lambda z, y, c, x: (z, y, 1 - c, x))
OVER_CX = permutation(lambda z, y, c, x: (z, y, 1 - c, 1 - x))
OVER_Z = [permutation(lambda z, y, c, x, k=k: ((z + k) % 4, y, c, x)) for k in range(4)]


Z_GROUPS = [
    [flat_index(z, y, c, x) for z in range(4)] for y in range(2) for c in range(2) for x in range(2)
]


def send(array, pairs):
    return lax.ppermute(array, ALL, pairs)


def plain(array):
    return with_layout_constraint(array, Layout(major_to_minor=tuple(range(array.ndim))))


def tie(*trees):
    return lax.optimization_barrier(trees)


def gather_z(shard):
    return [shard] + [send(shard, OVER_Z[k]) for k in (1, 2, 3)]


def halves(parts):
    return jnp.stack([p[0] for p in parts]), jnp.stack([p[1] for p in parts])


def gather_z_line(shard):
    return plain(lax.all_gather(shard, ALL, axis=0, tiled=False, axis_index_groups=Z_GROUPS))


def scatter_z_line(array):
    return lax.psum_scatter(array, ALL, scatter_dimension=0, tiled=False, axis_index_groups=Z_GROUPS)


def add_low(a, b):
    return (a.astype(f32) + b.astype(f32)).astype(bf16)


def take(array, at, axis):
    return lax.dynamic_index_in_dim(array, at, axis, keepdims=False)


def fold(g, at, axis, pairs):
    return take(g, at, axis), send(take(g, 1 - at, axis), pairs)


def fold_second(a, b, place):
    return fold(a, place[3], 2, OVER_X), fold(b, place[1], 1, OVER_Y)


def fold_third(pair, place):
    a, b = (add_low(*p) for p in pair)
    return fold(a, place[1], 1, OVER_Y), fold(b, place[3], 1, OVER_X)


def both(pair):
    return jnp.stack([add_low(*p) for p in pair], axis=1)


def fold_z(pair, place):
    z = place[0]
    g = both(pair)
    return [take(g, z, 0)] + [send(take(g, (z + k) % 4, 0), OVER_Z[k]) for k in (1, 2, 3)]


def total(parts):
    return sum(p.astype(f32) for p in parts)


def slope_table():
    slopes = np.exp2(-8.0 * (np.arange(H) + 1.0) / H).astype(np.float32)
    pieces, rest = [], slopes
    for _ in range(3):
        low = rest.astype(ml_dtypes.bfloat16).astype(np.float32)
        pieces.append(low)
        rest = rest - low
    return np.stack(pieces, axis=1).reshape(-1)


def moments(v):
    mean = jnp.mean(v, axis=-1, keepdims=True)
    center = v - mean
    return center, lax.rsqrt(jnp.mean(center * center, axis=-1, keepdims=True) + 1e-05)


def fast_shards(
    tokens,
    ln1_gain,
    ln1_bias,
    qkv_weight,
    qkv_bias,
    dense_weight,
    dense_bias,
    ln2_gain,
    ln2_bias,
    up_weight,
    up_bias,
    down_weight,
    down_bias,
    cotangent,
    seq_lengths,
    slot_order,
):
    rows, width = tokens.shape
    dp, seq = lax.axis_index("dp"), lax.axis_index("seq")
    place = (dp // 4, (dp // 2) % 2, dp % 2, seq)
    place_vec = jnp.stack([p.astype(jnp.int32) for p in place])

    def mixed(*blocks):
        stacked = jnp.stack(blocks).reshape(len(blocks), 2, 16, 512)
        return stacked.transpose(1, 0, 2, 3)

    w_in = [qkv_weight[:, 512 * i : 512 * i + 512] for i in range(6)]
    one = mixed(*w_in[0::2], *w_in[1::2], dense_weight[:, :512], dense_weight[:, 512:])
    two = up_weight.reshape(32, 4, 1024).transpose(1, 0, 2).reshape(2, 2, 32, 1024)
    three = down_weight.reshape(2, 1, 64, 1024)

    slot = dp * SG + seq
    my_seq = lax.dynamic_index_in_dim(slot_order, slot, 0, keepdims=False)
    every_seq = jnp.arange(seq_lengths.shape[0], dtype=jnp.int32)
    length = jnp.sum(jnp.where(every_seq == my_seq, seq_lengths, 0))
    valid = (jnp.arange(rows, dtype=jnp.int32) < length).astype(f32)
    slopes_split = slope_table()
    no_bias = jnp.zeros((512,), f32)
    bias0 = jnp.concatenate([qkv_bias[:512], no_bias, qkv_bias[1024:1536]])
    bias1 = jnp.concatenate([qkv_bias[512:1024], no_bias, qkv_bias[1536:]])

    one_z = gather_z(one)
    one_z, two, tokens, cotangent = tie(one_z, two, tokens, cotangent)

    a, b = halves([p[:, :3] for p in one_z])
    one_x, one_y = send(a, OVER_X), send(b, OVER_Y)
    two_z = gather_z_line(two)
    also_za, also_zb = halves([p[:, 3:] for p in one_z])
    one_x, one_y, also_za, also_zb, tokens, cotangent = tie(
        one_x, one_y, also_za, also_zb, tokens, cotangent
    )

    one_a, one_b = jnp.stack([a, one_x]), jnp.stack([b, one_y])
    one_xy, one_yx = send(one_a, OVER_Y), send(one_b, OVER_X)
    one_ca, one_cb = send(one_a, OVER_C), send(one_b, OVER_C)
    center, rsd = moments(tokens.astype(f32))
    a1 = (center * rsd * ln1_gain + ln1_bias).astype(bf16)
    grad_low = cotangent * valid[:, None].astype(bf16)
    one_xy, one_yx, one_ca, one_cb, a1, grad_low = tie(
        one_xy, one_yx, one_ca, one_cb, a1, grad_low
    )
    one_cxy, one_cyx = send(one_xy, OVER_C), send(one_yx, OVER_C)
    a, b = also_za, also_zb
    one_cxy, one_cyx, a, b, three = tie(one_cxy, one_cyx, a, b, three)

    also_x, also_y = send(a, OVER_X), send(b, OVER_Y)
    pieces = (one_a, one_xy, one_ca, one_cxy, one_b, one_yx, one_cb, one_cyx)
    qkv0, w0 = qkv_call(place_vec, pieces, a1, bias0, True)
    qkv0, also_x, also_y, two_z = tie(qkv0, also_x, also_y, two_z)
    also_a, also_b = jnp.stack([a, also_x]), jnp.stack([b, also_y])
    also_xy, also_yx = send(also_a, OVER_Y), send(also_b, OVER_X)
    also_ca, also_cb = send(also_a, OVER_C), send(also_b, OVER_C)
    three_z = gather_z_line(three)
    context0, lse0 = attn_fwd(length, jnp.asarray(slopes_split), qkv0, 0)
    context0, also_xy, also_yx, also_ca, also_cb, a1 = tie(
        context0, also_xy, also_yx, also_ca, also_cb, a1
    )

    also_cxy, also_cyx = send(also_xy, OVER_C), send(also_yx, OVER_C)
    also_cxy, also_cyx = tie(also_cxy, also_cyx)
    pieces = (also_a, also_xy, also_ca, also_cxy, also_b, also_yx, also_cb, also_cyx)
    two_c = send(two_z, OVER_C)
    two_x, two_y = plain(send(two_z, OVER_X)), plain(send(two_z, OVER_Y))
    qkv1, w1 = qkv_call(place_vec, pieces, a1, bias1, True)
    qkv1, two_c, three_z = tie(qkv1, two_c, three_z)
    context1, lse1 = attn_fwd(length, jnp.asarray(slopes_split), qkv1, 4)
    context0, context1, two_x, two_y, three_z = tie(context0, context1, two_x, two_y, three_z)

    two_xy, two_yx = send(two_x[:, 0], OVER_Y), send(two_y[:, 1], OVER_X)
    two_cx, two_cy = send(two_x, OVER_C), send(two_y, OVER_C)
    hidden, a2 = dense_call(context0, context1, w1, tokens, dense_bias, ln2_gain, ln2_bias)
    a2, two_xy, two_yx, two_cx, two_cy, three_z = tie(a2, two_xy, two_yx, two_cx, two_cy, three_z)
    two_cxy, two_cyx = send(two_xy, OVER_C), send(two_yx, OVER_C)
    two_cxy, two_cyx, a2, three_z = tie(two_cxy, two_cyx, a2, three_z)

    three_c = send(three_z, OVER_C)
    three_x, three_y = plain(send(three_z, OVER_X)), plain(send(three_z, OVER_Y))
    up_pieces = (two_z, two_x, two_y, two_xy, two_yx, two_c, two_cx, two_cy, two_cxy, two_cyx)
    u0, u1, slope0, slope1 = up_call(place_vec, up_pieces, a2, up_bias)
    u0, u1, grad_low, three_x, three_y, three_c = tie(
        u0, u1, grad_low, three_x, three_y, three_c
    )
    three_xy, three_yx = send(three_x[:, 0], OVER_Y), send(three_y[:, 1], OVER_X)
    three_cx, three_cy = send(three_x, OVER_C), send(three_y, OVER_C)

    down_keep, down_give = down_grad_call(place_vec, (u0, u1), grad_low)
    down_keep, down_give, grad_low, three_cx, three_cy, three_xy, three_yx = tie(
        down_keep, down_give, grad_low, three_cx, three_cy, three_xy, three_yx
    )
    three_cxy, three_cyx = send(three_xy, OVER_C), send(three_yx, OVER_C)
    down_b = jnp.sum(grad_low.astype(f32), axis=0)
    down_give, three_cxy, three_cyx, down_b, grad_low = tie(
        down_give, three_cxy, three_cyx, down_b, grad_low
    )

    pieces = (
        three_z, three_x, three_y, three_xy, three_yx,
        three_c, three_cx, three_cy, three_cxy, three_cyx,
    )
    down_got = send(down_give, OVER_C)
    grad_before, up_bias_grad = gate_call(place_vec, pieces, grad_low, (slope0, slope1))
    grad_before, a2, down_got = tie(grad_before, a2, down_got)
    down = add_low(down_keep, down_got).reshape(4, 2, 2, 2, 64, 1024)
    down = fold_second(down[:, :, :, 0], down[:, :, :, 1], place)
    up_keep, up_give = up_grad_call(place_vec, a2, grad_before)
    grad_before, up_keep, up_give = tie(grad_before, up_keep, up_give)

    up_got = send(up_give, OVER_C)
    grad_low_hidden, grad_hidden, sums = norm_up_call(
        place_vec, up_pieces, grad_before, hidden, ln2_gain, grad_low
    )
    grad_low_hidden, grad_hidden, sums, down, up_got = tie(
        grad_low_hidden, grad_hidden, sums, down, up_got
    )

    down = fold_third(down, place)
    up = add_low(up_keep, up_got).reshape(4, 2, 2, 32, 4096)
    up = fold_second(up[..., :2048], up[..., 2048:], place)
    early = jnp.concatenate(
        [sums[2], sums[0], sums[1], up_bias_grad.reshape(4096), down_b]
    ).reshape(8, 1024)
    grad_context = dense_back_call(grad_low_hidden, w1)
    q0, k0, v0 = attn_bwd(
        length, jnp.asarray(slopes_split), qkv0, context0, lse0, grad_context, 0
    )
    q0, k0, v0, down, up, a1, early = tie(q0, k0, v0, down, up, a1, early)

    owner_down = scatter_z_line(both(down))
    up = fold_third(up, place)
    third_keep, third_give, sums0 = columns_call(
        place_vec,
        [(context0, context1), (a1,)],
        [(grad_low_hidden, 0), (grad_low_hidden, 1), (q0, 0), (k0, 0), (v0, 0)],
        (0, 0, 1, 1, 1),
        "dense_grad",
    )
    third_keep, third_give, qkv1, up = tie(third_keep, third_give, qkv1, up)
    third_got = send(third_give, OVER_C)
    up = both(up)
    third_got, up, qkv1 = tie(third_got, up, qkv1)

    owner_up = scatter_z_line(up)
    third = add_low(third_keep, third_got).reshape(4, 2, 2, 32, 2560)
    third = fold_second(third[..., :1280], third[..., 1280:], place)
    q1, k1, v1 = attn_bwd(
        length, jnp.asarray(slopes_split), qkv1, context1, lse1, grad_context, 4
    )
    q1, k1, v1, third = tie(q1, k1, v1, third)

    third = fold_third(third, place)
    last_keep, last_give, sums1 = columns_call(
        place_vec, [(a1,)], [(q1, 0), (k1, 0), (v1, 0)], (0, 0, 0), "heads_grad"
    )
    last_keep, last_give, third, q0 = tie(last_keep, last_give, third, q0)
    last_got = send(last_give, OVER_C)
    third = both(third)
    last_got, third, q0, tokens = tie(last_got, third, q0, tokens)

    last = add_low(last_keep, last_got).reshape(4, 2, 2, 32, 1536)
    last = fold_second(last[..., :768], last[..., 768:], place)
    third = scatter_z_line(third)
    token_grad, sums = norm_qkv_call(
        [q0, k0, v0, q1, k1, v1], w0, w1, tokens, ln1_gain, grad_hidden
    )
    token_grad, sums, last, u0 = tie(token_grad, sums, last, u0)

    last = fold_third(last, place)
    vectors = [sums0[0, 1024:1536], sums1[0, :512], sums0[0, 2048:], sums1[0, 1024:]]
    late = jnp.concatenate(vectors + [sums[0], sums[1]]).reshape(4, 1024)
    late = jnp.concatenate([late, early])
    late_near = [send(late, pairs) for pairs in (OVER_C, OVER_X, OVER_CX)]
    block_output = down_call(place_vec, pieces, (u0, u1), hidden, down_bias)
    block_output, last, late, late_near = tie(block_output, last, late, late_near)

    late = late + sum(late_near)
    late_y = send(late, OVER_Y)
    last = fold_z(last, place)
    late, late_y, owner_up, owner_down, third = tie(late, late_y, owner_up, owner_down, third)
    late = late + late_y
    late_z = [send(late, OVER_Z[k]) for k in (1, 2, 3)]
    third = third.astype(f32)
    third = jnp.concatenate([third[0], third[1]], axis=1)
    owner_down = owner_down.astype(f32).reshape(128, 1024)
    owner_up = owner_up.astype(f32)
    owner_up = jnp.concatenate([owner_up[0], owner_up[1]], axis=1)
    late, late_z, last, owner_up, owner_down, third = tie(
        late, late_z, last, owner_up, owner_down, third
    )
    last = total(last)
    last = jnp.concatenate([last[0], last[1]], axis=1)
    late = late + sum(late_z)
    early = late[4:]
    owner_qkv = jnp.concatenate(
        [
            part
            for i in range(3)
            for part in (third[:, 1024 + 512 * i : 1536 + 512 * i], last[:, 512 * i : 512 * i + 512])
        ],
        axis=1,
    )
    return (
        block_output,
        token_grad,
        late[2],
        late[3],
        owner_qkv,
        late[:2].reshape(2 * width),
        third[:, :1024],
        early[0],
        early[1],
        early[2],
        owner_up,
        early[3:7].reshape(4 * width),
        owner_down,
        early[7],
    )


def solution(mesh):
    in_specs = (
        P(("dp", "seq"), None),
        P(),
        P(),
        P(("dp", "seq"), None),
        P(),
        P(("dp", "seq"), None),
        P(),
        P(),
        P(),
        P(("dp", "seq"), None),
        P(),
        P(("dp", "seq"), None),
        P(),
        P(("dp", "seq"), None),
        P(),
        P(),
    )
    out_specs = (
        P(("dp", "seq"), None),
        P(("dp", "seq"), None),
        P(),
        P(),
        P(("dp", "seq"), None),
        P(),
        P(("dp", "seq"), None),
        P(),
        P(),
        P(),
        P(("dp", "seq"), None),
        P(),
        P(("dp", "seq"), None),
        P(),
    )
    body = fast_shards if mesh.shape["dp"] == 16 and mesh.shape["seq"] == 2 else generic_shards
    return jax.shard_map(body, mesh=mesh, in_specs=in_specs, out_specs=out_specs, check_vma=False)
```

```python
import functools
import itertools

import jax
import jax.numpy as jnp
import ml_dtypes
import numpy as np
from jax import lax
from jax.experimental import pallas as pl
from jax.experimental.layout import Layout, with_layout_constraint
from jax.experimental.pallas import tpu as pltpu
from jax.sharding import PartitionSpec as P

H = 16
SEQLEN = 1024
SG = 2
BQ = 256
f32 = jnp.float32
bf16 = jnp.bfloat16
NT = (((1,), (1,)), ((), ()))


def dot(a, b):
    return jnp.dot(a, b, preferred_element_type=f32)


def dotnt(a, b):
    return lax.dot_general(a, b, NT, preferred_element_type=f32)


LOG2E=1.4426950408889634

def attn_fwd_kernel(len_ref, slope_ref, q_ref, k_ref, v_ref, o_ref, lse_ref):
    pair=pl.program_id(0)+len_ref[1]
    n=q_ref.shape[0]
    length=len_ref[0]
    lane=lax.broadcasted_iota(jnp.int32,(1,128),1)
    first=lane<64
    place=lax.broadcasted_iota(jnp.int32,(n,128),0)
    hi=(place//8*8).astype(f32); lo=(place%8).astype(f32)
    kf=jnp.where(lane<6,jnp.where(lane%2==0,hi,lo),jnp.where(lane==6,jnp.where(place<length,0.0,-1e30),0.0)).astype(bf16)
    kaug=jnp.concatenate([k_ref[...],kf],axis=1)
    vaug=jnp.concatenate([v_ref[...],jnp.ones((n,128),bf16)],axis=1)
    diag=lax.broadcasted_iota(jnp.int32,(BQ,BQ),1)<=lax.broadcasted_iota(jnp.int32,(BQ,BQ),0)
    feats=[]
    for h in range(2):
        j=3*(2*pair+h)
        mf=jnp.where(lane<2,slope_ref[j],jnp.where(lane<4,slope_ref[j+1],jnp.where(lane<6,slope_ref[j+2],jnp.where(lane==6,1.0,0.0)))).astype(bf16)
        feats.append(jnp.broadcast_to(mf,(BQ,128)))
    for i in range(n//BQ):
        nk=(i+1)*BQ
        q=q_ref[i*BQ:(i+1)*BQ,:]*jnp.array(0.125,bf16)
        outs=[];lses=[]
        for h in range(2):
            qa=jnp.concatenate([jnp.where(first if h==0 else ~first, q, jnp.zeros_like(q)),feats[h]],axis=1)
            s=dotnt(qa,kaug[:nk])
            sd=jnp.where(diag,s[:,nk-BQ:],-1e30)
            s=sd if i==0 else jnp.concatenate([s[:,:nk-BQ],sd],axis=1)
            m=jnp.max(s,axis=1,keepdims=True)*LOG2E
            p=jnp.exp2(s*LOG2E-m).astype(bf16)
            o=dot(p,vaug[:nk])
            tot=o[:,128:]
            outs.append(o[:,:128]/tot)
            lses.append((m+jnp.log2(tot))*(1.0/LOG2E))
        o_ref[i*BQ:(i+1)*BQ,:]=jnp.where(first,outs[0],outs[1]).astype(bf16)
        lse_ref[i*BQ:(i+1)*BQ,:]=jnp.where(first,lses[0],lses[1])

def attn_fwd(length,slopes,qkv):
    n=qkv.shape[0]; D=qkv.shape[1]//3; np_=D//128
    spec=lambda off: pl.BlockSpec((n,128),lambda p,*_: (0,p+off))
    return pl.pallas_call(attn_fwd_kernel,
        grid_spec=pltpu.PrefetchScalarGridSpec(num_scalar_prefetch=2,grid=(np_,),
            in_specs=[spec(0),spec(np_),spec(2*np_)],out_specs=[spec(0),spec(0)]),
        out_shape=[jax.ShapeDtypeStruct((n,D),bf16),jax.ShapeDtypeStruct((n,D),f32)],
        compiler_params=pltpu.CompilerParams(vmem_limit_bytes=63*2**20),
        cost_estimate=pl.CostEstimate(flops=int(2*2*n*n*D*2.5),bytes_accessed=n*D*12,transcendentals=n*n*10),
        name="attn_fwd")(length,slopes,qkv,qkv,qkv)

def split3(x):
    a=x.astype(bf16); r=x-a.astype(f32); b=r.astype(bf16); c=(r-b.astype(f32)).astype(bf16)
    return a,b,c

def attn_bwd_kernel(len_ref, slope_ref, q_ref, k_ref, v_ref, o_ref, lse_ref, do_ref, dq_ref, dk_ref, dv_ref, qa_ref, doa_ref, dqt_ref):
    pair=pl.program_id(0)+len_ref[1]
    n=q_ref.shape[0]
    nb=n//BQ
    length=len_ref[0]
    lane=lax.broadcasted_iota(jnp.int32,(1,128),1)
    sub=lane%64
    first=lane<64
    place=lax.broadcasted_iota(jnp.int32,(n,128),0)
    hi=(place//8*8).astype(f32); lo=(place%8).astype(f32)
    kf=jnp.where(sub<3,-1.0,jnp.where(sub<9,jnp.where(sub%2==1,hi,lo),jnp.where(sub==9,jnp.where(place<length,0.0,-1e30),0.0))).astype(bf16)
    vf=jnp.where(sub<3,-1.0,0.0).astype(bf16)
    k=k_ref[...]; v=v_ref[...]
    kaug=jnp.concatenate([k,kf],axis=1)
    vaug=jnp.concatenate([v,jnp.broadcast_to(vf,(n,128))],axis=1)
    q=q_ref[...]*jnp.array(0.125,bf16)
    do=do_ref[...]
    prod=do.astype(f32)*o_ref[...].astype(f32)
    same=(lax.broadcasted_iota(jnp.int32,(128,128),0)//64==lax.broadcasted_iota(jnp.int32,(128,128),1)//64).astype(bf16)
    p1,p2,p3=split3(prod)
    dd=dot(p1,same)+dot(p2,same)+dot(p3,same)
    d1,d2,d3=split3(dd)
    l1,l2,l3=split3(lse_ref[...])
    zero=jnp.zeros((n,128),bf16)
    for h in range(2):
        mine=first if h==0 else ~first
        m1=slope_ref[3*(2*pair+h)];m2=slope_ref[3*(2*pair+h)+1];m3=slope_ref[3*(2*pair+h)+2]
        mf=jnp.where(sub<5,m1,jnp.where(sub<7,m2,jnp.where(sub<9,m3,jnp.where(sub==9,1.0,0.0)))).astype(bf16)
        qf=jnp.where(sub==0,l1,jnp.where(sub==1,l2,jnp.where(sub==2,l3,jnp.broadcast_to(mf,(n,128)))))
        df=jnp.where(sub==0,d1,jnp.where(sub==1,d2,jnp.where(sub==2,d3,zero)))
        qa_ref[h]=jnp.concatenate([jnp.where(mine,q,zero),jnp.where(mine,qf,zero)],axis=1)
        doa_ref[h]=jnp.concatenate([jnp.where(mine,do,zero),jnp.where(mine,df,zero)],axis=1)
    kt=k.T
    diag=lax.broadcasted_iota(jnp.int32,(BQ,BQ),0)<=lax.broadcasted_iota(jnp.int32,(BQ,BQ),1)
    for j in range(nb):
        ks=slice(j*BQ,(j+1)*BQ); qs=slice(j*BQ,n)
        dvs=[];dks=[]
        for h in range(2):
            sT=dotnt(kaug[ks],qa_ref[h,qs,:])
            dpT=dotnt(vaug[ks],doa_ref[h,qs,:])
            p=jnp.exp(sT)
            pd=jnp.where(diag,p[:,:BQ],0.0)
            p=pd if j==nb-1 else jnp.concatenate([pd,p[:,BQ:]],axis=1)
            ds=(p*dpT).astype(bf16)
            dvs.append(dot(p.astype(bf16),do_ref[qs,:]))
            dks.append(dot(ds,q[qs]))
            t=dot(kt[64*h:64*h+64,ks],ds)
            if j==0: dqt_ref[64*h:64*h+64,:]=t
            else: dqt_ref[64*h:64*h+64,qs]+=t
        dv_ref[ks,:]=jnp.where(first,dvs[0],dvs[1]).astype(bf16)
        dk_ref[ks,:]=jnp.where(first,dks[0],dks[1]).astype(bf16)
    dq_ref[...]=(dqt_ref[...]*0.125).T.astype(bf16)

def attn_bwd(length,slopes3,qkv,o,lse,do,start):
    n=qkv.shape[0]; D=qkv.shape[1]//3; np_=D//128
    spec=lambda off: pl.BlockSpec((n,128),lambda p,*_: (0,p+off))
    return pl.pallas_call(attn_bwd_kernel,
        grid_spec=pltpu.PrefetchScalarGridSpec(num_scalar_prefetch=2,grid=(np_,),
            in_specs=[spec(0),spec(np_),spec(2*np_),spec(0),spec(0),spec(start)],out_specs=[spec(0)]*3,
            scratch_shapes=[pltpu.VMEM((2,n,256),bf16),pltpu.VMEM((2,n,256),bf16),pltpu.VMEM((128,n),f32)]),
        out_shape=[jax.ShapeDtypeStruct((n,D),bf16)]*3,
        compiler_params=pltpu.CompilerParams(vmem_limit_bytes=48*2**20),
        cost_estimate=pl.CostEstimate(flops=int(5*2*n*n*D*2.5),bytes_accessed=n*D*20,transcendentals=n*n*10),
        name="attn_bwd")(length,slopes3,qkv,qkv,qkv,o,lse,do)


def layer_norm(values, gain, shift):
    center = values - jnp.mean(values, axis=-1, keepdims=True)
    spread = jnp.mean(center * center, axis=-1, keepdims=True)
    return center * lax.rsqrt(spread + 1e-05) * gain + shift


def gelu_tanh(values):
    return jax.nn.gelu(values, approximate=True)


def generic_shards(
    tokens,
    ln1_gain,
    ln1_bias,
    qkv_weight,
    qkv_bias,
    dense_weight,
    dense_bias,
    ln2_gain,
    ln2_bias,
    up_weight,
    up_bias,
    down_weight,
    down_bias,
    cotangent,
    seq_lengths,
    slot_order,
):
    rows = tokens.shape[0]
    width = tokens.shape[1]
    group = rows * lax.axis_size("seq")
    f32 = jnp.float32
    bf16 = jnp.bfloat16
    window = SEQLEN
    w_qkv, w_dense, w_up, w_down = (
        lax.all_gather(qkv_weight, ("dp", "seq"), axis=0, tiled=True),
        lax.all_gather(dense_weight, ("dp", "seq"), axis=0, tiled=True),
        lax.all_gather(up_weight, ("dp", "seq"), axis=0, tiled=True),
        lax.all_gather(down_weight, ("dp", "seq"), axis=0, tiled=True),
    )
    order_group = lax.dynamic_slice_in_dim(slot_order, lax.axis_index("dp") * SG, SG)
    every_seq = jnp.arange(seq_lengths.shape[0], dtype=jnp.int32)
    lengths_group = jnp.sum(
        jnp.where(every_seq[None, :] == order_group[:, None], seq_lengths[None, :], 0), axis=1
    )
    slot_numbers = jnp.arange(SG, dtype=jnp.int32)

    def length_of(slots):
        return jnp.sum(
            jnp.where(slots[:, None] == slot_numbers[None, :], lengths_group[None, :], 0), axis=1
        )

    first_row = lax.axis_index("seq") * rows
    window_start = jnp.minimum(first_row // SEQLEN * SEQLEN, group - window)
    key_index = window_start + jnp.arange(window, dtype=jnp.int32)
    key_slot = key_index // SEQLEN
    key_place = key_index % SEQLEN
    key_live = key_place < length_of(key_slot)
    query_index = first_row + jnp.arange(rows, dtype=jnp.int32)
    query_slot = query_index // SEQLEN
    query_place = query_index % SEQLEN
    valid = (query_place < length_of(query_slot)).astype(f32)
    allowed = (
        (query_slot[:, None] == key_slot[None, :])
        & (key_place[None, :] <= query_place[:, None])
        & key_live[None, :]
    )
    offset = (key_place[None, :] - query_place[:, None]).astype(f32)
    slopes = jnp.exp2(-8.0 * (jnp.arange(H, dtype=f32) + 1.0) / H)
    inputs = tokens.astype(f32)
    normed_one, norm_one_back = jax.vjp(layer_norm, inputs, ln1_gain, ln1_bias)
    normed_low = normed_one.astype(bf16)
    bias_full = jnp.concatenate([qkv_bias[:width], jnp.zeros((width,), f32), qkv_bias[width:]])
    joined = (jnp.dot(normed_low, w_qkv, preferred_element_type=f32) + bias_full).astype(bf16)
    query = joined[:, :width]
    keys_group, values_group = (
        lax.all_gather(joined[:, width : 2 * width], "seq", axis=0, tiled=True),
        lax.all_gather(joined[:, 2 * width :], "seq", axis=0, tiled=True),
    )
    keys_all = lax.dynamic_slice_in_dim(keys_group, window_start, window, 0)
    values_all = lax.dynamic_slice_in_dim(values_group, window_start, window, 0)

    def split_heads(matrix):
        return matrix.reshape(matrix.shape[0], H, width // H).transpose(1, 0, 2)

    def merge_heads(stack):
        return stack.transpose(1, 0, 2).reshape(stack.shape[1], width)

    head_queries = split_heads(query)
    head_keys = split_heads(keys_all)
    head_values = split_heads(values_all)

    def scores_of(head_query, head_key, head_slope):
        scores = jnp.einsum("qd,kd->qk", head_query, head_key, preferred_element_type=f32) * 0.125
        return jnp.where(allowed, scores + head_slope * offset, -1e30)

    def head_forward(packed):
        head_query, head_key, head_value, head_slope = packed
        scores = scores_of(head_query, head_key, head_slope)
        top = jnp.max(scores, axis=-1, keepdims=True)
        expo = jnp.exp(scores - top)
        totals = jnp.sum(expo, axis=-1, keepdims=True)
        probs = (expo / totals).astype(bf16)
        result = jnp.einsum("qk,kd->qd", probs, head_value, preferred_element_type=f32)
        return (result, top[:, 0] + jnp.log(totals[:, 0]))

    head_context, head_lse = lax.map(head_forward, (head_queries, head_keys, head_values, slopes))
    context = merge_heads(head_context).astype(bf16)
    hidden = inputs + jnp.dot(context, w_dense, preferred_element_type=f32) + dense_bias
    normed_two, norm_two_back = jax.vjp(layer_norm, hidden, ln2_gain, ln2_bias)
    normed_two_low = normed_two.astype(bf16)
    before = jnp.dot(normed_two_low, w_up, preferred_element_type=f32) + up_bias
    active, gelu_back = jax.vjp(gelu_tanh, before)
    active_low = active.astype(bf16)
    outputs = hidden + jnp.dot(active_low, w_down, preferred_element_type=f32) + down_bias
    block_output = outputs.astype(bf16)
    back_qkv, back_dense, back_up, back_down = (
        lax.all_gather(qkv_weight, ("dp", "seq"), axis=0, tiled=True),
        lax.all_gather(dense_weight, ("dp", "seq"), axis=0, tiled=True),
        lax.all_gather(up_weight, ("dp", "seq"), axis=0, tiled=True),
        lax.all_gather(down_weight, ("dp", "seq"), axis=0, tiled=True),
    )
    grad_out = cotangent.astype(f32) * valid[:, None]
    grad_out_low = grad_out.astype(bf16)
    grad_down_w = jnp.einsum("rf,rd->fd", active_low, grad_out_low, preferred_element_type=f32)
    grad_down_b = jnp.sum(grad_out_low.astype(f32), axis=0)
    grad_active = jnp.einsum("rd,fd->rf", grad_out_low, back_down, preferred_element_type=f32)
    (grad_before,) = gelu_back(grad_active)
    grad_before_low = grad_before.astype(bf16)
    grad_up_w = jnp.einsum("rd,rf->df", normed_two_low, grad_before_low, preferred_element_type=f32)
    grad_up_b = jnp.sum(grad_before_low.astype(f32), axis=0)
    grad_normed_two = jnp.einsum("rf,df->rd", grad_before_low, back_up, preferred_element_type=f32)
    grad_hidden_norm, grad_gain_two, grad_shift_two = norm_two_back(grad_normed_two)
    grad_hidden = grad_out + grad_hidden_norm
    grad_hidden_low = grad_hidden.astype(bf16)
    grad_dense_w = jnp.einsum("rd,re->de", context, grad_hidden_low, preferred_element_type=f32)
    grad_dense_b = jnp.sum(grad_hidden_low.astype(f32), axis=0)
    grad_context = jnp.einsum(
        "re,de->rd", grad_hidden_low, back_dense, preferred_element_type=f32
    ).astype(bf16)

    def head_backward(packed):
        head_query, head_key, head_value, head_slope, head_grad, head_norm = packed
        scores = scores_of(head_query, head_key, head_slope)
        probs = jnp.exp(scores - head_norm[:, None])
        prob_grad = jnp.einsum("qd,kd->qk", head_grad, head_value, preferred_element_type=f32)
        value_grad = jnp.einsum(
            "qk,qd->kd", probs.astype(bf16), head_grad, preferred_element_type=f32
        )
        row_dot = jnp.sum(probs * prob_grad, axis=-1, keepdims=True)
        score_grad = (probs * (prob_grad - row_dot)).astype(bf16)
        query_grad = (
            jnp.einsum("qk,kd->qd", score_grad, head_key, preferred_element_type=f32) * 0.125
        )
        key_grad = (
            jnp.einsum("qk,qd->kd", score_grad, head_query, preferred_element_type=f32) * 0.125
        )
        return (query_grad, key_grad, value_grad)

    grad_queries, grad_keys, grad_values = lax.map(
        head_backward,
        (head_queries, head_keys, head_values, slopes, split_heads(grad_context), head_lse),
    )
    empty_group = jnp.zeros((group, width), f32)
    key_terms = lax.dynamic_update_slice_in_dim(
        empty_group, merge_heads(grad_keys), window_start, 0
    )
    value_terms = lax.dynamic_update_slice_in_dim(
        empty_group, merge_heads(grad_values), window_start, 0
    )
    grad_key, grad_value = (
        lax.psum_scatter(
            key_terms.astype(jnp.bfloat16), "seq", scatter_dimension=0, tiled=True
        ).astype(jnp.float32),
        lax.psum_scatter(
            value_terms.astype(jnp.bfloat16), "seq", scatter_dimension=0, tiled=True
        ).astype(jnp.float32),
    )
    grad_query = merge_heads(grad_queries)
    grad_joined = jnp.concatenate([grad_query, grad_key, grad_value], axis=1).astype(bf16)
    grad_qkv_w = jnp.einsum("rd,rc->dc", normed_low, grad_joined, preferred_element_type=f32)
    joined_sums = jnp.sum(grad_joined.astype(f32), axis=0)
    grad_qkv_b = jnp.concatenate([joined_sums[:width], joined_sums[2 * width :]])
    grad_normed_one = jnp.einsum("rc,dc->rd", grad_joined, back_qkv, preferred_element_type=f32)
    grad_input_norm, grad_gain_one, grad_shift_one = norm_one_back(grad_normed_one)
    token_grad = (grad_hidden + grad_input_norm).astype(bf16)
    owner_qkv, owner_dense, owner_up, owner_down = (
        lax.psum_scatter(grad_qkv_w, ("dp", "seq"), scatter_dimension=0, tiled=True),
        lax.psum_scatter(grad_dense_w, ("dp", "seq"), scatter_dimension=0, tiled=True),
        lax.psum_scatter(grad_up_w, ("dp", "seq"), scatter_dimension=0, tiled=True),
        lax.psum_scatter(grad_down_w, ("dp", "seq"), scatter_dimension=0, tiled=True),
    )
    (
        total_gain_one,
        total_shift_one,
        total_qkv_b,
        total_dense_b,
        total_gain_two,
        total_shift_two,
        total_up_b,
        total_down_b,
    ) = lax.psum(
        (
            grad_gain_one,
            grad_shift_one,
            grad_qkv_b,
            grad_dense_b,
            grad_gain_two,
            grad_shift_two,
            grad_up_b,
            grad_down_b,
        ),
        ("dp", "seq"),
    )
    return (
        block_output,
        token_grad,
        total_gain_one,
        total_shift_one,
        owner_qkv,
        total_qkv_b,
        owner_dense,
        total_dense_b,
        total_gain_two,
        total_shift_two,
        owner_up,
        total_up_b,
        owner_down,
        total_down_b,
    )


ALL = ("dp", "seq")


def flat_index(z, y, c, x):
    return ((z * 2 + y) * 2 + c) * 2 + x


TN = (((0,), (0,)), ((), ()))
MIB = 2**20


def owner_of(place_ref, half, zr, near, turn, core, turned):
    z, y, c, x = (place_ref[i] for i in range(4))
    xr, yr = (near, turn) if half == 0 else (turn, near)
    za = (z + 4 - zr) % 4 if turned else zr
    return flat_index(za, y + yr - 2 * y * yr, c + core - 2 * c * core, x + xr - 2 * x * xr)


def start_mixed(place_ref, pieces, w_ref, sem, turned):
    for half, zr, near, turn, core in itertools.product(range(2), range(4), *[range(2)] * 3):
        d = owner_of(place_ref, half, zr, near, turn, core, turned)
        rows = pl.ds(pl.multiple_of(d * 32 + half * 16, 16), 16)
        src = pieces[4 * half + 2 * core + turn].at[near, zr]
        pltpu.make_async_copy(src, w_ref.at[:, rows, :], sem).start()


def of_half(pieces, half):
    return [pieces[5 * core + i] for core in range(2) for i in (0, 1, 2, 3 + half)]


def piece(pieces, half, zr, xr, yr, core):
    ref = pieces[4 * core + xr + 2 * yr]
    return ref.at[zr] if xr and yr else ref.at[zr, half]


def owner(place_ref, zr, xr, yr, core):
    _, y, c, x = (place_ref[i] for i in range(4))
    return flat_index(zr, y + yr - 2 * y * yr, c + core - 2 * c * core, x + xr - 2 * x * xr)


def start_columns(place_ref, pieces, w_ref, sem, half):
    for zr, xr, yr, core in itertools.product(range(4), *[range(2)] * 3):
        d = owner(place_ref, zr, xr, yr, core)
        rows = pl.ds(pl.multiple_of(d * 32, 32), 32)
        src = piece(pieces, half, zr, xr, yr, core)
        pltpu.make_async_copy(src, w_ref.at[:, rows, :], sem).start()


def wait_all(ref, sem):
    pltpu.make_async_copy(ref, ref, sem).wait()


def start_rows(place_ref, pieces, w_ref, sems, step):
    for zr in range(4):

        @pl.when(step == max(zr - 1, 0))
        def _(zr=zr):
            for half, xr, yr, core in itertools.product(range(2), repeat=4):
                d = owner(place_ref, zr, xr, yr, core)
                rows = pl.ds(pl.multiple_of(d * 128 + half * 64, 64), 64)
                src = piece(of_half(pieces, half), half, zr, xr, yr, core).at[0]
                pltpu.make_async_copy(src, w_ref.at[rows, :], sems.at[zr]).start()


def wait_rows(w_ref, sems, z):
    part = w_ref.at[pl.ds(pl.multiple_of(z * 1024, 1024), 1024), :]
    pltpu.make_async_copy(part, part, sems.at[z]).wait()


def dottn(a, b):
    return lax.dot_general(a, b, TN, preferred_element_type=f32)


def spec(shape, index):
    return pl.BlockSpec(shape, index)


def params(mib=56):
    return pltpu.CompilerParams(vmem_limit_bytes=mib * MIB)


HBM = pl.BlockSpec(memory_space=pltpu.HBM)


def qkv_kernel(turned, place_ref, *refs):
    pieces, (a_ref, b_ref, o_ref, all_ref, w_ref, sem, out_sem) = refs[:8], refs[8:]
    step = pl.program_id(0)
    write = pltpu.make_async_copy(w_ref, all_ref, out_sem)

    @pl.when(step == 0)
    def _():
        start_mixed(place_ref, pieces, w_ref, sem, turned)
        wait_all(w_ref, sem)
        write.start()

    o_ref[...] = (dot(a_ref[...], w_ref[step]) + b_ref[...]).astype(bf16)

    @pl.when(step == 2)
    def _():
        write.wait()


def qkv_call(place, pieces, a, b, turned):
    n, d = a.shape
    blocks = pieces[0].shape[2]
    return pl.pallas_call(
        functools.partial(qkv_kernel, turned),
        grid_spec=pltpu.PrefetchScalarGridSpec(
            num_scalar_prefetch=1,
            grid=(3,),
            in_specs=[HBM] * 8
            + [spec((n, d), lambda i, *_: (0, 0)), spec((1, 512), lambda i, *_: (0, i))],
            out_specs=[spec((n, 512), lambda i, *_: (0, i)), HBM],
            scratch_shapes=[
                pltpu.VMEM((blocks, d, 512), bf16),
                pltpu.SemaphoreType.DMA,
                pltpu.SemaphoreType.DMA,
            ],
        ),
        out_shape=[
            jax.ShapeDtypeStruct((n, 1536), bf16),
            jax.ShapeDtypeStruct((blocks, d, 512), bf16),
        ],
        compiler_params=params(63),
        cost_estimate=pl.CostEstimate(
            flops=2 * n * d * 1536, bytes_accessed=2 * (n * d + 8 * d * 512 + 1536 * n), transcendentals=0
        ),
        name="qkv",
    )(place, *pieces, a, b.reshape(1, 1536))


def dense_kernel(c0_ref, c1_ref, w0_ref, w1_ref, x_ref, b_ref, g_ref, s_ref, h_ref, a_ref):
    half = [
        dot(c0_ref[...], w_ref[0, :512, :]) + dot(c1_ref[...], w_ref[0, 512:, :])
        for w_ref in (w0_ref, w1_ref)
    ]
    hidden = x_ref[...].astype(f32) + jnp.concatenate(half, axis=1) + b_ref[...]
    h_ref[...] = hidden
    center = hidden - jnp.mean(hidden, axis=1, keepdims=True)
    rsd = lax.rsqrt(jnp.mean(center * center, axis=1, keepdims=True) + 1e-05)
    a_ref[...] = (center * rsd * g_ref[...] + s_ref[...]).astype(bf16)


def dense_call(c0, c1, w, x, bias, gain, shift):
    n, d = x.shape
    rows = lambda c: spec((256, c), lambda i: (i, 0))
    vector = spec((1, d), lambda i: (0, 0))
    return pl.pallas_call(
        dense_kernel,
        grid=(n // 256,),
        in_specs=[rows(512), rows(512)]
        + [spec((1, d, 512), lambda i, b=b: (b, 0, 0)) for b in (3, 4)]
        + [rows(d), vector, vector, vector],
        out_specs=[rows(d), rows(d)],
        out_shape=[jax.ShapeDtypeStruct((n, d), f32), jax.ShapeDtypeStruct((n, d), bf16)],
        compiler_params=params(40),
        cost_estimate=pl.CostEstimate(flops=2 * n * d * d, bytes_accessed=12 * n * d, transcendentals=0),
        name="dense",
    )(c0, c1, w, w, x, bias.reshape(1, d), gain.reshape(1, d), shift.reshape(1, d))


def dense_back_kernel(g_ref, w0_ref, w1_ref, o_ref):
    o_ref[...] = (
        dotnt(g_ref[:, :512], w0_ref[0]) + dotnt(g_ref[:, 512:], w1_ref[0])
    ).astype(bf16)


def dense_back_call(g, w):
    n, d = g.shape
    rows = spec((256, d), lambda i: (i, 0))
    return pl.pallas_call(
        dense_back_kernel,
        grid=(n // 256,),
        in_specs=[rows] + [spec((1, d, 512), lambda i, b=b: (b, 0, 0)) for b in (3, 4)],
        out_specs=rows,
        out_shape=jax.ShapeDtypeStruct((n, d), bf16),
        compiler_params=params(40),
        cost_estimate=pl.CostEstimate(flops=2 * n * d * d, bytes_accessed=6 * n * d, transcendentals=0),
        name="dense_back",
    )(g, w, w)


def up_kernel(place_ref, *refs):
    pieces, (a_ref, b_ref, u0_ref, u1_ref, s0_ref, s1_ref, w_ref, sems) = refs[:10], refs[10:]
    step = pl.program_id(0)
    for half in range(2):
        part = w_ref.at[2 * half : 2 * half + 2]

        @pl.when(step == half)
        def _(half=half, part=part):
            start_columns(place_ref, of_half(pieces, half), part, sems.at[half], half)

        @pl.when(step == 4 * half)
        def _(half=half, part=part):
            wait_all(part, sems.at[half])

    c = 0.7978845608028654

    def block(u_ref, s_ref):
        w = w_ref[step // 2, :, pl.ds(pl.multiple_of(step % 2 * 512, 512), 512)]
        for r in range(0, a_ref.shape[0], 256):
            v = dot(a_ref[r : r + 256, :], w) + b_ref[...]
            square = v * v
            h = 0.5 + 0.5 * jnp.tanh(v * (c + (c * 0.044715) * square))
            u = v * h
            u_ref[r : r + 256, :] = u.astype(bf16)
            s_ref[r : r + 256, :] = (
                h + u * (1.0 - h) * (2.0 * c + (2.0 * c * 0.134145) * square)
            ).astype(bf16)

    @pl.when(step < 4)
    def _():
        block(u0_ref, s0_ref)

    @pl.when(step >= 4)
    def _():
        block(u1_ref, s1_ref)


def up_call(place, pieces, a, b):
    n, d = a.shape
    outs = [
        spec((n, 512), lambda i, *_: (0, jnp.minimum(i, 3))),
        spec((n, 512), lambda i, *_: (0, jnp.maximum(i - 4, 0))),
    ]
    return pl.pallas_call(
        up_kernel,
        grid_spec=pltpu.PrefetchScalarGridSpec(
            num_scalar_prefetch=1,
            grid=(8,),
            in_specs=[HBM] * 10
            + [spec((n, d), lambda i, *_: (0, 0)), spec((1, 512), lambda i, *_: (0, i))],
            out_specs=outs + outs,
            scratch_shapes=[pltpu.VMEM((4, d, 1024), bf16), pltpu.SemaphoreType.DMA((2,))],
        ),
        out_shape=[jax.ShapeDtypeStruct((n, 2048), bf16)] * 4,
        compiler_params=params(),
        cost_estimate=pl.CostEstimate(
            flops=2 * n * d * 4096, bytes_accessed=2 * (n * d + d * 4096 + 8192 * n), transcendentals=n * 4096
        ),
        name="up",
    )(place, *pieces, a, b.reshape(1, 4096))


def divide(acc_ref, keep_ref, give_ref, core):
    keep_ref[...] = acc_ref[:, pl.ds(core, 1)].reshape(keep_ref.shape)
    give_ref[...] = acc_ref[:, pl.ds(1 - core, 1)].reshape(give_ref.shape)


def down_grad_kernel(where_ref, u0_ref, u1_ref, g_ref, keep_ref, give_ref, acc_ref):
    step = pl.program_id(0)
    for half, u_ref in enumerate((u0_ref, u1_ref)):

        @pl.when(step // 4 == half)
        def _(u_ref=u_ref):
            acc_ref[...] = dottn(u_ref[...], g_ref[...]).astype(bf16).reshape(acc_ref.shape)

    divide(acc_ref, keep_ref, give_ref, where_ref[2])


def down_grad_call(where, u, g):
    n, d = g.shape
    out = spec((1, 256, d), lambda i, *_: (i, 0, 0))
    return pl.pallas_call(
        down_grad_kernel,
        grid_spec=pltpu.PrefetchScalarGridSpec(
            num_scalar_prefetch=1,
            grid=(8,),
            in_specs=[
                spec((n, 512), lambda i, *_: (0, jnp.minimum(i, 3))),
                spec((n, 512), lambda i, *_: (0, jnp.maximum(i - 4, 0))),
                spec((n, d), lambda i, *_: (0, 0)),
            ],
            out_specs=[out, out],
            scratch_shapes=[pltpu.VMEM((1, 2, 256, d), bf16)],
        ),
        out_shape=[jax.ShapeDtypeStruct((8, 256, d), bf16)] * 2,
        compiler_params=params(40),
        cost_estimate=pl.CostEstimate(
            flops=2 * n * d * 4096, bytes_accessed=2 * (n * d + d * 4096 + n * 4096), transcendentals=0
        ),
        name="down_grad",
    )(where, *u, g)


def divide_kernel(place_ref, keep_ref, got_ref, ka_ref, ga_ref, kb_ref, gb_ref, sum_ref):
    y, x = place_ref[1], place_ref[3]
    total = keep_ref[...].astype(f32) + got_ref[...].astype(f32)
    sum_ref[...] = total.astype(bf16).reshape(sum_ref.shape)
    ka_ref[...] = sum_ref[:, pl.ds(x, 1), :64, :].reshape(ka_ref.shape)
    ga_ref[...] = sum_ref[:, pl.ds(1 - x, 1), :64, :].reshape(ga_ref.shape)
    kb_ref[...] = sum_ref[pl.ds(y, 1), :, 64:, :].reshape(kb_ref.shape)
    gb_ref[...] = sum_ref[pl.ds(1 - y, 1), :, 64:, :].reshape(gb_ref.shape)


def divide_call(place, keep, got):
    d = keep.shape[2]
    block = spec((2, 256, d), lambda i, *_: (i, 0, 0))
    return pl.pallas_call(
        divide_kernel,
        grid_spec=pltpu.PrefetchScalarGridSpec(
            num_scalar_prefetch=1,
            grid=(4,),
            in_specs=[block, block],
            out_specs=[spec((1, 2, 64, d), lambda i, *_: (i, 0, 0, 0))] * 4,
            scratch_shapes=[pltpu.VMEM((2, 2, 128, d), bf16)],
        ),
        out_shape=[jax.ShapeDtypeStruct((4, 2, 64, d), bf16)] * 4,
        compiler_params=params(20),
        cost_estimate=pl.CostEstimate(flops=2**21, bytes_accessed=12 * 2**20, transcendentals=0),
        name="divide",
    )(place, keep, got)


def down_kernel(place_ref, *refs):
    pieces, (u0_ref, u1_ref, h_ref, b_ref, o_ref, acc_ref, w_ref, sems) = refs[:10], refs[10:]
    step = pl.program_id(0)

    start_rows(place_ref, pieces, w_ref, sems, step)
    wait_rows(w_ref, sems, step)
    w = w_ref[pl.ds(pl.multiple_of(step * 1024, 1024), 1024), :]

    @pl.when(step == 0)
    def _():
        acc_ref[...] = dot(u0_ref[...], w)

    @pl.when(step == 1)
    def _():
        acc_ref[...] += dot(u0_ref[...], w)

    @pl.when(step == 2)
    def _():
        acc_ref[...] += dot(u1_ref[...], w)

    @pl.when(step == 3)
    def _():
        for r in range(0, u1_ref.shape[0], 256):
            rows = slice(r, r + 256)
            part = acc_ref[rows, :] + dot(u1_ref[rows, :], w)
            o_ref[rows, :] = (h_ref[rows, :] + part + b_ref[...]).astype(bf16)


def down_call(place, pieces, u, hidden, bias):
    n, d = hidden.shape
    whole = lambda s: spec(s, lambda i, *_: (0, 0))
    return pl.pallas_call(
        down_kernel,
        grid_spec=pltpu.PrefetchScalarGridSpec(
            num_scalar_prefetch=1,
            grid=(4,),
            in_specs=[HBM] * 10
            + [
                spec((n, 1024), lambda i, *_: (0, jnp.minimum(i, 1))),
                spec((n, 1024), lambda i, *_: (0, jnp.maximum(i - 2, 0))),
                whole((n, d)),
                whole((1, d)),
            ],
            out_specs=whole((n, d)),
            scratch_shapes=[
                pltpu.VMEM((n, d), f32),
                pltpu.VMEM((4096, d), bf16),
                pltpu.SemaphoreType.DMA((4,)),
            ],
        ),
        out_shape=jax.ShapeDtypeStruct((n, d), bf16),
        compiler_params=params(),
        cost_estimate=pl.CostEstimate(
            flops=2 * n * d * 4096, bytes_accessed=2 * (3 * n * d + d * 4096 + n * 4096), transcendentals=0
        ),
        name="down",
    )(place, *pieces, *u, hidden, bias.reshape(1, d))


def gate_kernel(place_ref, *refs):
    pieces, (g_ref, s0_ref, s1_ref, z_ref, b_ref, w_ref, sems) = refs[:10], refs[10:]
    step = pl.program_id(0)

    start_rows(place_ref, pieces, w_ref, sems, step)
    wait_rows(w_ref, sems, step)
    w = w_ref[pl.ds(pl.multiple_of(step * 1024, 1024), 1024), :]
    total = None
    for r in range(0, g_ref.shape[0], 256):
        rows = slice(r, r + 256)
        slope = jnp.where(step < 2, s0_ref[rows, :], s1_ref[rows, :])
        v = (dotnt(g_ref[rows, :], w) * slope.astype(f32)).astype(bf16)
        z_ref[rows, :] = v
        part = jnp.sum(v.astype(f32).reshape(32, 8, v.shape[1]), axis=0)
        total = part if total is None else total + part
    b_ref[...] = jnp.sum(total, axis=0, keepdims=True)


def gate_call(place, pieces, g, slopes):
    n, d = g.shape
    return pl.pallas_call(
        gate_kernel,
        grid_spec=pltpu.PrefetchScalarGridSpec(
            num_scalar_prefetch=1,
            grid=(4,),
            in_specs=[HBM] * 10
            + [
                spec((n, d), lambda i, *_: (0, 0)),
                spec((n, 1024), lambda i, *_: (0, jnp.minimum(i, 1))),
                spec((n, 1024), lambda i, *_: (0, jnp.maximum(i - 2, 0))),
            ],
            out_specs=[
                spec((n, 1024), lambda i, *_: (0, i)),
                spec((1, 1024), lambda i, *_: (0, i)),
            ],
            scratch_shapes=[pltpu.VMEM((4096, d), bf16), pltpu.SemaphoreType.DMA((4,))],
        ),
        out_shape=[jax.ShapeDtypeStruct((n, 4096), bf16), jax.ShapeDtypeStruct((1, 4096), f32)],
        compiler_params=params(),
        cost_estimate=pl.CostEstimate(
            flops=2 * n * d * 4096, bytes_accessed=2 * (n * d + d * 4096 + 8192 * n), transcendentals=0
        ),
        name="gate",
    )(place, *pieces, g, *slopes)


def norm_back(x_ref, gain_ref, res_ref, acc_ref, out_refs, sums_ref):
    n, d = x_ref.shape

    def chunk(i, sums):
        rows = pl.ds(pl.multiple_of(i * 128, 128), 128)
        grad = acc_ref[rows, :]
        x = x_ref[rows, :].astype(f32)
        center = x - jnp.mean(x, axis=1, keepdims=True)
        rsd = lax.rsqrt(jnp.mean(center * center, axis=1, keepdims=True) + 1e-05)
        hat = center * rsd
        e = grad * gain_ref[...]
        back = rsd * (
            e - jnp.mean(e, axis=1, keepdims=True) - hat * jnp.mean(e * hat, axis=1, keepdims=True)
        )
        result = res_ref[rows, :].astype(f32) + back
        low = result.astype(bf16)
        out_refs[0][rows, :] = low
        if len(out_refs) > 1:
            out_refs[1][rows, :] = result
        fold = lambda v: jnp.sum(v.reshape(16, 8, d), axis=0)
        return sums[0] + fold(grad * hat), sums[1] + fold(grad), sums[2] + fold(low.astype(f32))

    zero = jnp.zeros((8, d), f32)
    sums = lax.fori_loop(0, n // 128, chunk, (zero, zero, zero))
    for k in range(3):
        sums_ref[k : k + 1, :] = jnp.sum(sums[k], axis=0, keepdims=True)


def norm_up_kernel(place_ref, *refs):
    pieces, (g_ref, x_ref, gain_ref, res_ref, low_ref, wide_ref, sums_ref, acc_ref, w_ref, sems) = (
        refs[:10],
        refs[10:],
    )
    step = pl.program_id(0)

    for half in range(2):

        @pl.when(step == half)
        def _(half=half):
            part = w_ref.at[2 * half : 2 * half + 2]
            start_columns(place_ref, of_half(pieces, half), part, sems.at[half], half)

    for half in range(2):

        @pl.when(step == 2 * half)
        def _():
            wait_all(w_ref.at[2 * half : 2 * half + 2], sems.at[half])

    @pl.when(step == 0)
    def _():
        acc_ref[...] = dotnt(g_ref[...], w_ref[0])

    @pl.when(step > 0)
    def _():
        acc_ref[...] += dotnt(g_ref[...], w_ref[step])

    @pl.when(step == 3)
    def _():
        norm_back(x_ref, gain_ref, res_ref, acc_ref, (low_ref, wide_ref), sums_ref)


def norm_up_call(place, pieces, g, x, gain, residual):
    n, d = x.shape
    ff = g.shape[1]
    whole = lambda s: spec(s, lambda i, *_: (0, 0))
    return pl.pallas_call(
        norm_up_kernel,
        grid_spec=pltpu.PrefetchScalarGridSpec(
            num_scalar_prefetch=1,
            grid=(4,),
            in_specs=[HBM] * 10
            + [spec((n, 1024), lambda i, *_: (0, i)), whole((n, d)), whole((1, d)), whole((n, d))],
            out_specs=[whole((n, d)), whole((n, d)), whole((8, d))],
            scratch_shapes=[
                pltpu.VMEM((n, d), f32),
                pltpu.VMEM((4, d, 1024), bf16),
                pltpu.SemaphoreType.DMA((2,)),
            ],
        ),
        out_shape=[
            jax.ShapeDtypeStruct((n, d), bf16),
            jax.ShapeDtypeStruct((n, d), f32),
            jax.ShapeDtypeStruct((8, d), f32),
        ],
        compiler_params=params(),
        cost_estimate=pl.CostEstimate(
            flops=2 * n * d * ff, bytes_accessed=2 * (8 * n * d + 2 * d * ff), transcendentals=0
        ),
        name="norm_up",
    )(place, *pieces, g, x, gain.reshape(1, d), residual)


def norm_qkv_kernel(*refs):
    g_refs = refs[:6]
    w0_ref, w1_ref, x_ref, gain_ref, res_ref, low_ref, sums_ref, acc_ref = refs[6:]
    step = pl.program_id(0)
    for i in range(3):

        @pl.when(step == i)
        def _(i=i):
            part = dotnt(g_refs[i][...], w0_ref[0]) + dotnt(g_refs[3 + i][...], w1_ref[0])
            acc_ref[...] = part if i == 0 else acc_ref[...] + part

    @pl.when(step == 2)
    def _():
        norm_back(x_ref, gain_ref, res_ref, acc_ref, (low_ref,), sums_ref)


def norm_qkv_call(grads, w0, w1, x, gain, residual):
    n, d = x.shape
    whole = lambda s: spec(s, lambda i: (0, 0))
    return pl.pallas_call(
        norm_qkv_kernel,
        grid=(3,),
        in_specs=[whole((n, 512))] * 6
        + [spec((1, d, 512), lambda i: (i, 0, 0))] * 2
        + [whole((n, d)), whole((1, d)), whole((n, d))],
        out_specs=[whole((n, d)), whole((8, d))],
        out_shape=[jax.ShapeDtypeStruct((n, d), bf16), jax.ShapeDtypeStruct((8, d), f32)],
        scratch_shapes=[pltpu.VMEM((n, d), f32)],
        compiler_params=params(),
        cost_estimate=pl.CostEstimate(
            flops=2 * n * d * 3072, bytes_accessed=2 * (8 * n * d + d * 3072), transcendentals=0
        ),
        name="norm_qkv",
    )(*grads, w0, w1, x, gain.reshape(1, d), residual)


def columns_kernel(plan, parts, where_ref, *refs):
    count = sum(parts)
    left_refs, right_refs = refs[:count], refs[count : count + len(plan)]
    keep_ref, give_ref, sums_ref, at_ref, acc_ref = refs[-5:]
    step = pl.program_id(0)
    for i, left in enumerate(plan):

        @pl.when(step == i)
        def _(i=i, left=left):
            if i == 0 or plan[i - 1] != left:
                begin = sum(parts[:left])
                row = 0
                for ref in left_refs[begin : begin + parts[left]]:
                    at_ref[row : row + ref.shape[1], :] = ref[...].T
                    row += ref.shape[1]
            right = right_refs[i][...]
            acc = dot(at_ref[...], right)
            acc_ref[...] = acc.astype(bf16).reshape(acc_ref.shape)
            total = jnp.sum(right.astype(f32).reshape(-1, 8, right.shape[1]), axis=0)
            sums_ref[...] = jnp.sum(total, axis=0, keepdims=True)

    divide(acc_ref, keep_ref, give_ref, where_ref[2])


def columns_call(where, lefts, rights, plan, name):
    flat = [a for left in lefts for a in left]
    n = flat[0].shape[0]
    d = sum(a.shape[1] for a in lefts[0])
    wide = 512 * len(rights)
    out = spec((8, 64, 512), lambda i, *_: (0, 0, i))
    return pl.pallas_call(
        functools.partial(columns_kernel, plan, [len(left) for left in lefts]),
        grid_spec=pltpu.PrefetchScalarGridSpec(
            num_scalar_prefetch=1,
            grid=(len(plan),),
            in_specs=[spec(a.shape, lambda i, *_: (0, 0)) for a in flat]
            + [spec((n, 512), lambda i, *_, b=b: (0, b)) for _, b in rights],
            out_specs=[out, out, spec((1, 512), lambda i, *_: (0, i))],
            scratch_shapes=[pltpu.VMEM((d, n), bf16), pltpu.VMEM((8, 2, 64, 512), bf16)],
        ),
        out_shape=[jax.ShapeDtypeStruct((8, 64, wide), bf16)] * 2
        + [jax.ShapeDtypeStruct((1, wide), f32)],
        compiler_params=params(40),
        cost_estimate=pl.CostEstimate(
            flops=2 * n * d * wide, bytes_accessed=2 * (2 * n * d + d * wide + n * wide), transcendentals=0
        ),
        name=name,
    )(where, *flat, *[r for r, _ in rights])


def up_grad_kernel(where_ref, a_ref, g_ref, keep_ref, give_ref, at_ref, acc_ref):
    @pl.when(pl.program_id(0) == 0)
    def _():
        at_ref[...] = a_ref[...].T

    acc_ref[...] = dot(at_ref[...], g_ref[...]).astype(bf16).reshape(acc_ref.shape)
    divide(acc_ref, keep_ref, give_ref, where_ref[2])


def up_grad_call(where, a, g):
    n, d = a.shape
    ff = g.shape[1]
    out = spec((8, 64, 512), lambda i, *_: (0, 0, i))
    return pl.pallas_call(
        up_grad_kernel,
        grid_spec=pltpu.PrefetchScalarGridSpec(
            num_scalar_prefetch=1,
            grid=(ff // 512,),
            in_specs=[spec((n, d), lambda i, *_: (0, 0)), spec((n, 512), lambda i, *_: (0, i))],
            out_specs=[out, out],
            scratch_shapes=[pltpu.VMEM((d, n), bf16), pltpu.VMEM((8, 2, 64, 512), bf16)],
        ),
        out_shape=[jax.ShapeDtypeStruct((8, 64, ff), bf16)] * 2,
        compiler_params=params(40),
        cost_estimate=pl.CostEstimate(
            flops=2 * n * d * ff, bytes_accessed=2 * (n * d + d * ff + n * ff), transcendentals=0
        ),
        name="up_grad",
    )(where, a, g)


def permutation(move):
    pairs = []
    for z in range(4):
        for y in range(2):
            for c in range(2):
                for x in range(2):
                    pairs.append((flat_index(z, y, c, x), flat_index(*move(z, y, c, x))))
    return pairs


OVER_X = permutation(lambda z, y, c, x: (z, y, c, 1 - x))
OVER_Y = permutation(lambda z, y, c, x: (z, 1 - y, c, x))
OVER_C = permutation(lambda z, y, c, x: (z, y, 1 - c, x))
OVER_CX = permutation(lambda z, y, c, x: (z, y, 1 - c, 1 - x))
OVER_Z = [permutation(lambda z, y, c, x, k=k: ((z + k) % 4, y, c, x)) for k in range(4)]


Z_GROUPS = [
    [flat_index(z, y, c, x) for z in range(4)] for y in range(2) for c in range(2) for x in range(2)
]


def send(array, pairs):
    return lax.ppermute(array, ALL, pairs)


def plain(array):
    return with_layout_constraint(array, Layout(major_to_minor=tuple(range(array.ndim))))


def tie(*trees):
    return lax.optimization_barrier(trees)


def gather_z(shard):
    return [shard] + [send(shard, OVER_Z[k]) for k in (1, 2, 3)]


def halves(parts):
    return jnp.stack([p[0] for p in parts]), jnp.stack([p[1] for p in parts])


def gather_z_line(shard):
    return plain(lax.all_gather(shard, ALL, axis=0, tiled=False, axis_index_groups=Z_GROUPS))


def scatter_z_line(array):
    return lax.psum_scatter(array, ALL, scatter_dimension=0, tiled=False, axis_index_groups=Z_GROUPS)


def add_low(a, b):
    return (a.astype(f32) + b.astype(f32)).astype(bf16)


def take(array, at, axis):
    return lax.dynamic_index_in_dim(array, at, axis, keepdims=False)


def fold(g, at, axis, pairs):
    return take(g, at, axis), send(take(g, 1 - at, axis), pairs)


def fold_second(a, b, place):
    return fold(a, place[3], 2, OVER_X), fold(b, place[1], 1, OVER_Y)


def fold_third(pair, place):
    a, b = (add_low(*p) for p in pair)
    return fold(a, place[1], 1, OVER_Y), fold(b, place[3], 1, OVER_X)


def both(pair):
    return jnp.stack([add_low(*p) for p in pair], axis=1)


def fold_z(pair, place):
    z = place[0]
    g = both(pair)
    return [take(g, z, 0)] + [send(take(g, (z + k) % 4, 0), OVER_Z[k]) for k in (1, 2, 3)]


def total(parts):
    return sum(p.astype(f32) for p in parts)


def slope_table():
    slopes = np.exp2(-8.0 * (np.arange(H) + 1.0) / H).astype(np.float32)
    pieces, rest = [], slopes
    for _ in range(3):
        low = rest.astype(ml_dtypes.bfloat16).astype(np.float32)
        pieces.append(low)
        rest = rest - low
    return np.stack(pieces, axis=1).reshape(-1)


def moments(v):
    mean = jnp.mean(v, axis=-1, keepdims=True)
    center = v - mean
    return center, lax.rsqrt(jnp.mean(center * center, axis=-1, keepdims=True) + 1e-05)


def fast_shards(
    tokens,
    ln1_gain,
    ln1_bias,
    qkv_weight,
    qkv_bias,
    dense_weight,
    dense_bias,
    ln2_gain,
    ln2_bias,
    up_weight,
    up_bias,
    down_weight,
    down_bias,
    cotangent,
    seq_lengths,
    slot_order,
):
    rows, width = tokens.shape
    dp, seq = lax.axis_index("dp"), lax.axis_index("seq")
    place = (dp // 4, (dp // 2) % 2, dp % 2, seq)
    place_vec = jnp.stack([p.astype(jnp.int32) for p in place])

    def mixed(*blocks):
        stacked = jnp.stack(blocks).reshape(len(blocks), 2, 16, 512)
        return stacked.transpose(1, 0, 2, 3)

    w_in = [qkv_weight[:, 512 * i : 512 * i + 512] for i in range(6)]
    one = mixed(*w_in[0::2], *w_in[1::2], dense_weight[:, :512], dense_weight[:, 512:])
    two = up_weight.reshape(32, 4, 1024).transpose(1, 0, 2).reshape(2, 2, 32, 1024)
    three = down_weight.reshape(2, 1, 64, 1024)

    slot = dp * SG + seq
    my_seq = lax.dynamic_index_in_dim(slot_order, slot, 0, keepdims=False)
    every_seq = jnp.arange(seq_lengths.shape[0], dtype=jnp.int32)
    length = jnp.sum(jnp.where(every_seq == my_seq, seq_lengths, 0))
    valid = (jnp.arange(rows, dtype=jnp.int32) < length).astype(f32)
    slopes_split = slope_table()
    no_bias = jnp.zeros((512,), f32)
    bias0 = jnp.concatenate([qkv_bias[:512], no_bias, qkv_bias[1024:1536]])
    bias1 = jnp.concatenate([qkv_bias[512:1024], no_bias, qkv_bias[1536:]])

    bias0, bias1 = bias0.reshape(1, 1536), bias1.reshape(1, 1536)
    first_heads, other_heads = (jnp.stack([length, jnp.int32(s)]) for s in (0, 4))
    split_slopes = jnp.asarray(slopes_split)

    one_z = gather_z(one)
    one_z, two, tokens, cotangent = tie(one_z, two, tokens, cotangent)

    a, b = halves([p[:, :3] for p in one_z])
    one_x, one_y = send(a, OVER_X), send(b, OVER_Y)
    two_z = gather_z_line(two)
    also_za, also_zb = halves([p[:, 3:] for p in one_z])
    one_x, one_y, also_za, also_zb, tokens, cotangent = tie(
        one_x, one_y, also_za, also_zb, tokens, cotangent
    )
    place_vec, bias0, bias1, first_heads, other_heads, valid, one_x = tie(
        place_vec, bias0, bias1, first_heads, other_heads, valid, one_x
    )

    one_a, one_b = jnp.stack([a, one_x]), jnp.stack([b, one_y])
    one_xy, one_yx = send(one_a, OVER_Y), send(one_b, OVER_X)
    one_ca, one_cb = send(one_a, OVER_C), send(one_b, OVER_C)
    center, rsd = moments(tokens.astype(f32))
    a1 = (center * rsd * ln1_gain + ln1_bias).astype(bf16)
    grad_low = cotangent * valid[:, None].astype(bf16)
    one_xy, one_yx, one_ca, one_cb, a1, grad_low = tie(
        one_xy, one_yx, one_ca, one_cb, a1, grad_low
    )
    one_cxy, one_cyx = send(one_xy, OVER_C), send(one_yx, OVER_C)
    a, b = also_za, also_zb
    one_cxy, one_cyx, a, b, three = tie(one_cxy, one_cyx, a, b, three)

    also_x, also_y = send(a, OVER_X), send(b, OVER_Y)
    pieces = (one_a, one_xy, one_ca, one_cxy, one_b, one_yx, one_cb, one_cyx)
    qkv0, w0 = qkv_call(place_vec, pieces, a1, bias0, True)
    qkv0, also_x, also_y, two_z = tie(qkv0, also_x, also_y, two_z)
    also_a, also_b = jnp.stack([a, also_x]), jnp.stack([b, also_y])
    also_xy, also_yx = send(also_a, OVER_Y), send(also_b, OVER_X)
    also_ca, also_cb = send(also_a, OVER_C), send(also_b, OVER_C)
    three_z = gather_z_line(three)
    context0, lse0 = attn_fwd(first_heads, split_slopes, qkv0)
    context0, also_xy, also_yx, also_ca, also_cb, a1 = tie(
        context0, also_xy, also_yx, also_ca, also_cb, a1
    )

    also_cxy, also_cyx = send(also_xy, OVER_C), send(also_yx, OVER_C)
    also_cxy, also_cyx = tie(also_cxy, also_cyx)
    pieces = (also_a, also_xy, also_ca, also_cxy, also_b, also_yx, also_cb, also_cyx)
    two_c = send(two_z, OVER_C)
    two_x, two_y = plain(send(two_z, OVER_X)), plain(send(two_z, OVER_Y))
    qkv1, w1 = qkv_call(place_vec, pieces, a1, bias1, True)
    qkv1, two_c, three_z = tie(qkv1, two_c, three_z)
    context1, lse1 = attn_fwd(other_heads, split_slopes, qkv1)
    context0, context1, two_x, two_y, three_z = tie(context0, context1, two_x, two_y, three_z)

    two_xy, two_yx = send(two_x[:, 0], OVER_Y), send(two_y[:, 1], OVER_X)
    two_cx, two_cy = send(two_x, OVER_C), send(two_y, OVER_C)
    hidden, a2 = dense_call(context0, context1, w1, tokens, dense_bias, ln2_gain, ln2_bias)
    a2, two_xy, two_yx, two_cx, two_cy, three_z = tie(a2, two_xy, two_yx, two_cx, two_cy, three_z)
    two_cxy, two_cyx = send(two_xy, OVER_C), send(two_yx, OVER_C)
    two_cxy, two_cyx, a2, three_z = tie(two_cxy, two_cyx, a2, three_z)

    three_c = send(three_z, OVER_C)
    three_x, three_y = plain(send(three_z, OVER_X)), plain(send(three_z, OVER_Y))
    up_pieces = (two_z, two_x, two_y, two_xy, two_yx, two_c, two_cx, two_cy, two_cxy, two_cyx)
    u0, u1, slope0, slope1 = up_call(place_vec, up_pieces, a2, up_bias)
    u0, u1, grad_low, three_x, three_y, three_c = tie(
        u0, u1, grad_low, three_x, three_y, three_c
    )
    three_xy, three_yx = send(three_x[:, 0], OVER_Y), send(three_y[:, 1], OVER_X)
    three_cx, three_cy = send(three_x, OVER_C), send(three_y, OVER_C)

    down_keep, down_give = down_grad_call(place_vec, (u0, u1), grad_low)
    down_keep, down_give, grad_low, three_cx, three_cy, three_xy, three_yx = tie(
        down_keep, down_give, grad_low, three_cx, three_cy, three_xy, three_yx
    )
    three_cxy, three_cyx = send(three_xy, OVER_C), send(three_yx, OVER_C)
    down_b = jnp.sum(grad_low.astype(f32), axis=0)
    down_give, three_cxy, three_cyx, down_b, grad_low = tie(
        down_give, three_cxy, three_cyx, down_b, grad_low
    )

    pieces = (
        three_z, three_x, three_y, three_xy, three_yx,
        three_c, three_cx, three_cy, three_cxy, three_cyx,
    )
    down_got = send(down_give, OVER_C)
    grad_before, up_bias_grad = gate_call(place_vec, pieces, grad_low, (slope0, slope1))
    grad_before, a2, down_got = tie(grad_before, a2, down_got)
    keep_a, give_a, keep_b, give_b = divide_call(place_vec, down_keep, down_got)
    down = (keep_a, send(give_a, OVER_X)), (keep_b, send(give_b, OVER_Y))
    up_keep, up_give = up_grad_call(place_vec, a2, grad_before)
    grad_before, up_keep, up_give = tie(grad_before, up_keep, up_give)

    up_got = send(up_give, OVER_C)
    grad_low_hidden, grad_hidden, sums = norm_up_call(
        place_vec, up_pieces, grad_before, hidden, ln2_gain, grad_low
    )
    grad_low_hidden, grad_hidden, sums, down, up_got = tie(
        grad_low_hidden, grad_hidden, sums, down, up_got
    )

    down = fold_third(down, place)
    up = add_low(up_keep, up_got).reshape(4, 2, 2, 32, 4096)
    up = fold_second(up[..., :2048], up[..., 2048:], place)
    early = jnp.concatenate(
        [sums[2], sums[0], sums[1], up_bias_grad.reshape(4096), down_b]
    ).reshape(8, 1024)
    grad_context = dense_back_call(grad_low_hidden, w1)
    q0, k0, v0 = attn_bwd(
        first_heads, split_slopes, qkv0, context0, lse0, grad_context, 0
    )
    q0, k0, v0, down, up, a1, early = tie(q0, k0, v0, down, up, a1, early)

    owner_down = scatter_z_line(plain(both(down)))
    up = fold_third(up, place)
    third_keep, third_give, sums0 = columns_call(
        place_vec,
        [(context0, context1), (a1,)],
        [(grad_low_hidden, 0), (grad_low_hidden, 1), (q0, 0), (k0, 0), (v0, 0)],
        (0, 0, 1, 1, 1),
        "dense_grad",
    )
    third_keep, third_give, qkv1, up = tie(third_keep, third_give, qkv1, up)
    third_got = send(third_give, OVER_C)
    up = both(up)
    third_got, up, qkv1 = tie(third_got, up, qkv1)

    owner_up = scatter_z_line(up)
    third = add_low(third_keep, third_got).reshape(4, 2, 2, 32, 2560)
    third = fold_second(third[..., :1280], third[..., 1280:], place)
    q1, k1, v1 = attn_bwd(
        other_heads, split_slopes, qkv1, context1, lse1, grad_context, 4
    )
    q1, k1, v1, third = tie(q1, k1, v1, third)

    third = fold_third(third, place)
    last_keep, last_give, sums1 = columns_call(
        place_vec, [(a1,)], [(q1, 0), (k1, 0), (v1, 0)], (0, 0, 0), "heads_grad"
    )
    last_keep, last_give, third, q0 = tie(last_keep, last_give, third, q0)
    last_got = send(last_give, OVER_C)
    third = both(third)
    last_got, third, q0, tokens = tie(last_got, third, q0, tokens)

    last = add_low(last_keep, last_got).reshape(4, 2, 2, 32, 1536)
    last = fold_second(last[..., :768], last[..., 768:], place)
    third = scatter_z_line(third)
    token_grad, sums = norm_qkv_call(
        [q0, k0, v0, q1, k1, v1], w0, w1, tokens, ln1_gain, grad_hidden
    )
    token_grad, sums, last, u0 = tie(token_grad, sums, last, u0)

    last = fold_third(last, place)
    vectors = [sums0[0, 1024:1536], sums1[0, :512], sums0[0, 2048:], sums1[0, 1024:]]
    late = jnp.concatenate(vectors + [sums[0], sums[1]]).reshape(4, 1024)
    late = jnp.concatenate([late, early])
    late_near = [send(late, pairs) for pairs in (OVER_C, OVER_X, OVER_CX)]
    block_output = down_call(place_vec, pieces, (u0, u1), hidden, down_bias)
    block_output, last, late, late_near = tie(block_output, last, late, late_near)

    late = late + sum(late_near)
    late_y = send(late, OVER_Y)
    last = fold_z(last, place)
    late, late_y, owner_up, owner_down, third = tie(late, late_y, owner_up, owner_down, third)
    late = late + late_y
    late_z = [send(late, OVER_Z[k]) for k in (1, 2, 3)]
    third = third.astype(f32)
    third = jnp.concatenate([third[0], third[1]], axis=1)
    owner_down = owner_down.astype(f32).reshape(128, 1024)
    owner_up = owner_up.astype(f32)
    owner_up = jnp.concatenate([owner_up[0], owner_up[1]], axis=1)
    late, late_z, last, owner_up, owner_down, third = tie(
        late, late_z, last, owner_up, owner_down, third
    )
    last = total(last)
    last = jnp.concatenate([last[0], last[1]], axis=1)
    late = late + sum(late_z)
    early = late[4:]
    owner_qkv = jnp.concatenate(
        [
            part
            for i in range(3)
            for part in (third[:, 1024 + 512 * i : 1536 + 512 * i], last[:, 512 * i : 512 * i + 512])
        ],
        axis=1,
    )
    return (
        block_output,
        token_grad,
        late[2],
        late[3],
        owner_qkv,
        late[:2].reshape(2 * width),
        third[:, :1024],
        early[0],
        early[1],
        early[2],
        owner_up,
        early[3:7].reshape(4 * width),
        owner_down,
        early[7],
    )


def solution(mesh):
    in_specs = (
        P(("dp", "seq"), None),
        P(),
        P(),
        P(("dp", "seq"), None),
        P(),
        P(("dp", "seq"), None),
        P(),
        P(),
        P(),
        P(("dp", "seq"), None),
        P(),
        P(("dp", "seq"), None),
        P(),
        P(("dp", "seq"), None),
        P(),
        P(),
    )
    out_specs = (
        P(("dp", "seq"), None),
        P(("dp", "seq"), None),
        P(),
        P(),
        P(("dp", "seq"), None),
        P(),
        P(("dp", "seq"), None),
        P(),
        P(),
        P(),
        P(("dp", "seq"), None),
        P(),
        P(("dp", "seq"), None),
        P(),
    )
    body = fast_shards if mesh.shape["dp"] == 16 and mesh.shape["seq"] == 2 else generic_shards
    return jax.shard_map(body, mesh=mesh, in_specs=in_specs, out_specs=out_specs, check_vma=False)
```
